32 devices in a mesh: dp: 8 (over z, core), seq: 4 (over y, x).
Axes of the slice: x: 2, y: 2, z: 4, core: 2. Of those that a mesh axis runs over, the one named last changes fastest.
Arguments:
- tokens: bfloat16 [32, 512, 768], P('dp', 'seq'), may hold values from -6 to 6
- doc_ids: int32 [32, 512], P('dp'), may hold values from 0 to 3, as said below
- norm_gain: float32 [768], replicated, may hold values from 0.5 to 1.5
- value_weight: bfloat16 [768, 3072], replicated, may hold values from -0.21875 to 0.21875
- forward_weight: bfloat16 [768, 1536], replicated, may hold values from -0.21875 to 0.21875
- backward_weight: bfloat16 [768, 1536], replicated, may hold values from -0.21875 to 0.21875
- update_weight: bfloat16 [1536, 3072], replicated, may hold values from -0.15625 to 0.15625
- output_weight: bfloat16 [3072, 768], replicated, may hold values from -0.3125 to 0.3125
- kernel_params: float32 [2, 4, 64, 1536], P(None, None, None, 'seq'), as said below
- cotangent: bfloat16 [32, 512, 768], P('dp', 'seq'), may hold values from -6 to 6
Outputs:
- layer_out: bfloat16 [32, 512, 768], P('dp', 'seq')
- tokens_grad: bfloat16 [32, 512, 768], P('dp', 'seq')
- norm_gain_grad: float32 [768], P(('dp', 'seq'))
- value_weight_grad: float32 [768, 3072], P(('dp', 'seq'))
- forward_weight_grad: float32 [768, 1536], P(('dp', 'seq'))
- backward_weight_grad: float32 [768, 1536], P(('dp', 'seq'))
- update_weight_grad: float32 [1536, 3072], P(('dp', 'seq'))
- output_weight_grad: float32 [3072, 768], P(('dp', 'seq'))
- kernel_params_grad: float32 [2, 4, 64, 1536], P(None, None, 'dp', 'seq')
The draws below stay inside these ranges and needn't reach their ends.
Inputs may be any that keep to these rules, and one draw needn't show every extreme that they name: `doc_ids`: each row of 512 positions holds either one document, numbered 0, or 4 documents of 128 positions each, numbered 0, 1, ... in order; the rows of every index of dp include rows of both kinds. Decay rates kernel_params[k, 0] are positive and frequencies kernel_params[k, 1] lie in [0, 3]; k = 0 is the forward direction, k = 1 the backward one.
All inputs are finite; a program needn't handle non-finite values.
Results may differ from the reference program's by a relative error of at most 0.012.
The reference program's roundings to bfloat16 on the way count: a program that leaves them out, or rounds other values in their place, can miss the bound.
Values may be sent and summed in bfloat16 or wider, within the bound.
No kernel may reach another device: no remote copies, remote signals or barrier semaphores. Data moves between devices by JAX's collectives and lax.ppermute only.
A program may use at most 704 MiB of HBM per device.

```python
import math
import jax
import jax.numpy as jnp
from jax import lax

D = 768
HID = 3072
SSM = 1536
STATE = 64
LENGTH = 512
BLOCK = 128
ROWS_GRP = 4
ROWS = 32


def draw_doc_ids(key, part):
    key = jax.random.fold_in(key, 7)
    first_key, second_key, third_key = jax.random.split(key, 3)
    group_count = ROWS // ROWS_GRP
    row_kinds = jax.random.randint(first_key, (group_count, ROWS_GRP), 0, 2)
    long_at = jax.random.randint(second_key, (group_count, 1), 0, ROWS_GRP)
    short_at = (long_at + jax.random.randint(third_key, (group_count, 1), 1, ROWS_GRP)) % ROWS_GRP
    row_slots = jnp.arange(ROWS_GRP)[None, :]
    row_kinds = jnp.where(row_slots == long_at, 1, jnp.where(row_slots == short_at, 0, row_kinds))
    sections = (jnp.arange(LENGTH) // BLOCK)[None, None, :]
    doc_numbers = jnp.where(row_kinds[:, :, None] == 1, 0, sections)
    return doc_numbers.reshape(ROWS, LENGTH).astype(jnp.int32)


def draw_kernel_params(key, part):
    key = jax.random.fold_in(key, 13)
    sub_keys = jax.random.split(key, 3)
    param_shape = (2, STATE, SSM)
    decay_rate = jnp.exp(jax.random.uniform(sub_keys[0], param_shape, jnp.float32, math.log(0.0005), math.log(0.05)))
    coefficient = jnp.clip(jax.random.normal(sub_keys[2], (2, 2, STATE, SSM), jnp.float32), -4.0, 4.0) * 0.02
    frequency = jax.random.uniform(sub_keys[1], param_shape, jnp.float32, 0.0, 3.0)
    return jnp.concatenate([decay_rate[:, None], frequency[:, None], coefficient], axis=1).astype(jnp.float32)


def block_levels(own_key, shape, cuts, least, high):
    level = 1.0
    for dim, shards_of in cuts:
        draws = jax.random.uniform(jax.random.fold_in(jax.random.fold_in(own_key, 6), dim), (shards_of,), jnp.float32, least / len(cuts), high / len(cuts))
        level = level * jnp.repeat(jnp.exp(draws), shape[dim] // shards_of).reshape((-1,) + (1,) * (len(shape) - 1 - dim))
    return level


def centred(own_key, extent, scale, most, shards=(), kind=jnp.bfloat16):
    values = scale * jax.random.normal(own_key, extent, jnp.float32)
    if shards:
        values = values * block_levels(own_key, extent, shards, -0.22, 0.18)
    return jnp.clip(values, -most, most).astype(kind)


def setup_inputs(seed: int = 0) -> dict:
    keys = jax.random.split(jax.random.key(seed), 11)
    return {
        "tokens": centred(keys[0], (ROWS, LENGTH, D), 1.0, 6.0, ((0, 8), (1, 4))),
        "doc_ids": draw_doc_ids(jax.random.fold_in(keys[10], 71), 0),
        "norm_gain": jnp.clip(1.0 + 0.1 * jax.random.normal(keys[2], (D,), jnp.float32), 0.5, 1.5),
        "value_weight": centred(keys[3], (D, HID), D ** -0.5, 0.21875),
        "forward_weight": centred(keys[4], (D, SSM), D ** -0.5, 0.21875),
        "backward_weight": centred(keys[5], (D, SSM), D ** -0.5, 0.21875),
        "update_weight": centred(keys[6], (SSM, HID), SSM ** -0.5, 0.15625),
        "output_weight": centred(keys[7], (HID, D), (HID // 8) ** -0.5, 0.3125),
        "kernel_params": draw_kernel_params(jax.random.fold_in(keys[10], 71), 0),
        "cotangent": centred(keys[9], (ROWS, LENGTH, D), 1.0, 6.0, ((0, 8), (1, 4))),
    }


@jax.custom_vjp
def low(v):
    return lax.optimization_barrier(v.astype(jnp.bfloat16)).astype(jnp.float32)

@jax.custom_vjp
def low_back(v):
    return v

def low_keep(v):
    return (low(v), None)

def low_pass(kept, grad):
    return (grad,)

def back_keep(v):
    return (v, None)

def back_low(kept, grad):
    return (low(grad),)
low.defvjp(low_keep, low_pass)
low_back.defvjp(back_keep, back_low)

def gelu(inputs):
    return jax.nn.gelu(inputs, approximate=False)

def kernel_block(params_block):
    positions = jnp.arange(LENGTH).astype(params_block.dtype)[:, None, None]
    phases = positions * params_block[1][None]
    modes = jnp.exp(-positions * params_block[0][None]) * (params_block[2][None] * jnp.cos(phases) - params_block[3][None] * jnp.sin(phases))
    return lax.optimization_barrier(jnp.sum(modes, axis=1))

def one_way(params_dir):
    pieces = params_dir.reshape(4, STATE, SSM // 128, 128).transpose(2, 0, 1, 3)
    kernels = lax.map(jax.checkpoint(kernel_block), pieces)
    return kernels.transpose(1, 0, 2).reshape(LENGTH, SSM)

def kernel_from(params):
    return lax.map(one_way, params)

def conv_doc(values, kernel, doc_numbers):
    padded_len = 2 * LENGTH
    kernel_hat = jnp.fft.rfft(kernel, n=padded_len, axis=0)
    firsts = doc_numbers[:, ::BLOCK]
    starts = jnp.concatenate([jnp.ones_like(firsts[:, :1]) == 1, firsts[:, 1:] != firsts[:, :-1]], axis=1)
    running = jnp.zeros_like(values)
    for section in range(LENGTH // BLOCK):
        inside = (doc_numbers == firsts[:, section:section + 1]).astype(values.dtype)
        spectrum = jnp.fft.rfft(values * inside[:, :, None], n=padded_len, axis=1)
        smooth = jnp.fft.irfft(spectrum * kernel_hat[None], n=padded_len, axis=1)[:, :LENGTH]
        weight = inside * starts[:, section:section + 1].astype(values.dtype)
        running = running + weight[:, :, None] * smooth
    return running

def matmul_high(first_mat, second_mat):
    return jnp.einsum('rtd,dh->rth', first_mat, second_mat, precision=lax.Precision.HIGHEST)

def block_forward(inputs, gain, value_w, forward_w, backward_w, update_w, output_w, kernel, doc_numbers):
    centered = inputs - lax.optimization_barrier(jnp.mean(inputs, axis=-1, keepdims=True))
    inv_std = lax.rsqrt(lax.optimization_barrier(jnp.mean(centered * centered, axis=-1, keepdims=True)) + 1e-05)
    normed = low(centered * inv_std * gain)
    value_act = gelu(low_back(matmul_high(normed, value_w)))
    forward_act = low(low_back(gelu(low_back(matmul_high(normed, forward_w)))))
    backward_act = low(low_back(gelu(low_back(matmul_high(normed, backward_w)))))
    kernel_low = low(kernel)
    convolve = jax.checkpoint(conv_doc)
    along = low_back(convolve(forward_act, kernel_low[0], doc_numbers))
    against = low_back(convolve(backward_act[:, ::-1], kernel_low[1], doc_numbers[:, ::-1])[:, ::-1])
    product = low(low_back(along * against))
    update_act = gelu(low_back(matmul_high(product, update_w)))
    gated = low(update_act * value_act)
    return inputs + matmul_high(gated, output_w)

def reference(tokens, doc_ids, norm_gain, value_weight, forward_weight, backward_weight, update_weight, output_weight, kernel_params, cotangent):
    weights = tuple((weight.astype(jnp.float32) for weight in (value_weight, forward_weight, backward_weight, update_weight, output_weight)))
    kernel, kernel_back = jax.vjp(kernel_from, kernel_params)
    group_size = math.gcd(ROWS, max(1, 4096 // LENGTH))
    count = ROWS // group_size
    token_groups = tokens.astype(jnp.float32).reshape(count, group_size, LENGTH, D)
    doc_groups = doc_ids.reshape(count, group_size, LENGTH)
    cot_groups = cotangent.astype(jnp.float32).reshape(count, group_size, LENGTH, D)

    def accumulate(totals, pieces):
        token_part, doc_part, cot_part = pieces

        def forward(inputs, gain, value_w, forward_w, backward_w, update_w, output_w, kern_in):
            return block_forward(inputs, gain, value_w, forward_w, backward_w, update_w, output_w, kern_in, doc_part)
        result, pullback = jax.vjp(forward, token_part, norm_gain, *weights, kernel)
        gradients = pullback(cot_part)
        updated = tuple((total + grad_piece for total, grad_piece in zip(totals, gradients[1:])))
        return (updated, (result.astype(jnp.bfloat16), gradients[0].astype(jnp.bfloat16)))
    starting = (jnp.zeros(norm_gain.shape, jnp.float32),) + tuple((jnp.zeros(weight.shape, jnp.float32) for weight in weights)) + (jnp.zeros(kernel.shape, jnp.float32),)
    totals, (outputs, input_grads) = lax.scan(accumulate, starting, (token_groups, doc_groups, cot_groups))
    params_grad = kernel_back(totals[6])[0]
    return (outputs.reshape(ROWS, LENGTH, D), input_grads.reshape(ROWS, LENGTH, D), totals[0], totals[1], totals[2], totals[3], totals[4], totals[5], params_grad)
```

```python
import functools
import math

import jax
import jax.numpy as jnp
import ml_dtypes
import numpy as np
from jax import lax
from jax.experimental import pallas as pl
from jax.experimental.pallas import tpu as pltpu
from jax.sharding import PartitionSpec as P

LENGTH = 512
BLOCK = 128
SECTIONS = LENGTH // BLOCK
FREQ = 128
HALF_FREQ = FREQ // 2
LOW = 16
VMEM = 56 * 1024 * 1024
BF16 = jnp.bfloat16
F32 = jnp.float32


def dot(first_mat, second_mat):
    return jnp.dot(first_mat, second_mat, preferred_element_type=F32)


def dot_rt(first_mat, second_mat):
    return lax.dot_general(
        first_mat, second_mat, (((1,), (1,)), ((), ())), preferred_element_type=F32
    )


def dot_lt(first_mat, second_mat):
    return lax.dot_general(
        first_mat, second_mat, (((0,), (0,)), ((), ())), preferred_element_type=F32
    )


def fourier_tables():
    order = np.concatenate([np.arange(0, FREQ, 2), np.arange(1, FREQ, 2)])
    angle = 2.0 * np.pi * (order[:, None] + 0.5) * np.arange(BLOCK)[None, :] / (2 * BLOCK)
    table = np.concatenate([np.cos(angle), -np.sin(angle)], axis=0)
    high = table.astype(ml_dtypes.bfloat16)
    low = (table - high.astype(np.float64)).astype(ml_dtypes.bfloat16)
    forward = np.concatenate([high, low], axis=1)
    scale = ml_dtypes.bfloat16(1.0 / FREQ)
    inverse = np.stack([high.T * scale, low.T * scale]).astype(ml_dtypes.bfloat16)
    return jnp.asarray(forward), jnp.asarray(inverse)


def gelu_pair(v):
    bell = jnp.exp(v * v * -0.5)
    denom = 1.0 + jnp.abs(v) * (0.3275911 / math.sqrt(2.0))
    t = pl.reciprocal(denom, approx=True)
    t = t * (2.0 - denom * t)
    poly = t * (0.5 * 1.061405429) + (0.5 * -1.453152027)
    poly = poly * t + (0.5 * 1.421413741)
    poly = poly * t + (0.5 * -0.284496736)
    poly = poly * t + (0.5 * 0.254829592)
    tail = poly * t * bell
    cdf = jnp.where(v >= 0.0, 1.0 - tail, tail)
    return v * cdf, cdf + v * (1.0 / math.sqrt(2.0 * math.pi)) * bell


def cmul(first, second):
    return (
        first[0] * second[0] - first[1] * second[1],
        first[0] * second[1] + first[1] * second[0],
    )


def powers_of(decay, frequency, count):
    mag = jnp.exp(-decay)
    powers = [(mag * jnp.cos(frequency), mag * jnp.sin(frequency))]
    for _ in range(count - 1):
        powers.append(cmul(powers[-1], powers[-1]))
    return powers


def low_powers(low_re, low_im, n, lanes):
    steps = lax.broadcasted_iota(jnp.int32, (LOW, lanes), 0)
    total = None
    for bit in range(4):
        row_re = jnp.broadcast_to(low_re[bit, pl.ds(n, 1), :], (LOW, lanes))
        row_im = jnp.broadcast_to(low_im[bit, pl.ds(n, 1), :], (LOW, lanes))
        chosen = (steps & (1 << bit)) != 0
        factor = (jnp.where(chosen, row_re, 1.0), jnp.where(chosen, row_im, 0.0))
        total = factor if total is None else cmul(total, factor)
    return total


def kernel_gen_body(info_ref, par_ref, out_ref, high_re, high_im, low_re, low_im):
    modes, lanes = par_ref.shape[2:]
    powers = powers_of(par_ref[0, 0], par_ref[0, 1], 9)
    for bit in range(4):
        low_re[bit] = powers[bit][0]
        low_im[bit] = powers[bit][1]
    second_half = info_ref[0] == 1
    start = (
        jnp.where(second_half, powers[8][0], 1.0),
        jnp.where(second_half, powers[8][1], 0.0),
    )
    current = cmul((par_ref[0, 2], par_ref[0, 3]), start)
    highs = out_ref.shape[1] // LOW
    for i in range(highs):
        high_re[i] = current[0]
        high_im[i] = current[1]
        current = cmul(current, powers[4])

    def one_mode(n, totals):
        lows = low_powers(low_re, low_im, n, lanes)
        return tuple(
            totals[i]
            + high_re[i, pl.ds(n, 1), :] * lows[0]
            - high_im[i, pl.ds(n, 1), :] * lows[1]
            for i in range(highs)
        )

    totals = lax.fori_loop(0, modes, one_mode, (jnp.zeros((LOW, lanes), F32),) * highs)
    for i in range(highs):
        out_ref[0, pl.ds(i * LOW, LOW), :] = totals[i].astype(BF16)


def kernel_gen(info, params):
    dirs, _, modes, channels = params.shape
    lanes = 128
    lags = LENGTH // 2
    return pl.pallas_call(
        kernel_gen_body,
        out_shape=jax.ShapeDtypeStruct((dirs, lags, channels), BF16),
        grid_spec=pltpu.PrefetchScalarGridSpec(
            num_scalar_prefetch=1,
            grid=(dirs, channels // lanes),
            in_specs=[pl.BlockSpec((1, 4, modes, lanes), lambda k, c, info: (k, 0, 0, c))],
            out_specs=pl.BlockSpec((1, lags, lanes), lambda k, c, info: (k, 0, c)),
            scratch_shapes=[
                pltpu.VMEM((lags // LOW, modes, lanes), F32),
                pltpu.VMEM((lags // LOW, modes, lanes), F32),
                pltpu.VMEM((4, modes, lanes), F32),
                pltpu.VMEM((4, modes, lanes), F32),
            ],
        ),
        compiler_params=pltpu.CompilerParams(vmem_limit_bytes=VMEM),
        name="kernel_gen",
    )(info, params)


def params_grad_body(par_ref, up_ref, out_ref, high_re, high_im, low_re, low_im):
    modes, lanes = par_ref.shape[2:]
    powers = powers_of(par_ref[0, 0], par_ref[0, 1], 5)
    for bit in range(4):
        low_re[bit] = powers[bit][0]
        low_im[bit] = powers[bit][1]
    highs = up_ref.shape[1] // LOW
    current = (jnp.ones((modes, lanes), F32), jnp.zeros((modes, lanes), F32))
    for i in range(highs):
        high_re[i] = current[0]
        high_im[i] = current[1]
        current = cmul(current, powers[4])
    steps = lax.broadcasted_iota(jnp.int32, (LOW, lanes), 0).astype(F32)
    for n in range(modes):
        plain = [jnp.zeros((LOW, lanes), F32)] * 2
        ramped = [jnp.zeros((LOW, lanes), F32)] * 2
        for i in range(highs):
            grads = up_ref[0, pl.ds(i * LOW, LOW), :].astype(F32)
            term_re = grads * high_re[i, pl.ds(n, 1), :]
            term_im = grads * high_im[i, pl.ds(n, 1), :]
            plain = [plain[0] + term_re, plain[1] + term_im]
            if i:
                ramped = [ramped[0] + term_re * float(i), ramped[1] + term_im * float(i)]
        lows = low_powers(low_re, low_im, n, lanes)
        ramped = [LOW * ramped[0] + steps * plain[0], LOW * ramped[1] + steps * plain[1]]
        sum_re, sum_im = (jnp.sum(part, axis=0, keepdims=True) for part in cmul(plain, lows))
        lag_re, lag_im = (jnp.sum(part, axis=0, keepdims=True) for part in cmul(ramped, lows))
        real = par_ref[0, 2, pl.ds(n, 1), :]
        imag = par_ref[0, 3, pl.ds(n, 1), :]
        out_ref[0, 0, pl.ds(n, 1), :] = imag * lag_im - real * lag_re
        out_ref[0, 1, pl.ds(n, 1), :] = -(real * lag_im + imag * lag_re)
        out_ref[0, 2, pl.ds(n, 1), :] = sum_re
        out_ref[0, 3, pl.ds(n, 1), :] = -sum_im


def params_grad_of(params, upstream):
    dirs, _, modes, channels = params.shape
    lanes = 128
    lags = upstream.shape[1]
    return pl.pallas_call(
        params_grad_body,
        out_shape=jax.ShapeDtypeStruct(params.shape, F32),
        grid=(dirs, channels // lanes),
        in_specs=[
            pl.BlockSpec((1, 4, modes, lanes), lambda k, c: (k, 0, 0, c)),
            pl.BlockSpec((1, lags, lanes), lambda k, c: (k, 0, c)),
        ],
        out_specs=pl.BlockSpec((1, 4, modes, lanes), lambda k, c: (k, 0, 0, c)),
        scratch_shapes=[
            pltpu.VMEM((lags // LOW, modes, lanes), F32),
            pltpu.VMEM((lags // LOW, modes, lanes), F32),
            pltpu.VMEM((4, modes, lanes), F32),
            pltpu.VMEM((4, modes, lanes), F32),
        ],
        compiler_params=pltpu.CompilerParams(vmem_limit_bytes=VMEM),
        name="params_grad",
    )(params, upstream)


def norm_stats(rows):
    centered = rows - jnp.mean(rows, axis=1, keepdims=True)
    inv_std = lax.rsqrt(jnp.mean(centered * centered, axis=1, keepdims=True) + 1e-05)
    return centered * inv_std, inv_std


def in_body(*refs):
    pieces = refs[:-8]
    gain_ref, fw_ref, bw_ref, normed_ref, fa_ref, fs_ref, ba_ref, bs_ref = refs[-8:]

    @pl.when(pl.program_id(0) == 0)
    def _():
        for index, piece in enumerate(pieces):
            rows = piece.shape[0]
            unit, _ = norm_stats(piece[...].astype(F32))
            normed_ref[pl.ds(index * rows, rows), :] = (unit * gain_ref[...]).astype(BF16)

    for w_ref, a_ref, s_ref in ((fw_ref, fa_ref, fs_ref), (bw_ref, ba_ref, bs_ref)):
        for start in range(0, normed_ref.shape[0], BLOCK):
            rows = pl.ds(start, BLOCK)
            act, slope = gelu_pair(dot(normed_ref[rows, :], w_ref[...]))
            a_ref[rows, :] = act.astype(a_ref.dtype)
            s_ref[rows, :] = slope.astype(s_ref.dtype)


def in_proj(pieces, gain, forward_weight, backward_weight):
    width, channels = forward_weight.shape
    rows = sum(piece.shape[0] for piece in pieces)
    tile = 512
    whole = lambda t: (0, 0)
    column = lambda t: (0, t)
    return pl.pallas_call(
        in_body,
        out_shape=[
            jax.ShapeDtypeStruct((rows, width), BF16),
            jax.ShapeDtypeStruct((rows, channels), BF16),
            jax.ShapeDtypeStruct((rows, channels), F32),
            jax.ShapeDtypeStruct((rows, channels), BF16),
            jax.ShapeDtypeStruct((rows, channels), F32),
        ],
        grid=(channels // tile,),
        in_specs=[pl.BlockSpec(piece.shape, whole) for piece in pieces]
        + [
            pl.BlockSpec((1, width), whole),
            pl.BlockSpec((width, tile), column),
            pl.BlockSpec((width, tile), column),
        ],
        out_specs=[pl.BlockSpec((rows, width), whole)]
        + [pl.BlockSpec((rows, tile), column)] * 4,
        compiler_params=pltpu.CompilerParams(vmem_limit_bytes=VMEM),
        cost_estimate=pl.CostEstimate(
            flops=4 * rows * width * channels, bytes_accessed=20_000_000, transcendentals=0
        ),
        name="in_proj",
    )(*pieces, gain.reshape(1, -1), forward_weight, backward_weight)


def value_body(normed_ref, w_ref, a_ref, s_ref):
    for start in range(0, normed_ref.shape[0], BLOCK):
        rows = pl.ds(start, BLOCK)
        act, slope = gelu_pair(dot(normed_ref[rows, :], w_ref[...]))
        a_ref[rows, :] = act
        s_ref[rows, :] = slope


def value_proj(normed, weight):
    rows, width = normed.shape
    hidden = weight.shape[1]
    tile = 512
    whole = lambda t: (0, 0)
    column = lambda t: (0, t)
    return pl.pallas_call(
        value_body,
        out_shape=[jax.ShapeDtypeStruct((rows, hidden), F32)] * 2,
        grid=(hidden // tile,),
        in_specs=[pl.BlockSpec((rows, width), whole), pl.BlockSpec((width, tile), column)],
        out_specs=[pl.BlockSpec((rows, tile), column)] * 2,
        compiler_params=pltpu.CompilerParams(vmem_limit_bytes=VMEM),
        cost_estimate=pl.CostEstimate(
            flops=2 * rows * width * hidden, bytes_accessed=18_000_000, transcendentals=0
        ),
        name="value_proj",
    )(normed, weight)


def row_block(ref, section, seq, local):
    parts = BLOCK // local
    pieces = []
    for part in range(parts):
        place = (section * parts + part) ^ seq
        pieces.append((pl.multiple_of(place * local, local), local))
    return pieces


def load_block(ref, section, seq, local):
    pieces = [ref[pl.ds(start, size), :] for start, size in row_block(ref, section, seq, local)]
    return pieces[0] if len(pieces) == 1 else jnp.concatenate(pieces, axis=0)


def store_block(ref, section, seq, local, value):
    offset = 0
    for start, size in row_block(ref, section, seq, local):
        ref[pl.ds(start, size), :] = value[offset : offset + size].astype(ref.dtype)
        offset += size


def spectrum(table_ref, block):
    return dot(table_ref[...], jnp.concatenate([block, block], axis=0))


def split_store(high_ref, low_ref, index, rows, lanes, value):
    high = value.astype(BF16)
    high_ref[index, rows, lanes] = high
    low_ref[index, rows, lanes] = (value - high.astype(F32)).astype(BF16)


def inverse(inverse_ref, high_ref, low_ref, index):
    return (
        dot(inverse_ref[0], high_ref[index])
        + dot(inverse_ref[0], low_ref[index])
        + dot(inverse_ref[1], high_ref[index])
    )


CHUNK = 16


def chunks(lanes):
    for parity in range(2):
        for start in range(parity * HALF_FREQ, (parity + 1) * HALF_FREQ, CHUNK):
            for lane in range(0, lanes, 128):
                yield parity, pl.ds(start, CHUNK), pl.ds(FREQ + start, CHUNK), pl.ds(lane, 128)


def load_spectra(ref, re_rows, im_rows, lanes):
    return [(ref[i, re_rows, lanes], ref[i, im_rows, lanes]) for i in range(SECTIONS)]


def turned(value, parity):
    return (-value[1], value[0]) if parity == 0 else (value[1], -value[0])


def cadd(first, second):
    return (first[0] + second[0], first[1] + second[1])


def band_spectra(parts, parity, longer):
    bands = [parts[0]]
    for m in range(1, SECTIONS):
        re, im = cadd(parts[m], turned(parts[m - 1], parity))
        bands.append((re * longer, im * longer))
    return bands


def cfma(total, first, second, conj):
    if conj:
        re = first[0] * second[0] + first[1] * second[1]
        im = first[0] * second[1] - first[1] * second[0]
    else:
        re = first[0] * second[0] - first[1] * second[1]
        im = first[0] * second[1] + first[1] * second[0]
    return (re, im) if total is None else (total[0] + re, total[1] + im)


def conv_spectra(bands, values, ahead):
    outs = []
    for i in range(SECTIONS):
        total = None
        for m in range(SECTIONS):
            source = i + m if ahead else i - m
            if 0 <= source < SECTIONS:
                total = cfma(total, bands[m], values[source], ahead)
        outs.append(total)
    return outs


def conv_fwd_body(
    info_ref, table_ref, inverse_ref, xf_ref, xb_ref, kernel_ref, prod_ref, al_ref, ag_ref,
    x_spec, k_spec, y_high, y_low, *, local,
):
    seq = info_ref[1]
    longer = info_ref[2].astype(F32)
    lanes_all = xf_ref.shape[1]
    for direction, (x_ref, out_ref) in enumerate(((xf_ref, al_ref), (xb_ref, ag_ref))):
        for i in range(SECTIONS):
            x_spec[i] = spectrum(table_ref, load_block(x_ref, i, seq, local))
            k_spec[i] = spectrum(table_ref, kernel_ref[direction, pl.ds(i * BLOCK, BLOCK), :])
        for parity, re_rows, im_rows, lanes in chunks(lanes_all):
            bands = band_spectra(load_spectra(k_spec, re_rows, im_rows, lanes), parity, longer)
            values = load_spectra(x_spec, re_rows, im_rows, lanes)
            for i, (re, im) in enumerate(conv_spectra(bands, values, direction == 1)):
                split_store(y_high, y_low, i, re_rows, lanes, re)
                split_store(y_high, y_low, i, im_rows, lanes, im)
        for i in range(SECTIONS):
            store_block(out_ref, i, seq, local, inverse(inverse_ref, y_high, y_low, i))
    prod_ref[...] = (al_ref[...] * ag_ref[...]).astype(BF16)


def conv_fwd(info, tables, act_forward, act_backward, kernel_low, local):
    rows, channels = act_forward.shape
    lanes = 256
    whole = lambda c, info: (0, 0)
    whole3 = lambda c, info: (0, 0, 0)
    column = lambda c, info: (0, c)
    forward, back = tables
    return pl.pallas_call(
        functools.partial(conv_fwd_body, local=local),
        out_shape=[
            jax.ShapeDtypeStruct((rows, channels), BF16),
            jax.ShapeDtypeStruct((rows, channels), F32),
            jax.ShapeDtypeStruct((rows, channels), F32),
        ],
        grid_spec=pltpu.PrefetchScalarGridSpec(
            num_scalar_prefetch=1,
            grid=(channels // lanes,),
            in_specs=[
                pl.BlockSpec(forward.shape, whole),
                pl.BlockSpec(back.shape, whole3),
                pl.BlockSpec((rows, lanes), column),
                pl.BlockSpec((rows, lanes), column),
                pl.BlockSpec((2, LENGTH, lanes), lambda c, info: (0, 0, c)),
            ],
            out_specs=[pl.BlockSpec((rows, lanes), column)] * 3,
            scratch_shapes=[
                pltpu.VMEM((SECTIONS, 2 * FREQ, lanes), F32),
                pltpu.VMEM((SECTIONS, 2 * FREQ, lanes), F32),
                pltpu.VMEM((SECTIONS, 2 * FREQ, lanes), BF16),
                pltpu.VMEM((SECTIONS, 2 * FREQ, lanes), BF16),
            ],
        ),
        compiler_params=pltpu.CompilerParams(vmem_limit_bytes=VMEM),
        cost_estimate=pl.CostEstimate(
            flops=10_000_000_000, bytes_accessed=16_000_000, transcendentals=0
        ),
        name="conv_fwd",
    )(info, forward, back, act_forward, act_backward, kernel_low)


def conv_bwd_body(
    info_ref, table_ref, inverse_ref, gp_ref, al_ref, ag_ref, xf_ref, xb_ref, sf_ref, sb_ref,
    kernel_ref, gf_ref, gb_ref, gk_ref, x_spec, k_spec, g_spec, y_high, y_low, h_high, h_low,
    *, local,
):
    seq = info_ref[1]
    longer = info_ref[2].astype(F32)
    lanes_all = xf_ref.shape[1]
    ways = ((xf_ref, ag_ref, sf_ref, gf_ref), (xb_ref, al_ref, sb_ref, gb_ref))
    for direction, (x_ref, other_ref, slope_ref, out_ref) in enumerate(ways):
        for i in range(SECTIONS):
            upstream = load_block(gp_ref, i, seq, local).astype(F32)
            upstream = (upstream * load_block(other_ref, i, seq, local)).astype(BF16)
            g_spec[i] = spectrum(table_ref, upstream)
            x_spec[i] = spectrum(table_ref, load_block(x_ref, i, seq, local))
            k_spec[i] = spectrum(table_ref, kernel_ref[direction, pl.ds(i * BLOCK, BLOCK), :])
        for parity, re_rows, im_rows, lanes in chunks(lanes_all):
            grads = load_spectra(g_spec, re_rows, im_rows, lanes)
            bands = band_spectra(load_spectra(k_spec, re_rows, im_rows, lanes), parity, longer)
            for i, (re, im) in enumerate(conv_spectra(bands, grads, direction == 0)):
                split_store(y_high, y_low, i, re_rows, lanes, re)
                split_store(y_high, y_low, i, im_rows, lanes, im)
            values = load_spectra(x_spec, re_rows, im_rows, lanes)
            after = None
            for m in reversed(range(SECTIONS)):
                total = None
                for i in range(m, SECTIONS):
                    if direction == 0:
                        total = cfma(total, values[i - m], grads[i], True)
                    else:
                        total = cfma(total, grads[i - m], values[i], True)
                if m:
                    total = (total[0] * longer, total[1] * longer)
                folded = total
                if after is not None:
                    folded = cadd(total, turned(after, 1 - parity))
                split_store(h_high, h_low, m, re_rows, lanes, folded[0])
                split_store(h_high, h_low, m, im_rows, lanes, folded[1])
                after = total
        for i in range(SECTIONS):
            grad_act = inverse(inverse_ref, y_high, y_low, i).astype(BF16).astype(F32)
            grad_in = grad_act * load_block(slope_ref, i, seq, local)
            store_block(out_ref, i, seq, local, grad_in)
            gk_ref[direction, pl.ds(i * BLOCK, BLOCK), :] = inverse(
                inverse_ref, h_high, h_low, i
            ).astype(BF16)


def conv_bwd(info, tables, grad_product, along, against, act_f, act_b, slope_f, slope_b, kernel_low, local):
    rows, channels = act_f.shape
    lanes = 256
    whole = lambda c, info: (0, 0)
    whole3 = lambda c, info: (0, 0, 0)
    column = lambda c, info: (0, c)
    column3 = lambda c, info: (0, 0, c)
    forward, back = tables
    return pl.pallas_call(
        functools.partial(conv_bwd_body, local=local),
        out_shape=[
            jax.ShapeDtypeStruct((rows, channels), BF16),
            jax.ShapeDtypeStruct((rows, channels), BF16),
            jax.ShapeDtypeStruct((2, LENGTH, channels), BF16),
        ],
        grid_spec=pltpu.PrefetchScalarGridSpec(
            num_scalar_prefetch=1,
            grid=(channels // lanes,),
            in_specs=[
                pl.BlockSpec(forward.shape, whole),
                pl.BlockSpec(back.shape, whole3),
            ]
            + [pl.BlockSpec((rows, lanes), column)] * 7
            + [pl.BlockSpec((2, LENGTH, lanes), column3)],
            out_specs=[
                pl.BlockSpec((rows, lanes), column),
                pl.BlockSpec((rows, lanes), column),
                pl.BlockSpec((2, LENGTH, lanes), column3),
            ],
            scratch_shapes=[pltpu.VMEM((SECTIONS, 2 * FREQ, lanes), F32)] * 3
            + [pltpu.VMEM((SECTIONS, 2 * FREQ, lanes), BF16)] * 4,
        ),
        compiler_params=pltpu.CompilerParams(vmem_limit_bytes=VMEM),
        cost_estimate=pl.CostEstimate(
            flops=20_000_000_000, bytes_accessed=30_000_000, transcendentals=0
        ),
        name="conv_bwd",
    )(info, forward, back, grad_product, along, against, act_f, act_b, slope_f, slope_b, kernel_low)


def middle_body(prod_ref, cot_ref, uw_ref, ow_ref, va_ref, vs_ref, gated_ref, du_ref, dv_ref):
    for start in range(0, prod_ref.shape[0], BLOCK):
        rows = pl.ds(start, BLOCK)
        update_act, update_slope = gelu_pair(dot(prod_ref[rows, :], uw_ref[...]))
        grad_gated = dot_rt(cot_ref[rows, :], ow_ref[...])
        value_act = va_ref[rows, :]
        gated_ref[rows, :] = (update_act * value_act).astype(BF16)
        du_ref[rows, :] = (grad_gated * value_act * update_slope).astype(BF16)
        dv_ref[rows, :] = (grad_gated * update_act * vs_ref[rows, :]).astype(BF16)


def middle(product, cot, update_weight, output_weight, value_act, value_slope):
    rows, channels = product.shape
    hidden, width = output_weight.shape
    tile = 512
    whole = lambda t: (0, 0)
    column = lambda t: (0, t)
    return pl.pallas_call(
        middle_body,
        out_shape=[jax.ShapeDtypeStruct((rows, hidden), BF16)] * 3,
        grid=(hidden // tile,),
        in_specs=[
            pl.BlockSpec((rows, channels), whole),
            pl.BlockSpec((rows, width), whole),
            pl.BlockSpec((channels, tile), column),
            pl.BlockSpec((tile, width), lambda t: (t, 0)),
            pl.BlockSpec((rows, tile), column),
            pl.BlockSpec((rows, tile), column),
        ],
        out_specs=[pl.BlockSpec((rows, tile), column)] * 3,
        compiler_params=pltpu.CompilerParams(vmem_limit_bytes=VMEM),
        cost_estimate=pl.CostEstimate(
            flops=2 * rows * hidden * (channels + width), bytes_accessed=36_000_000, transcendentals=0
        ),
        name="middle",
    )(product, cot, update_weight, output_weight, value_act, value_slope)


def weight_grad_body(info_ref, lhs_ref, rhs_ref, send_ref, keep_ref, total, *, groups):
    core = info_ref[0]
    total[...] = dot_lt(lhs_ref[...], rhs_ref[...])
    size = total.shape[0] // (2 * groups)
    for group in range(groups):
        other = pl.multiple_of((2 * group + 1 - core) * size, 8)
        mine = pl.multiple_of((2 * group + core) * size, 8)
        send_ref[group] = total[pl.ds(other, size), :].astype(BF16)
        keep_ref[group] = total[pl.ds(mine, size), :].astype(BF16)


def weight_grad(info, lhs, rhs, n_dp, tile):
    rows, height = lhs.shape
    columns = rhs.shape[1]
    groups = n_dp // 2
    size = height // n_dp
    out_spec = pl.BlockSpec((groups, size, tile), lambda t, info: (0, 0, t))
    return pl.pallas_call(
        functools.partial(weight_grad_body, groups=groups),
        out_shape=[jax.ShapeDtypeStruct((groups, size, columns), BF16)] * 2,
        grid_spec=pltpu.PrefetchScalarGridSpec(
            num_scalar_prefetch=1,
            grid=(columns // tile,),
            in_specs=[
                pl.BlockSpec((rows, height), lambda t, info: (0, 0)),
                pl.BlockSpec((rows, tile), lambda t, info: (0, t)),
            ],
            out_specs=[out_spec, out_spec],
            scratch_shapes=[pltpu.VMEM((height, tile), F32)],
        ),
        compiler_params=pltpu.CompilerParams(vmem_limit_bytes=VMEM),
        cost_estimate=pl.CostEstimate(
            flops=2 * rows * height * columns, bytes_accessed=2 * height * columns, transcendentals=0
        ),
        name="weight_grad",
    )(info, lhs, rhs)


def out_body(*refs):
    pieces = refs[:-10]
    (cot_ref, gain_ref, gv_ref, df_ref, db_ref, fw_ref, bw_ref, tg_ref, gg_ref, total) = refs[-10:]
    step = pl.program_id(0)

    @pl.when(step == 0)
    def _():
        total[...] = gv_ref[...]

    total[...] += dot_rt(df_ref[...], fw_ref[...]) + dot_rt(db_ref[...], bw_ref[...])

    @pl.when(step == pl.num_programs(0) - 1)
    def _():
        ones = jnp.ones((pieces[0].shape[0], 128), BF16)
        gain_total = None
        for index, piece in enumerate(pieces):
            rows = pl.ds(index * piece.shape[0], piece.shape[0])
            unit, inv_std = norm_stats(piece[...].astype(F32))
            grad_normed = total[rows, :]
            terms = grad_normed * unit
            high = terms.astype(BF16)
            low = (terms - high.astype(F32)).astype(BF16)
            sums = dot_lt(high, ones) + dot_lt(low, ones)
            gain_total = sums if gain_total is None else gain_total + sums
            grad_unit = grad_normed * gain_ref[...]
            grad_input = inv_std * (
                grad_unit
                - jnp.mean(grad_unit, axis=1, keepdims=True)
                - unit * jnp.mean(grad_unit * unit, axis=1, keepdims=True)
            )
            tg_ref[rows, :] = (cot_ref[rows, :].astype(F32) + grad_input).astype(BF16)
        gg_ref[...] = gain_total


def out_proj(pieces, cot, gain, grad_value_part, grad_f, grad_b, forward_weight, backward_weight):
    rows, width = cot.shape
    channels = grad_f.shape[1]
    tile = 512
    whole = lambda t: (0, 0)
    column = lambda t: (0, t)
    return pl.pallas_call(
        out_body,
        out_shape=[
            jax.ShapeDtypeStruct((rows, width), BF16),
            jax.ShapeDtypeStruct((width, 128), F32),
        ],
        grid=(channels // tile,),
        in_specs=[pl.BlockSpec(piece.shape, whole) for piece in pieces]
        + [
            pl.BlockSpec((rows, width), whole),
            pl.BlockSpec((1, width), whole),
            pl.BlockSpec((rows, width), whole),
            pl.BlockSpec((rows, tile), column),
            pl.BlockSpec((rows, tile), column),
            pl.BlockSpec((width, tile), column),
            pl.BlockSpec((width, tile), column),
        ],
        out_specs=[pl.BlockSpec((rows, width), whole), pl.BlockSpec((width, 128), whole)],
        scratch_shapes=[pltpu.VMEM((rows, width), F32)],
        compiler_params=pltpu.CompilerParams(vmem_limit_bytes=VMEM),
        cost_estimate=pl.CostEstimate(
            flops=4 * rows * width * channels, bytes_accessed=14_000_000, transcendentals=0
        ),
        name="out_proj",
    )(*pieces, cot, gain.reshape(1, -1), grad_value_part, grad_f, grad_b, forward_weight, backward_weight)


def swap(value, axis, mask):
    return lax.ppermute(value, axis, [(i, i ^ mask) for i in range(lax.axis_size(axis))])


def bit_view(value, dim, bit):
    size = value.shape[dim]
    low = 1 << bit
    return value.reshape(value.shape[:dim] + (size // (2 * low), 2, low) + value.shape[dim + 1 :])


def take_bit(value, dim, bit, which):
    picked = lax.dynamic_index_in_dim(bit_view(value, dim, bit), which, dim + 1, keepdims=False)
    shape = value.shape[:dim] + (value.shape[dim] // 2,) + value.shape[dim + 1 :]
    return picked.reshape(shape)


def total_of(pieces):
    total = pieces[0].astype(F32)
    for piece in pieces[1:]:
        total = total + piece.astype(F32)
    return total


def scatter_sum(send, keep, seq_bits, dp_index, seq_index):
    n_dp, n_seq = lax.axis_size("dp"), lax.axis_size("seq")
    shape = (n_dp // 2, n_seq, send.shape[1] // n_seq, send.shape[2])
    pieces = [keep.reshape(shape), swap(send, "dp", 1).reshape(shape)]
    steps = [("seq", 1, bit, bit, seq_index) for bit in seq_bits]
    steps += [("dp", 0, bit - 1, bit, dp_index) for bit in range(1, n_dp.bit_length() - 1)]
    done = {0: [], 1: []}
    for axis, dim, place, bit, index in steps:
        place = place - sum(1 for lower in done[dim] if lower < place)
        done[dim].append(bit - (1 if dim == 0 else 0))
        mine = (index >> bit) & 1
        other = total_of([take_bit(piece, dim, place, 1 - mine) for piece in pieces]).astype(BF16)
        pieces = [take_bit(piece, dim, place, mine) for piece in pieces]
        pieces.append(swap(other, axis, 1 << bit))
    return total_of(pieces).reshape(shape[2], shape[3])


def to_rows(value, n_seq):
    seq_index = lax.axis_index("seq")
    pieces = []
    for mask in range(n_seq):
        piece = lax.dynamic_index_in_dim(value, seq_index ^ mask, 0, keepdims=False)
        pieces.append(piece if mask == 0 else swap(piece, "seq", mask))
    return pieces


def from_rows(value, n_seq, local):
    seq_index = lax.axis_index("seq")
    result = jnp.zeros((n_seq, local, value.shape[1]), value.dtype)
    for mask in range(n_seq):
        piece = value[mask * local : (mask + 1) * local]
        piece = piece if mask == 0 else swap(piece, "seq", mask)
        result = lax.dynamic_update_index_in_dim(result, piece, seq_index ^ mask, 0)
    return result


def on_device(
    tokens,
    doc_ids,
    norm_gain,
    value_weight,
    forward_weight,
    backward_weight,
    update_weight,
    output_weight,
    kernel_params,
    cotangent,
):
    n_dp, n_seq = lax.axis_size("dp"), lax.axis_size("seq")
    dp_index, seq_index = lax.axis_index("dp"), lax.axis_index("seq")
    local = tokens.shape[1]
    channels = forward_weight.shape[1]
    own_channels = kernel_params.shape[3]
    core = dp_index % 2
    docs = lax.dynamic_index_in_dim(doc_ids, seq_index, 0, keepdims=False)
    longer = (docs[0] == docs[-1]).astype(jnp.int32)
    info = jnp.stack([core, seq_index, longer]).astype(jnp.int32)
    tables = fourier_tables()

    token_pieces = to_rows(tokens, n_seq)
    half = kernel_gen(info, kernel_params)
    halves = jnp.zeros((2, half.shape[1], n_seq, own_channels), BF16)
    for mask in range(n_seq):
        piece = half if mask == 0 else swap(half, "seq", mask)
        halves = lax.dynamic_update_index_in_dim(halves, piece, seq_index ^ mask, 2)
    halves = halves.reshape(2, half.shape[1], channels)
    others = swap(halves, "dp", 1)
    kernel_low = jnp.where(
        core == 0,
        jnp.concatenate([halves, others], axis=1),
        jnp.concatenate([others, halves], axis=1),
    )

    normed, act_f, slope_f, act_b, slope_b = in_proj(
        token_pieces, norm_gain, forward_weight, backward_weight
    )
    value_act, value_slope = value_proj(normed, value_weight)
    cot = jnp.concatenate(to_rows(cotangent, n_seq), axis=0)
    product, along, against = conv_fwd(info, tables, act_f, act_b, kernel_low, local)
    gated, grad_update_in, grad_value_in = middle(
        product, cot, update_weight, output_weight, value_act, value_slope
    )

    seq_bits = list(range(n_seq.bit_length() - 1))
    up, down = seq_bits, seq_bits[::-1]
    hidden = update_weight.shape[1]
    update_send = weight_grad(info, product, grad_update_in, n_dp, 512)
    columns = hidden // 2
    update_first = scatter_sum(
        update_send[0][:, :, :columns], update_send[1][:, :, :columns], up, dp_index, seq_index
    )
    update_second = scatter_sum(
        update_send[0][:, :, columns:], update_send[1][:, :, columns:], down, dp_index, seq_index
    )
    value_grad = scatter_sum(
        *weight_grad(info, normed, grad_value_in, n_dp, 512), up, dp_index, seq_index
    )
    output_grad = scatter_sum(
        *weight_grad(info, gated, cot, n_dp, 256), down, dp_index, seq_index
    )

    tokens_flat = jnp.concatenate(token_pieces, axis=0)
    layer_rows = (tokens_flat.astype(F32) + dot(gated, output_weight)).astype(BF16)
    layer_out = from_rows(layer_rows, n_seq, local)

    grad_product = dot_rt(grad_update_in, update_weight).astype(BF16)
    grad_f, grad_b, grad_kernel = conv_bwd(
        info, tables, grad_product, along, against, act_f, act_b, slope_f, slope_b, kernel_low, local
    )
    grad_value_part = dot_rt(grad_value_in, value_weight)
    tokens_grad_rows, gain_columns = out_proj(
        token_pieces, cot, norm_gain, grad_value_part, grad_f, grad_b, forward_weight, backward_weight
    )
    tokens_grad = from_rows(tokens_grad_rows, n_seq, local)

    lags = LENGTH // 2
    own_half = lax.dynamic_slice_in_dim(grad_kernel, core * lags, lags, 1)
    other_half = lax.dynamic_slice_in_dim(grad_kernel, (1 - core) * lags, lags, 1)
    arrived = swap(other_half, "dp", 1)
    summed = (own_half.astype(F32) + arrived.astype(F32)).reshape(2, lags, n_seq, own_channels)
    pieces = []
    for mask in range(n_seq):
        piece = lax.dynamic_index_in_dim(summed, seq_index ^ mask, 2, keepdims=False)
        pieces.append(piece if mask == 0 else swap(piece.astype(BF16), "seq", mask))
    total = total_of(pieces)
    for bit in range(1, n_dp.bit_length() - 1):
        low_total = total.astype(BF16)
        total = low_total.astype(F32) + swap(low_total, "dp", 1 << bit).astype(F32)
    total = total.astype(BF16)
    others = swap(total, "dp", 1)
    upstream = jnp.where(
        core == 0,
        jnp.concatenate([total, others], axis=1),
        jnp.concatenate([others, total], axis=1),
    )
    modes_own = kernel_params.shape[2] // n_dp
    params_own = lax.dynamic_slice_in_dim(kernel_params, dp_index * modes_own, modes_own, 2)
    params_grad = params_grad_of(params_own, upstream)

    inner_grads = jnp.concatenate([grad_f, grad_b], axis=1)
    inner_send, inner_keep = weight_grad(info, normed, inner_grads, n_dp, 512)
    gain_view = gain_columns.astype(BF16).reshape(n_dp // 2, 2, -1, 128)
    inner_send = jnp.concatenate(
        [inner_send, lax.dynamic_index_in_dim(gain_view, 1 - core, 1, keepdims=False)], axis=2
    )
    inner_keep = jnp.concatenate(
        [inner_keep, lax.dynamic_index_in_dim(gain_view, core, 1, keepdims=False)], axis=2
    )
    inner_grad = scatter_sum(inner_send, inner_keep, up, dp_index, seq_index)

    return (
        layer_out,
        tokens_grad,
        inner_grad[:, 2 * channels],
        value_grad,
        inner_grad[:, :channels],
        inner_grad[:, channels : 2 * channels],
        jnp.concatenate([update_first, update_second], axis=1),
        output_grad,
        params_grad,
    )


def solution(mesh):
    placed = (
        P("dp", "seq", None),
        P("dp", None),
        P(),
        P(),
        P(),
        P(),
        P(),
        P(),
        P(None, None, None, "seq"),
        P("dp", "seq", None),
    )
    return jax.shard_map(
        on_device,
        mesh=mesh,
        in_specs=placed,
        out_specs=(
            P("dp", "seq", None),
            P("dp", "seq", None),
            P(("dp", "seq")),
            P(("dp", "seq"), None),
            P(("dp", "seq"), None),
            P(("dp", "seq"), None),
            P(("dp", "seq"), None),
            P(("dp", "seq"), None),
            P(None, None, "dp", "seq"),
        ),
        check_vma=False,
    )
```

```python
import functools
import math

import jax
import jax.numpy as jnp
import ml_dtypes
import numpy as np
from jax import lax
from jax.experimental import pallas as pl
from jax.experimental.pallas import tpu as pltpu
from jax.sharding import PartitionSpec as P

LENGTH = 512
BLOCK = 128
SECTIONS = LENGTH // BLOCK
FREQ = 128
HALF_FREQ = FREQ // 2
LOW = 16
INNER = 768
HIDDEN_TILE = 512
ANY = pl.BlockSpec(memory_space=pl.ANY)
VMEM = 56 * 1024 * 1024
FULL_VMEM = 63 * 1024 * 1024
BF16 = jnp.bfloat16
F32 = jnp.float32


def cost(microseconds):
    return pl.CostEstimate(flops=int(microseconds * 2e+07), bytes_accessed=0, transcendentals=0)


def dot(first_mat, second_mat):
    return jnp.dot(first_mat, second_mat, preferred_element_type=F32)


def dot_rt(first_mat, second_mat):
    return lax.dot_general(
        first_mat, second_mat, (((1,), (1,)), ((), ())), preferred_element_type=F32
    )


def dot_lt(first_mat, second_mat):
    return lax.dot_general(
        first_mat, second_mat, (((0,), (0,)), ((), ())), preferred_element_type=F32
    )


def fourier_tables():
    order = np.concatenate([np.arange(0, FREQ, 2), np.arange(1, FREQ, 2)])
    angle = 2.0 * np.pi * (order[:, None] + 0.5) * np.arange(BLOCK)[None, :] / (2 * BLOCK)
    table = np.concatenate([np.cos(angle), -np.sin(angle)], axis=0)
    high = table.astype(ml_dtypes.bfloat16)
    low = (table - high.astype(np.float64)).astype(ml_dtypes.bfloat16)
    forward = np.concatenate([high, low], axis=1)
    scale = ml_dtypes.bfloat16(1.0 / FREQ)
    inverse = np.stack([high.T * scale, low.T * scale]).astype(ml_dtypes.bfloat16)
    return jnp.asarray(forward), jnp.asarray(inverse)


def gelu_pair(v):
    cdf = 0.5 * lax.erf(v * (1.0 / math.sqrt(2.0))) + 0.5
    bell = jnp.exp(v * v * -0.5)
    return v * cdf, cdf + v * (1.0 / math.sqrt(2.0 * math.pi)) * bell


def cmul(first, second):
    return (
        first[0] * second[0] - first[1] * second[1],
        first[0] * second[1] + first[1] * second[0],
    )


def turn_of(angle):
    part = angle * 0.25
    square = part * part
    sin = part * (1.0 + square * (-1 / 6 + square * (1 / 120 + square * (-1 / 5040 + square / 362880))))
    cos = 1.0 + square * (
        -0.5 + square * (1 / 24 + square * (-1 / 720 + square * (1 / 40320 - square / 3628800)))
    )
    for _ in range(2):
        cos, sin = 1.0 - 2.0 * sin * sin, 2.0 * sin * cos
    return cos, sin


def powers_of(decay, frequency, count):
    mag = jnp.exp(-decay)
    cos, sin = turn_of(frequency)
    powers = [(mag * cos, mag * sin)]
    for _ in range(count - 1):
        powers.append(cmul(powers[-1], powers[-1]))
    return powers


def kernel_gen_body(info_ref, par_ref, out_ref, low_re, low_im, total_ref):
    channels = par_ref.shape[3]
    width = 128 if channels % 128 == 0 else channels
    for lane in range(0, channels, width):
        lanes = pl.ds(lane, width)
        powers = powers_of(par_ref[0, 0, :, lanes], par_ref[0, 1, :, lanes], 9)
        current = (jnp.ones_like(powers[0][0]), jnp.zeros_like(powers[0][0]))
        for j in range(LOW):
            low_re[j, :, lanes] = current[0]
            low_im[j, :, lanes] = current[1]
            current = cmul(current, powers[0])
        second_half = info_ref[0] == 1
        start = (
            jnp.where(second_half, powers[8][0], 1.0),
            jnp.where(second_half, powers[8][1], 0.0),
        )

        def some_lags(i, highs, lanes=lanes, place=lane // width, step=powers[5]):
            for j in range(LOW):
                re, im = low_re[j, :, lanes], low_im[j, :, lanes]
                for half, high in enumerate(highs):
                    terms = high[0] * re - high[1] * im
                    row = pl.ds((2 * i + half) * LOW + j, 1)
                    total_ref[place, row, :] = jnp.sum(terms, axis=0, keepdims=True)
            return tuple(cmul(high, step) for high in highs)

        first = cmul((par_ref[0, 2, :, lanes], par_ref[0, 3, :, lanes]), start)
        lax.fori_loop(
            0, out_ref.shape[1] // (2 * LOW), some_lags, (first, cmul(first, powers[4]))
        )
    for place in range(channels // width):
        out_ref[0, :, place * width : (place + 1) * width] = total_ref[place].astype(BF16)


def kernel_gen(info, params):
    dirs, kinds, modes, channels = params.shape
    width = 128 if channels % 128 == 0 else channels
    lags = LENGTH // 2
    return pl.pallas_call(
        kernel_gen_body,
        out_shape=jax.ShapeDtypeStruct((dirs, lags, channels), BF16),
        grid_spec=pltpu.PrefetchScalarGridSpec(
            num_scalar_prefetch=1,
            grid=(dirs,),
            in_specs=[pl.BlockSpec((1, kinds, modes, channels), lambda k, info: (k, 0, 0, 0))],
            out_specs=pl.BlockSpec((1, lags, channels), lambda k, info: (k, 0, 0)),
            scratch_shapes=[
                pltpu.VMEM((LOW, modes, channels), F32),
                pltpu.VMEM((LOW, modes, channels), F32),
                pltpu.VMEM((channels // width, lags, width), F32),
            ],
        ),
        compiler_params=pltpu.CompilerParams(vmem_limit_bytes=VMEM),
        cost_estimate=cost(9),
        name="kernel_gen",
    )(info, params)


def pass_body(*refs):
    pass


def pass_after(value, after):
    return pl.pallas_call(
        pass_body,
        out_shape=jax.ShapeDtypeStruct(value.shape, value.dtype),
        in_specs=[ANY] * (1 + len(after)),
        out_specs=ANY,
        input_output_aliases={0: 0},
        cost_estimate=cost(1),
        name="pass_after",
    )(value, *after)


def stack_body(*refs, count, inner):
    for index, ref in enumerate(refs[:count]):
        if inner:
            refs[-1][:, index] = ref[...]
        else:
            refs[-1][index] = ref[...]


def stack_pieces(pieces, after, inner=False):
    shape = pieces[0].shape
    out = (len(pieces),) + shape
    if inner:
        out = shape[:1] + (len(pieces),) + shape[1:]
    result = pl.pallas_call(
        functools.partial(stack_body, count=len(pieces), inner=inner),
        out_shape=jax.ShapeDtypeStruct(out, pieces[0].dtype),
        grid=(1,),
        in_specs=[pl.BlockSpec(shape, lambda t: (0,) * len(shape))] * len(pieces)
        + [ANY] * len(after),
        out_specs=pl.BlockSpec(out, lambda t: (0,) * len(out)),
        cost_estimate=cost(3),
        name="stack_pieces",
    )(*pieces, *after)
    return result.reshape((-1,) + shape[1:]) if inner else result


def params_grad_body(info_ref, par_ref, mine_ref, other_ref, *rest):
    out_ref, low_re, low_im, up_ref = rest[-4:]
    parts, rows = mine_ref.shape[:2]
    half = parts * rows // 2
    first_is_mine = info_ref[0] == 0
    for index in range(parts // 2):
        place = (pl.program_id(0) * (parts // 2) + index) ^ (info_ref[3] >> 1)
        mine, other = mine_ref[place].astype(F32), other_ref[place].astype(F32)
        up_ref[pl.ds(index * rows, rows), :] = jnp.where(first_is_mine, mine, other)
        up_ref[pl.ds(half + index * rows, rows), :] = jnp.where(first_is_mine, other, mine)
    powers = powers_of(par_ref[0, 0], par_ref[0, 1], 5)
    one = (jnp.ones_like(powers[0][0]), jnp.zeros_like(powers[0][0]))
    current = one
    for j in range(LOW):
        low_re[j] = current[0]
        low_im[j] = current[1]
        current = cmul(current, powers[0])
    zero = jnp.zeros_like(one[0])

    def some_lags(i, carry):
        high, plain, ramped = carry
        for part in range(4):
            first = pl.multiple_of((4 * i + part) * LOW, LOW)
            grads = up_ref[pl.ds(first, LOW), :]
            sums, ramps = [zero] * 2, [zero] * 2
            for j in reversed(range(LOW)):
                sums[0] = sums[0] + grads[j : j + 1, :] * low_re[j]
                sums[1] = sums[1] + grads[j : j + 1, :] * low_im[j]
                if j:
                    ramps = [ramps[0] + sums[0], ramps[1] + sums[1]]
            start = first.astype(F32)
            lagged = (ramps[0] + start * sums[0], ramps[1] + start * sums[1])
            plain = tuple(a + b for a, b in zip(plain, cmul(high, sums)))
            ramped = tuple(a + b for a, b in zip(ramped, cmul(high, lagged)))
            high = cmul(high, powers[4])
        return high, plain, ramped

    carry = (one, (zero, zero), (zero, zero))
    _, plain, ramped = lax.fori_loop(0, up_ref.shape[0] // (4 * LOW), some_lags, carry)
    real, imag = par_ref[0, 2], par_ref[0, 3]
    out_ref[0, 0] = imag * ramped[1] - real * ramped[0]
    out_ref[0, 1] = -(real * ramped[1] + imag * ramped[0])
    out_ref[0, 2] = plain[0]
    out_ref[0, 3] = -plain[1]


def params_grad_of(info, params, mine, other, n_dp, after):
    dirs, kinds, modes, channels = params.shape
    own = modes // n_dp
    place = lambda k, info: (k, 0, info[3], 0)
    if own % 8:
        params = lax.dynamic_slice_in_dim(params, lax.axis_index("dp") * own, own, 2)
        place = lambda k, info: (k, 0, 0, 0)
    return pl.pallas_call(
        params_grad_body,
        out_shape=jax.ShapeDtypeStruct((dirs, kinds, own, channels), F32),
        grid_spec=pltpu.PrefetchScalarGridSpec(
            num_scalar_prefetch=1,
            grid=(dirs,),
            in_specs=[
                pl.BlockSpec((1, kinds, own, channels), place),
                pl.BlockSpec(mine.shape, lambda k, info: (0, 0, 0)),
                pl.BlockSpec(mine.shape, lambda k, info: (0, 0, 0)),
            ]
            + [ANY] * len(after),
            out_specs=pl.BlockSpec((1, kinds, own, channels), lambda k, info: (k, 0, 0, 0)),
            scratch_shapes=[pltpu.VMEM((LOW, own, channels), F32)] * 2
            + [pltpu.VMEM((LENGTH, channels), F32)],
        ),
        compiler_params=pltpu.CompilerParams(vmem_limit_bytes=VMEM),
        cost_estimate=cost(5),
        name="params_grad",
    )(info, params, mine, other, *after)


def norm_stats(rows):
    centered = rows - jnp.mean(rows, axis=1, keepdims=True)
    inv_std = lax.rsqrt(jnp.mean(centered * centered, axis=1, keepdims=True) + 1e-05)
    return centered * inv_std, inv_std


def in_body(tokens_ref, gain_ref, *refs):
    *weight_refs, normed_ref = refs[:4]
    out_refs = refs[4:]

    @pl.when(pl.program_id(0) == 0)
    def _():
        for start in range(0, tokens_ref.shape[0], BLOCK):
            rows = pl.ds(start, BLOCK)
            unit, _ = norm_stats(tokens_ref[rows, :].astype(F32))
            normed_ref[rows, :] = (unit * gain_ref[...]).astype(BF16)

    size = 2 * BLOCK
    for index, w_ref in enumerate(weight_refs):
        a_ref, s_ref = out_refs[2 * index : 2 * index + 2]
        for start in range(0, normed_ref.shape[0], size):
            rows = pl.ds(start, size)
            act, slope = gelu_pair(dot(normed_ref[rows, :], w_ref[...]))
            a_ref[rows, :] = act.astype(a_ref.dtype)
            s_ref[rows, :] = slope.astype(s_ref.dtype)


def in_proj(tokens, gain, forward_weight, backward_weight, value_weight):
    width, channels = forward_weight.shape
    hidden = value_weight.shape[1]
    rows = tokens.shape[0]
    steps = 3
    whole = lambda t: (0, 0)
    column = lambda t: (0, t)
    widths = [weight.shape[1] // steps for weight in (forward_weight, backward_weight, value_weight)]
    out_widths = [channels] * 4 + [hidden] * 2
    return pl.pallas_call(
        in_body,
        out_shape=[
            jax.ShapeDtypeStruct((rows, out_width), BF16) for out_width in [width] + out_widths
        ],
        grid=(steps,),
        in_specs=[pl.BlockSpec((rows, width), whole), pl.BlockSpec((1, width), whole)]
        + [pl.BlockSpec((width, tile), column) for tile in widths],
        out_specs=[pl.BlockSpec((rows, width), whole)]
        + [pl.BlockSpec((rows, out_width // steps), column) for out_width in out_widths],
        compiler_params=pltpu.CompilerParams(vmem_limit_bytes=VMEM),
        cost_estimate=cost(14),
        name="in_proj",
    )(tokens, gain.reshape(1, -1), forward_weight, backward_weight, value_weight)


def load_block(ref, section):
    return ref[pl.ds(section * BLOCK, BLOCK), :]


def store_block(ref, section, value):
    ref[pl.ds(section * BLOCK, BLOCK), :] = value.astype(ref.dtype)


def spectra(table_ref, blocks, out_ref):
    wide = jnp.concatenate(blocks, axis=1)
    out_ref[...] = dot(table_ref[...], jnp.concatenate([wide, wide], axis=0))


def split_store(high_ref, low_ref, rows, columns, value):
    high_ref[rows, columns] = value.astype(BF16)


def inverse(inverse_ref, high_ref, low_ref):
    return dot(inverse_ref[0], high_ref[...])


CHUNK = 16


def chunks(width):
    for start in range(0, FREQ, CHUNK):
        for lane in range(0, width, 128):
            parity = start // HALF_FREQ
            columns = [pl.ds(i * width + lane, 128) for i in range(SECTIONS)]
            yield parity, pl.ds(start, CHUNK), pl.ds(FREQ + start, CHUNK), columns


def load_spectra(ref, re_rows, im_rows, columns):
    return [(ref[re_rows, column], ref[im_rows, column]) for column in columns]


def turned(value, parity):
    return (-value[1], value[0]) if parity == 0 else (value[1], -value[0])


def cadd(first, second):
    return (first[0] + second[0], first[1] + second[1])


def band_spectra(parts, parity, longer):
    bands = [parts[0]]
    for m in range(1, SECTIONS):
        re, im = cadd(parts[m], turned(parts[m - 1], parity))
        bands.append((re * longer, im * longer))
    return bands


def cfma(total, first, second, conj):
    if conj:
        re = first[0] * second[0] + first[1] * second[1]
        im = first[0] * second[1] - first[1] * second[0]
    else:
        re = first[0] * second[0] - first[1] * second[1]
        im = first[0] * second[1] + first[1] * second[0]
    return (re, im) if total is None else (total[0] + re, total[1] + im)


def conv_spectra(bands, values, ahead):
    outs = []
    for i in range(SECTIONS):
        total = None
        for m in range(SECTIONS):
            source = i + m if ahead else i - m
            if 0 <= source < SECTIONS:
                total = cfma(total, bands[m], values[source], ahead)
        outs.append(total)
    return outs


def tile_pieces(info_ref, count):
    return [j ^ (info_ref[1] & (count - 1)) for j in range(count)]


def kernel_blocks(info_ref, mine_ref, other_ref, direction):
    first_is_mine = info_ref[0] == 0
    places = tile_pieces(info_ref, mine_ref.shape[0])
    mine = [mine_ref[place, direction] for place in places]
    other = [other_ref[place, direction] for place in places]
    mine = mine[0] if len(mine) == 1 else jnp.concatenate(mine, axis=1)
    other = other[0] if len(other) == 1 else jnp.concatenate(other, axis=1)
    halves = [jnp.where(first_is_mine, mine, other), jnp.where(first_is_mine, other, mine)]
    per = halves[0].shape[0] // BLOCK
    return [half[i * BLOCK : (i + 1) * BLOCK] for half in halves for i in range(per)]


def conv_fwd_body(
    info_ref, table_ref, inverse_ref, xf_ref, xb_ref, mine_ref, other_ref, *rest
):
    prod_ref, al_ref, ag_ref = rest[-11:-8]
    scratch = rest[-8:]
    longer = info_ref[2].astype(F32)
    width = xf_ref.shape[1]
    for direction, (x_ref, out_ref) in enumerate(((xf_ref, al_ref), (xb_ref, ag_ref))):
        x_spec, k_spec, y_high, y_low = scratch[4 * direction : 4 * direction + 4]
        blocks = [load_block(x_ref, i) for i in range(SECTIONS)]
        spectra(table_ref, blocks, x_spec)
        spectra(table_ref, kernel_blocks(info_ref, mine_ref, other_ref, direction), k_spec)
        for parity, re_rows, im_rows, columns in chunks(width):
            bands = band_spectra(load_spectra(k_spec, re_rows, im_rows, columns), parity, longer)
            values = load_spectra(x_spec, re_rows, im_rows, columns)
            for column, (re, im) in zip(columns, conv_spectra(bands, values, direction == 1)):
                split_store(y_high, y_low, re_rows, column, re)
                split_store(y_high, y_low, im_rows, column, im)
        result = inverse(inverse_ref, y_high, y_low)
        for i in range(SECTIONS):
            store_block(out_ref, i, result[:, i * width : (i + 1) * width])
    prod_ref[...] = (al_ref[...] * ag_ref[...]).astype(BF16)


def kernel_spec(own, count):
    shift = count.bit_length() - 1
    return pl.BlockSpec(
        (count, 2, LENGTH // 2, own), lambda c, info: (c ^ (info[1] >> shift), 0, 0, 0)
    )


def tile_of(own):
    count = 1
    while (count * own) % 128:
        count *= 2
    return count, count * own


def conv_fwd(info, tables, act_forward, act_backward, mine, other, after):
    rows, channels = act_forward.shape
    count, width = tile_of(mine.shape[3])
    whole = lambda c, info: (0, 0)
    whole3 = lambda c, info: (0, 0, 0)
    column = lambda c, info: (0, c)
    forward, back = tables
    wide = SECTIONS * width
    return pl.pallas_call(
        conv_fwd_body,
        out_shape=[
            jax.ShapeDtypeStruct((rows, channels), BF16),
            jax.ShapeDtypeStruct((rows, channels), F32),
            jax.ShapeDtypeStruct((rows, channels), F32),
        ],
        grid_spec=pltpu.PrefetchScalarGridSpec(
            num_scalar_prefetch=1,
            grid=(channels // width,),
            in_specs=[
                pl.BlockSpec(forward.shape, whole),
                pl.BlockSpec(back.shape, whole3),
                pl.BlockSpec((rows, width), column),
                pl.BlockSpec((rows, width), column),
                kernel_spec(mine.shape[3], count),
                kernel_spec(mine.shape[3], count),
            ]
            + [ANY] * len(after),
            out_specs=[pl.BlockSpec((rows, width), column)] * 3,
            scratch_shapes=[
                pltpu.VMEM((2 * FREQ, wide), F32),
                pltpu.VMEM((2 * FREQ, wide), F32),
                pltpu.VMEM((2 * FREQ, wide), BF16),
                pltpu.VMEM((2 * FREQ, wide), BF16),
            ]
            * 2,
        ),
        compiler_params=pltpu.CompilerParams(vmem_limit_bytes=VMEM),
        cost_estimate=cost(17),
        name="conv_fwd",
    )(info, forward, back, act_forward, act_backward, mine, other, *after)


def conv_bwd_body(
    info_ref, table_ref, inverse_ref, gp_ref, al_ref, ag_ref, xf_ref, xb_ref, sf_ref, sb_ref,
    mine_ref, other_ref, *rest,
):
    gf_ref, gb_ref, keep_ref, send_ref = rest[-18:-14]
    scratch = rest[-14:]
    longer = info_ref[2].astype(F32)
    width = xf_ref.shape[1]
    ways = ((xf_ref, ag_ref, sf_ref, gf_ref), (xb_ref, al_ref, sb_ref, gb_ref))
    for direction, (x_ref, other_way, slope_ref, out_ref) in enumerate(ways):
        x_spec, k_spec, g_spec, y_high, y_low, h_high, h_low = scratch[7 * direction : 7 * direction + 7]
        upstream = [
            (
                load_block(gp_ref, i).astype(F32)
                * load_block(other_way, i)
            ).astype(BF16)
            for i in range(SECTIONS)
        ]
        spectra(table_ref, upstream, g_spec)
        spectra(table_ref, kernel_blocks(info_ref, mine_ref, other_ref, direction), k_spec)
        spectra(table_ref, [load_block(x_ref, i) for i in range(SECTIONS)], x_spec)
        for parity, re_rows, im_rows, columns in chunks(width):
            grads = load_spectra(g_spec, re_rows, im_rows, columns)
            bands = band_spectra(load_spectra(k_spec, re_rows, im_rows, columns), parity, longer)
            for column, (re, im) in zip(columns, conv_spectra(bands, grads, direction == 0)):
                split_store(y_high, y_low, re_rows, column, re)
                split_store(y_high, y_low, im_rows, column, im)
            values = load_spectra(x_spec, re_rows, im_rows, columns)
            above = None
            for m in reversed(range(SECTIONS)):
                total = None
                for i in range(m, SECTIONS):
                    if direction == 0:
                        total = cfma(total, values[i - m], grads[i], True)
                    else:
                        total = cfma(total, grads[i - m], values[i], True)
                if m:
                    total = (total[0] * longer, total[1] * longer)
                folded = total
                if above is not None:
                    folded = cadd(total, turned(above, 1 - parity))
                split_store(h_high, h_low, re_rows, columns[m], folded[0])
                split_store(h_high, h_low, im_rows, columns[m], folded[1])
                above = total
        result = inverse(inverse_ref, y_high, y_low)
        for i in range(SECTIONS):
            grad_act = result[:, i * width : (i + 1) * width].astype(BF16).astype(F32)
            slope = load_block(slope_ref, i).astype(F32)
            store_block(out_ref, i, grad_act * slope)
        result = inverse(inverse_ref, h_high, h_low).astype(BF16)
        first_is_mine = info_ref[0] == 0
        own, per = keep_ref.shape[3], keep_ref.shape[2]
        half = SECTIONS // 2
        for piece in range(keep_ref.shape[1]):
            for i in range(half):
                low = result[:, i * width + piece * own : i * width + (piece + 1) * own]
                top = (half + i) * width
                high = result[:, top + piece * own : top + (piece + 1) * own]
                for start in range(0, BLOCK, per):
                    place = ((direction * half + i) * BLOCK + start) // per
                    first, second = low[start : start + per], high[start : start + per]
                    keep_ref[place, piece] = jnp.where(first_is_mine, first, second)
                    send_ref[place, piece] = jnp.where(first_is_mine, second, first)


def conv_bwd(
    info, tables, grad_product, along, against, act_f, act_b, slope_f, slope_b, mine, other, parts,
    after,
):
    rows, channels = act_f.shape
    own = mine.shape[3]
    count, width = tile_of(own)
    whole = lambda c, info: (0, 0)
    whole3 = lambda c, info: (0, 0, 0)
    column = lambda c, info: (0, c)
    forward, back = tables
    wide = SECTIONS * width
    return pl.pallas_call(
        conv_bwd_body,
        out_shape=[
            jax.ShapeDtypeStruct((rows, channels), BF16),
            jax.ShapeDtypeStruct((rows, channels), BF16),
            jax.ShapeDtypeStruct((parts, mine.shape[0], LENGTH // parts, own), BF16),
            jax.ShapeDtypeStruct((parts, mine.shape[0], LENGTH // parts, own), BF16),
        ],
        grid_spec=pltpu.PrefetchScalarGridSpec(
            num_scalar_prefetch=1,
            grid=(channels // width,),
            in_specs=[
                pl.BlockSpec(forward.shape, whole),
                pl.BlockSpec(back.shape, whole3),
            ]
            + [pl.BlockSpec((rows, width), column)] * 7
            + [kernel_spec(own, count)] * 2
            + [ANY] * len(after),
            out_specs=[
                pl.BlockSpec((rows, width), column),
                pl.BlockSpec((rows, width), column),
                pl.BlockSpec((parts, count, LENGTH // parts, own), lambda c, info: (0, c, 0, 0)),
                pl.BlockSpec((parts, count, LENGTH // parts, own), lambda c, info: (0, c, 0, 0)),
            ],
            scratch_shapes=(
                [pltpu.VMEM((2 * FREQ, wide), F32)] * 3 + [pltpu.VMEM((2 * FREQ, wide), BF16)] * 4
            )
            * 2,
        ),
        compiler_params=pltpu.CompilerParams(vmem_limit_bytes=VMEM),
        cost_estimate=cost(28),
        name="conv_bwd",
    )(
        info, forward, back, grad_product, along, against, act_f, act_b, slope_f, slope_b,
        mine, other, *after,
    )


def packed_rows(total_ref, core, n_dp, n_seq, small, out_ref):
    size = total_ref.shape[0] // n_dp
    per = size // n_seq
    groups = n_dp // 2
    count = n_seq * small
    for group in range(groups):
        for place, which in enumerate((1 - core, core)):
            start = pl.multiple_of((2 * group + which) * size, 8)
            value = total_ref[pl.ds(start, size), :]
            for fold in range(per // small):
                first = fold * small
                rows = [value[s * per + first : s * per + first + small] for s in range(n_seq)]
                target = ((place * (per // small) + fold) * groups + group) * count
                out_ref[pl.ds(target, count), :] = jnp.concatenate(rows, axis=0).astype(out_ref.dtype)


def store_split(result, groups, folds, send_ref, keep_ref, offset):
    count = send_ref.shape[1]
    width = result.shape[1]
    for place, ref in enumerate((send_ref, keep_ref)):
        for fold in range(folds):
            for group in range(groups):
                first = ((place * folds + fold) * groups + group) * count
                columns = pl.ds(offset + fold * width, width)
                ref[group, :, columns] = result[first : first + count].astype(BF16)


def middle_body(
    info_ref, prod_ref, normed_ref, cot_ref, uw_ref, ow_ref, va_ref, vs_ref, *rest, n_dp, n_seq, small
):
    send_ref, keep_ref, og_ref, gated_ref, dv_ref, gp_ref, nt_ref = rest[:7]
    du_ref, pt_ref, flipped, gp_acc = rest[7:]
    step = pl.program_id(0)

    @pl.when(step == 0)
    def _():
        for source, target in ((prod_ref, pt_ref), (normed_ref, nt_ref)):
            rows = flipped.at[pl.ds(0, source.shape[1])]
            rows[...] = source[...].astype(F32).T
            packed_rows(rows, info_ref[0], n_dp, n_seq, small, target)
        gp_acc[...] = jnp.zeros_like(gp_acc)

    size = 2 * BLOCK
    for start in range(0, prod_ref.shape[0], size):
        rows = pl.ds(start, size)
        update_act, update_slope = gelu_pair(dot(prod_ref[rows, :], uw_ref[...]))
        grad_gated = dot_rt(cot_ref[rows, :], ow_ref[...])
        value_act = va_ref[rows, :].astype(F32)
        gated_ref[rows, :] = (update_act * value_act).astype(BF16)
        du_ref[rows, :] = (grad_gated * value_act * update_slope).astype(BF16)
        dv_ref[rows, :] = (grad_gated * update_act * vs_ref[rows, :].astype(F32)).astype(BF16)
    folds = prod_ref.shape[1] // normed_ref.shape[1]
    tile = uw_ref.shape[1]
    groups = n_dp // 2
    store_split(dot(pt_ref[...], du_ref[...]), groups, folds, send_ref, keep_ref, 0)
    store_split(dot(nt_ref[...], dv_ref[...]), groups, 1, send_ref, keep_ref, folds * tile)
    og_ref[...] = dot_lt(gated_ref[...], cot_ref[...]).astype(BF16)
    gp_acc[...] += dot_rt(du_ref[...], uw_ref[...])

    @pl.when(step == pl.num_programs(0) - 1)
    def _():
        gp_ref[...] = gp_acc[...].astype(BF16)


def middle(
    info, product, normed, cot, update_weight, output_weight, value_act, value_slope, n_dp, n_seq
):
    rows, channels = product.shape
    hidden, width = output_weight.shape
    tile = HIDDEN_TILE
    steps = hidden // tile
    small = width // (n_dp * n_seq)
    groups = n_dp // 2
    block = (channels // width + 1) * tile
    whole = lambda t, info: (0, 0)
    column = lambda t, info: (0, t)
    out_block = pl.BlockSpec((groups, n_seq * small, block), lambda t, info: (0, 0, t))
    return pl.pallas_call(
        functools.partial(middle_body, n_dp=n_dp, n_seq=n_seq, small=small),
        out_shape=[jax.ShapeDtypeStruct((groups, n_seq * small, steps * block), BF16)] * 2
        + [
            jax.ShapeDtypeStruct((hidden, width), BF16),
            jax.ShapeDtypeStruct((rows, hidden), BF16),
            jax.ShapeDtypeStruct((rows, hidden), BF16),
            jax.ShapeDtypeStruct((rows, channels), BF16),
            jax.ShapeDtypeStruct((width, rows), BF16),
        ],
        grid_spec=pltpu.PrefetchScalarGridSpec(
            num_scalar_prefetch=1,
            grid=(steps,),
            in_specs=[
                pl.BlockSpec((rows, channels), whole),
                pl.BlockSpec((rows, width), whole),
                pl.BlockSpec((rows, width), whole),
                pl.BlockSpec((channels, tile), column),
                pl.BlockSpec((tile, width), lambda t, info: (t, 0)),
                pl.BlockSpec((rows, tile), column),
                pl.BlockSpec((rows, tile), column),
            ],
            out_specs=[
                out_block,
                out_block,
                pl.BlockSpec((tile, width), lambda t, info: (t, 0)),
                pl.BlockSpec((rows, tile), column),
                pl.BlockSpec((rows, tile), column),
                pl.BlockSpec((rows, channels), whole),
                pl.BlockSpec((width, rows), whole),
            ],
            scratch_shapes=[
                pltpu.VMEM((rows, tile), BF16),
                pltpu.VMEM((channels, rows), BF16),
                pltpu.VMEM((channels, rows), F32),
                pltpu.VMEM((rows, channels), F32),
            ],
        ),
        compiler_params=pltpu.CompilerParams(vmem_limit_bytes=VMEM),
        cost_estimate=cost(40),
        name="middle",
    )(info, product, normed, cot, update_weight, output_weight, value_act, value_slope)


def layer_body(gated_ref, dv_ref, ow_ref, vw_ref, tokens_ref, *rest):
    layer_ref, gv_ref, lo_acc = rest[-3:]
    step = pl.program_id(0)

    @pl.when(step == 0)
    def _():
        lo_acc[...] = jnp.zeros_like(lo_acc)
        gv_ref[...] = jnp.zeros_like(gv_ref)

    lo_acc[...] += dot(gated_ref[...], ow_ref[...])
    gv_ref[...] += dot_rt(dv_ref[...], vw_ref[...])

    @pl.when(step == pl.num_programs(0) - 1)
    def _():
        layer_ref[...] = (tokens_ref[...].astype(F32) + lo_acc[...]).astype(BF16)


def layer_rows_of(gated, grad_value_in, output_weight, value_weight, tokens, after):
    rows, hidden = gated.shape
    width = output_weight.shape[1]
    tile = 1024
    whole = lambda t: (0, 0)
    column = lambda t: (0, t)
    return pl.pallas_call(
        layer_body,
        out_shape=[
            jax.ShapeDtypeStruct((rows, width), BF16),
            jax.ShapeDtypeStruct((rows, width), F32),
        ],
        grid=(hidden // tile,),
        in_specs=[
            pl.BlockSpec((rows, tile), column),
            pl.BlockSpec((rows, tile), column),
            pl.BlockSpec((tile, width), lambda t: (t, 0)),
            pl.BlockSpec((width, tile), column),
            pl.BlockSpec((rows, width), whole),
        ]
        + [ANY] * len(after),
        out_specs=[pl.BlockSpec((rows, width), whole)] * 2,
        scratch_shapes=[pltpu.VMEM((rows, width), F32)],
        compiler_params=pltpu.CompilerParams(vmem_limit_bytes=VMEM),
        cost_estimate=cost(9),
        name="layer_rows",
    )(gated, grad_value_in, output_weight, value_weight, tokens, *after)


def inner_grad_body(nt_ref, df_ref, db_ref, *rest, groups):
    send_ref, keep_ref = rest[-2:]
    tile = df_ref.shape[1]
    store_split(dot(nt_ref[...], df_ref[...]), groups, 1, send_ref, keep_ref, 0)
    store_split(dot(nt_ref[...], db_ref[...]), groups, 1, send_ref, keep_ref, tile)


def inner_weight_grad(normed_t, grad_f, grad_b, n_dp, n_seq, after):
    width, rows = normed_t.shape
    channels = grad_f.shape[1]
    small = width // (n_dp * n_seq)
    groups = n_dp // 2
    column = lambda t: (0, t)
    out_block = pl.BlockSpec((groups, n_seq * small, 2 * INNER), lambda t: (0, 0, t))
    return pl.pallas_call(
        functools.partial(inner_grad_body, groups=groups),
        out_shape=[jax.ShapeDtypeStruct((groups, n_seq * small, 2 * channels), BF16)] * 2,
        grid=(channels // INNER,),
        in_specs=[
            pl.BlockSpec((width, rows), lambda t: (0, 0)),
            pl.BlockSpec((rows, INNER), column),
            pl.BlockSpec((rows, INNER), column),
        ]
        + [ANY] * len(after),
        out_specs=[out_block, out_block],
        compiler_params=pltpu.CompilerParams(vmem_limit_bytes=VMEM),
        cost_estimate=cost(6),
        name="inner_weight_grad",
    )(normed_t, grad_f, grad_b, *after)


def out_body(
    tokens_ref, cot_ref, gain_ref, gv_ref, layer_ref, df_ref, db_ref, fw_ref, bw_ref, *rest
):
    out_ref, total = rest[-2:]
    step = pl.program_id(0)

    @pl.when(step == 0)
    def _():
        total[...] = gv_ref[...]

    total[...] += dot_rt(df_ref[...], fw_ref[...]) + dot_rt(db_ref[...], bw_ref[...])

    @pl.when(step == pl.num_programs(0) - 1)
    def _():
        size = out_ref.shape[2]
        for index in range(out_ref.shape[0]):
            rows = pl.ds(index * size, size)
            unit, inv_std = norm_stats(tokens_ref[rows, :].astype(F32))
            grad_unit = total[rows, :] * gain_ref[...]
            grad_input = inv_std * (
                grad_unit
                - jnp.mean(grad_unit, axis=1, keepdims=True)
                - unit * jnp.mean(grad_unit * unit, axis=1, keepdims=True)
            )
            out_ref[index, 0] = layer_ref[rows, :]
            out_ref[index, 1] = (cot_ref[rows, :].astype(F32) + grad_input).astype(BF16)


def out_proj(
    tokens, cot, gain, grad_value_part, layer_rows, grad_f, grad_b, forward_weight, backward_weight,
    n_seq, after,
):
    rows, channels = grad_f.shape
    width = tokens.shape[1]
    tile = INNER
    whole = lambda t: (0, 0)
    column = lambda t: (0, t)
    shape = (n_seq, 2, rows // n_seq, width)
    return pl.pallas_call(
        out_body,
        out_shape=jax.ShapeDtypeStruct(shape, BF16),
        grid=(channels // tile,),
        in_specs=[
            pl.BlockSpec((rows, width), whole),
            pl.BlockSpec((rows, width), whole),
            pl.BlockSpec((1, width), whole),
            pl.BlockSpec((rows, width), whole),
            pl.BlockSpec((rows, width), whole),
            pl.BlockSpec((rows, tile), column),
            pl.BlockSpec((rows, tile), column),
            pl.BlockSpec((width, tile), column),
            pl.BlockSpec((width, tile), column),
        ]
        + [ANY] * len(after),
        out_specs=pl.BlockSpec(shape, lambda t: (0, 0, 0, 0)),
        scratch_shapes=[pltpu.VMEM((rows, width), F32)],
        compiler_params=pltpu.CompilerParams(vmem_limit_bytes=VMEM),
        cost_estimate=cost(10),
        name="out_proj",
    )(
        tokens, cot, gain.reshape(1, -1), grad_value_part, layer_rows, grad_f, grad_b,
        forward_weight, backward_weight, *after,
    )


def swap(value, axis, mask):
    return lax.ppermute(value, axis, [(i, i ^ mask) for i in range(lax.axis_size(axis))])


def total_of(pieces):
    total = pieces[0].astype(F32)
    for piece in pieces[1:]:
        total = total + piece.astype(F32)
    return total


def with_bit(index, place, bit):
    low = index & ((1 << place) - 1)
    return ((index >> place) << (place + 1)) | (bit << place) | low


SLOT = {"dp": 3, "seq": 1}


def grid_place(step, grid):
    if grid[0] * grid[1] == 1:
        return [0, 0]
    step = jnp.minimum(step, grid[0] * grid[1] - 1)
    if grid[1] == 1:
        return [step, 0]
    return [step // grid[1], step % grid[1]] if grid[0] > 1 else [0, step]


class Scatter:

    def __init__(self, info, pieces, shape, order):
        self.info, self.shape, self.order = info, shape, list(order)
        self.pieces = list(pieces)
        self.stages = []

    def place(self, axis, bit):
        dim, place = (0, bit - 1) if axis == "dp" else (1, bit)
        lower = [b for a, b, _, _ in self.stages if a == axis and b < bit]
        return dim, place - len(lower)

    def index_map(self, level, column, last, grid):
        stages = self.stages[level:]

        def found(step, info):
            coords = grid_place(step, grid)
            if last is not None:
                axis, bit, dim, place = last
                coords[dim] = with_bit(coords[dim], place, 1 - ((info[SLOT[axis]] >> bit) & 1))
            for axis, bit, dim, place in reversed(stages):
                coords[dim] = with_bit(coords[dim], place, (info[SLOT[axis]] >> bit) & 1)
            return (coords[0], coords[1], 0, column)

        return found

    def sizes(self, stages):
        sizes = list(self.shape[:2])
        for _, _, dim, _ in stages:
            sizes[dim] //= 2
        return sizes

    def specs(self, last):
        stages = self.stages + ([last] if last else [])
        touched = {stage[2] for stage in stages}
        sizes = self.sizes(stages)
        lead = [1 if dim in touched else self.shape[dim] for dim in range(2)]
        grid = [sizes[dim] // lead[dim] for dim in range(2)]
        block = tuple(lead) + self.shape[2:]
        specs = [
            pl.BlockSpec(block, self.index_map(level, column, last, grid))
            for level, column, _ in self.pieces
        ]
        return block, grid, specs

    def next_stage(self):
        axis, bit = self.order[0]
        return (axis, bit) + self.place(axis, bit)


def add_body(info_ref, *refs, layout, first_out):
    refs = list(refs)
    out_refs = refs[first_out:]
    for count, out, column in layout:
        total = total_of([refs.pop(0)[...] for _ in range(count)]).astype(BF16)
        width = total.shape[3]
        out_refs[out][:, :, :, column * width : (column + 1) * width] = total


def step_apart(groups, after=(), passed=()):
    arrays, in_specs, out_specs, out_shape, layout, steps = [], [], [], [], [], 1
    for group in groups:
        merged = len({scatter.order[0] for scatter in group}) == 1
        for index, scatter in enumerate(group):
            stage = scatter.next_stage()
            block, grid, specs = scatter.specs(stage)
            sizes = scatter.sizes(scatter.stages + [stage])
            arrays += [piece for _, _, piece in scatter.pieces]
            in_specs += specs
            steps = max(steps, grid[0] * grid[1])
            width = scatter.shape[3]

            def out_map(step, info, grid=grid):
                return (*grid_place(step, grid), 0, 0)

            layout.append((len(specs), len(out_shape) - (1 if merged and index else 0), index if merged else 0))
            if merged and index:
                continue
            wide = width * len(group) if merged else width
            out_shape.append(jax.ShapeDtypeStruct(tuple(sizes) + (scatter.shape[2], wide), BF16))
            out_specs.append(pl.BlockSpec(block[:3] + (wide,), out_map))
    sums = len(out_shape)
    first_passed = 1 + len(arrays) + len(after)
    out_shape += [jax.ShapeDtypeStruct(value.shape, value.dtype) for value in passed]
    sent = pl.pallas_call(
        functools.partial(add_body, layout=tuple(layout), first_out=len(arrays) + len(after) + len(passed)),
        out_shape=out_shape,
        grid_spec=pltpu.PrefetchScalarGridSpec(
            num_scalar_prefetch=1,
            grid=(steps,),
            in_specs=in_specs + [ANY] * (len(after) + len(passed)),
            out_specs=out_specs + [ANY] * len(passed),
        ),
        input_output_aliases={first_passed + i: sums + i for i in range(len(passed))},
        compiler_params=pltpu.CompilerParams(vmem_limit_bytes=FULL_VMEM),
        cost_estimate=cost(3),
        name="add_sent",
    )(groups[0][0].info, *arrays, *after, *passed)
    arrived = {}
    for scatter, (_, out, column) in zip([s for group in groups for s in group], layout):
        axis, bit = scatter.order[0]
        if out not in arrived:
            arrived[out] = swap(sent[out], axis, 1 << bit)
        scatter.stages.append(scatter.next_stage())
        scatter.order.pop(0)
        scatter.pieces.append((len(scatter.stages), column, arrived[out]))
    return [sent[0], *sent[sums:]] if passed else sent[0]


def step_together(scatters, after=(), merged=False):
    return step_apart([scatters] if merged else [[scatter] for scatter in scatters], after)


def partner_body(info_ref, *refs, count, partners):
    outs = refs[-partners:]
    for index, out_ref in enumerate(outs):
        out_ref[...] = total_of([ref[0, 0] for ref in refs[index * count : (index + 1) * count]]).astype(BF16)


def sums_for_partners(scatter, partners, after):
    specs = []
    for mask in range(partners):
        for level, column, _ in scatter.pieces:
            whole = scatter.index_map(level, column, None, [1, 1])

            def found(step, info, whole=whole, mask=mask):
                place = whole(step, info)
                return (place[0], info[SLOT["seq"]] ^ mask, 0, 0)

            specs.append(pl.BlockSpec((1, 1) + scatter.shape[2:], found))
    count = len(scatter.pieces)
    shape = scatter.shape[2:]
    return pl.pallas_call(
        functools.partial(partner_body, count=count, partners=partners),
        out_shape=[jax.ShapeDtypeStruct(shape, BF16)] * partners,
        grid_spec=pltpu.PrefetchScalarGridSpec(
            num_scalar_prefetch=1,
            grid=(1,),
            in_specs=specs + [ANY] * len(after),
            out_specs=[pl.BlockSpec(shape, lambda t, info: (0, 0))] * partners,
        ),
        compiler_params=pltpu.CompilerParams(vmem_limit_bytes=VMEM),
        cost_estimate=cost(3),
        name="partner_sums",
    )(scatter.info, *[piece for _, _, piece in scatter.pieces] * partners, *after)


def sum_body(*refs, count):
    refs[-1][0] = total_of([ref[...] for ref in refs[:count]]).astype(BF16)


def sum_of(pieces, after):
    shape = pieces[0].shape
    return pl.pallas_call(
        functools.partial(sum_body, count=len(pieces)),
        out_shape=jax.ShapeDtypeStruct((1,) + shape, BF16),
        grid=(1,),
        in_specs=[pl.BlockSpec(shape, lambda t: (0, 0))] * len(pieces) + [ANY] * len(after),
        out_specs=pl.BlockSpec((1,) + shape, lambda t: (0, 0, 0)),
        cost_estimate=cost(3),
        name="sum_of",
    )(*pieces, *after)


def finish(scatters, out_shape, write, after, name):
    arrays, specs, counts = [], [], []
    for scatter in scatters:
        own = scatter.specs(None)[2]
        specs += own
        arrays += [piece for _, _, piece in scatter.pieces]
        counts.append(len(own))

    def body(info_ref, *refs):
        refs = list(refs)
        sums = [total_of([refs.pop(0)[0, 0] for _ in range(count)]) for count in counts]
        write(sums, *refs[len(after) :])

    return pl.pallas_call(
        body,
        out_shape=out_shape,
        grid_spec=pltpu.PrefetchScalarGridSpec(
            num_scalar_prefetch=1,
            grid=(1,),
            in_specs=specs + [ANY] * len(after),
            out_specs=[
                pl.BlockSpec(shape.shape, lambda t, info: (0, 0)) for shape in out_shape
            ],
        ),
        compiler_params=pltpu.CompilerParams(vmem_limit_bytes=VMEM),
        cost_estimate=cost(3),
        name=name,
    )(scatters[0].info, *arrays, *after)


def to_row(value):
    moved = lax.all_to_all(value, "seq", split_axis=0, concat_axis=0, tiled=True)
    return moved.reshape(-1, value.shape[2])


def on_device(
    tokens,
    doc_ids,
    norm_gain,
    value_weight,
    forward_weight,
    backward_weight,
    update_weight,
    output_weight,
    kernel_params,
    cotangent,
):
    n_dp, n_seq = lax.axis_size("dp"), lax.axis_size("seq")
    dp_index, seq_index = lax.axis_index("dp"), lax.axis_index("seq")
    channels = forward_weight.shape[1]
    own_channels = kernel_params.shape[3]
    core = dp_index % 2
    docs = lax.dynamic_index_in_dim(doc_ids, seq_index, 0, keepdims=False)
    longer = (docs[0] == docs[-1]).astype(jnp.int32)
    info = jnp.stack([core, seq_index, longer, dp_index]).astype(jnp.int32)
    tables = fourier_tables()

    row_tokens = to_row(tokens)
    half = pass_after(kernel_gen(info, kernel_params), [row_tokens])
    halves = [half if mask == 0 else swap(half, "seq", mask) for mask in range(n_seq)]
    normed, act_f, slope_f, act_b, slope_b, value_act, value_slope = in_proj(
        row_tokens, norm_gain, forward_weight, backward_weight, value_weight
    )
    mine = stack_pieces(halves, [value_act])
    other = swap(mine, "dp", 1)
    cot = to_row(cotangent)
    product, along, against = conv_fwd(info, tables, act_f, act_b, mine, other, [])

    seq_bits = [("seq", bit) for bit in range(n_seq.bit_length() - 1)]
    dp_bits = [("dp", bit) for bit in range(1, n_dp.bit_length() - 1)]
    shape = (n_dp // 2, n_seq, tokens.shape[2] // (n_dp * n_seq))

    def scatter_of(send, keep, order, columns=None):
        width = send.shape[2] // (columns or 1)
        whole = shape + (send.shape[2],)
        arrays = [keep.reshape(whole), swap(send, "dp", 1).reshape(whole)]
        return [
            Scatter(info, [(0, column, array) for array in arrays], shape + (width,), order[column])
            for column in range(columns or 1)
        ]

    send, keep, output_part, gated, grad_value_in, grad_product, normed_t = middle(
        info, product, normed, cot, update_weight, output_weight, value_act, value_slope, n_dp, n_seq
    )
    output_sum = lax.psum_scatter(output_part, "dp", scatter_dimension=0, tiled=True)
    layer_rows, grad_value_part = layer_rows_of(
        gated, grad_value_in, output_weight, value_weight, row_tokens, []
    )
    both = scatter_of(send, keep, [seq_bits + dp_bits, seq_bits[::-1] + dp_bits], 2)
    sent = step_apart([both[:1], both[1:]], [layer_rows])
    parts = n_dp // 2
    grad_f, grad_b, kernel_keep, kernel_send = conv_bwd(
        info, tables, grad_product, along, against, act_f, act_b, slope_f, slope_b, mine, other,
        parts, [sent],
    )
    send, keep = inner_weight_grad(normed_t, grad_f, grad_b, n_dp, n_seq, [])

    sent, send, kernel_send = step_apart([both[:1], both[1:]], [], [send, kernel_send])
    inner = scatter_of(send, keep, [seq_bits + dp_bits, seq_bits[::-1] + dp_bits], 2)
    blocks = kernel_keep.shape
    kernel = [
        Scatter(
            info,
            [(0, 0, kernel_keep), (0, 0, swap(kernel_send, "dp", 1))],
            blocks,
            dp_bits,
        )
    ]
    for _ in range(n_seq.bit_length() - 3):
        sent = step_apart([both[:1], both[1:]], [sent])
    sent = step_apart([inner[:1], inner[1:], kernel], [sent])
    out_pieces = out_proj(
        row_tokens, cot, norm_gain, grad_value_part, layer_rows, grad_f, grad_b,
        forward_weight, backward_weight, n_seq, [sent],
    )
    sent = step_apart([both, kernel], [sent, out_pieces])
    while kernel[0].order:
        sent = step_apart([kernel], [sent])
    output_blocks = (1, n_seq, output_sum.shape[0] // n_seq, output_sum.shape[1])
    output = [Scatter(info, [(0, 0, output_sum.reshape(output_blocks))], output_blocks, seq_bits[::-1])]
    for _ in range(n_seq.bit_length() - 2):
        sent = step_apart([inner[:1], inner[1:], output], [sent])
    halves = sums_for_partners(kernel[0], n_seq, [sent])
    halves = [half if mask == 0 else swap(half, "seq", mask) for mask, half in enumerate(halves)]
    sent = step_apart([inner, output], [halves[0]])
    while both[0].order:
        sent = step_apart([both], [sent])
    part = sum_of(halves, [sent])
    parts = [part if mask == 0 else swap(part, "dp", mask << 1) for mask in range(n_dp // 2)]
    while inner[0].order:
        sent = step_apart([inner], [part])
    gathered = stack_pieces(parts, [sent]).reshape((-1,) + part.shape[1:])
    others = swap(gathered, "dp", 1)
    moved = lax.all_to_all(out_pieces, "seq", split_axis=0, concat_axis=0, tiled=True)

    width = tokens.shape[2]
    small = width // (n_dp * n_seq)
    hidden = update_weight.shape[1]
    folds = channels // width
    tile = HIDDEN_TILE

    def write_first(sums, update_ref, value_ref, output_ref):
        column = 0
        output_ref[...] = sums[-1]
        for total in sums[:-1]:
            for start in range(0, total.shape[1], (folds + 1) * tile):
                columns = pl.ds(column, tile)
                for fold in range(folds):
                    part = total[:, start + fold * tile : start + (fold + 1) * tile]
                    update_ref[pl.ds(fold * small, small), columns] = part
                value_ref[:, columns] = total[:, start + folds * tile : start + (folds + 1) * tile]
                column += tile

    def write_inner(sums, forward_ref, backward_ref):
        for index, total in enumerate(sums):
            columns = pl.ds(index * INNER, INNER)
            forward_ref[:, columns] = total[:, :INNER]
            backward_ref[:, columns] = total[:, INNER : 2 * INNER]

    shape_of = lambda *shape: jax.ShapeDtypeStruct(shape, F32)
    params_grad = params_grad_of(info, kernel_params, gathered, others, n_dp, [])
    update_grad, value_grad, output_grad = finish(
        both + output,
        [shape_of(folds * small, hidden), shape_of(small, hidden), shape_of(*output_blocks[2:])],
        write_first,
        [params_grad],
        "first_sums",
    )
    forward_grad, backward_grad = finish(
        inner, [shape_of(small, channels)] * 2, write_inner, [update_grad], "inner_sums"
    )
    layer_out, tokens_grad = moved[:, 0], moved[:, 1]

    own_rows = lambda value: lax.dynamic_slice_in_dim(value, (dp_index * n_seq + seq_index) * small, small, 0)
    gain_sums = sum(
        jnp.sum(own_rows(weight).astype(F32) * grad, axis=1)
        for weight, grad in (
            (value_weight, value_grad), (forward_weight, forward_grad), (backward_weight, backward_grad)
        )
    )
    gain_grad = gain_sums / own_rows(norm_gain)
    return (
        layer_out,
        tokens_grad,
        gain_grad,
        value_grad,
        forward_grad,
        backward_grad,
        update_grad,
        output_grad,
        params_grad,
    )


def solution(mesh):
    placed = (
        P("dp", "seq", None),
        P("dp", None),
        P(),
        P(),
        P(),
        P(),
        P(),
        P(),
        P(None, None, None, "seq"),
        P("dp", "seq", None),
    )
    return jax.shard_map(
        on_device,
        mesh=mesh,
        in_specs=placed,
        out_specs=(
            P("dp", "seq", None),
            P("dp", "seq", None),
            P(("dp", "seq")),
            P(("dp", "seq"), None),
            P(("dp", "seq"), None),
            P(("dp", "seq"), None),
            P(("dp", "seq"), None),
            P(("dp", "seq"), None),
            P(None, None, "dp", "seq"),
        ),
        check_vma=False,
    )
```

```python
import functools
import math

import jax
import jax.numpy as jnp
import ml_dtypes
import numpy as np
from jax import lax
from jax.experimental import pallas as pl
from jax.experimental.pallas import tpu as pltpu
from jax.sharding import PartitionSpec as P

LENGTH = 512
BLOCK = 128
SECTIONS = LENGTH // BLOCK
FREQ = 128
HALF_FREQ = FREQ // 2
LOW = 16
INNER = 768
HIDDEN_TILE = 512
ANY = pl.BlockSpec(memory_space=pl.ANY)
VMEM = 56 * 1024 * 1024
FULL_VMEM = 63 * 1024 * 1024
BF16 = jnp.bfloat16
F32 = jnp.float32


def cost(microseconds):
    return pl.CostEstimate(flops=int(microseconds * 2e+07), bytes_accessed=0, transcendentals=0)


def dot(first_mat, second_mat):
    return jnp.dot(first_mat, second_mat, preferred_element_type=F32)


def dot_rt(first_mat, second_mat):
    return lax.dot_general(
        first_mat, second_mat, (((1,), (1,)), ((), ())), preferred_element_type=F32
    )


def dot_lt(first_mat, second_mat):
    return lax.dot_general(
        first_mat, second_mat, (((0,), (0,)), ((), ())), preferred_element_type=F32
    )


def fourier_tables():
    order = np.concatenate([np.arange(0, FREQ, 2), np.arange(1, FREQ, 2)])
    angle = 2.0 * np.pi * (order[:, None] + 0.5) * np.arange(BLOCK)[None, :] / (2 * BLOCK)
    table = np.concatenate([np.cos(angle), -np.sin(angle)], axis=0)
    high = table.astype(ml_dtypes.bfloat16)
    low = (table - high.astype(np.float64)).astype(ml_dtypes.bfloat16)
    forward = np.concatenate([high, low], axis=1)
    scale = ml_dtypes.bfloat16(1.0 / FREQ)
    inverse = np.stack([high.T * scale, low.T * scale]).astype(ml_dtypes.bfloat16)
    return jnp.asarray(forward), jnp.asarray(inverse)


def gelu_pair(v):
    cdf = 0.5 * lax.erf(v * (1.0 / math.sqrt(2.0))) + 0.5
    bell = jnp.exp(v * v * -0.5)
    return v * cdf, cdf + v * (1.0 / math.sqrt(2.0 * math.pi)) * bell


def cmul(first, second):
    return (
        first[0] * second[0] - first[1] * second[1],
        first[0] * second[1] + first[1] * second[0],
    )


def turn_of(angle):
    part = angle * 0.25
    square = part * part
    sin = part * (1.0 + square * (-1 / 6 + square * (1 / 120 + square * (-1 / 5040 + square / 362880))))
    cos = 1.0 + square * (
        -0.5 + square * (1 / 24 + square * (-1 / 720 + square * (1 / 40320 - square / 3628800)))
    )
    for _ in range(2):
        cos, sin = 1.0 - 2.0 * sin * sin, 2.0 * sin * cos
    return cos, sin


def powers_of(decay, frequency, count):
    mag = jnp.exp(-decay)
    cos, sin = turn_of(frequency)
    powers = [(mag * cos, mag * sin)]
    for _ in range(count - 1):
        powers.append(cmul(powers[-1], powers[-1]))
    return powers


def kernel_gen_body(info_ref, par_ref, out_ref, low_re, low_im, total_ref):
    channels = par_ref.shape[3]
    width = 128 if channels % 128 == 0 else channels
    for lane in range(0, channels, width):
        lanes = pl.ds(lane, width)
        powers = powers_of(par_ref[0, 0, :, lanes], par_ref[0, 1, :, lanes], 9)
        current = (jnp.ones_like(powers[0][0]), jnp.zeros_like(powers[0][0]))
        for j in range(LOW):
            low_re[j, :, lanes] = current[0]
            low_im[j, :, lanes] = current[1]
            current = cmul(current, powers[0])
        second_half = info_ref[0] == 1
        start = (
            jnp.where(second_half, powers[8][0], 1.0),
            jnp.where(second_half, powers[8][1], 0.0),
        )

        def some_lags(i, highs, lanes=lanes, place=lane // width, step=powers[5]):
            for j in range(LOW):
                re, im = low_re[j, :, lanes], low_im[j, :, lanes]
                for half, high in enumerate(highs):
                    terms = high[0] * re - high[1] * im
                    row = pl.ds((2 * i + half) * LOW + j, 1)
                    total_ref[place, row, :] = jnp.sum(terms, axis=0, keepdims=True)
            return tuple(cmul(high, step) for high in highs)

        first = cmul((par_ref[0, 2, :, lanes], par_ref[0, 3, :, lanes]), start)
        lax.fori_loop(
            0, out_ref.shape[1] // (2 * LOW), some_lags, (first, cmul(first, powers[4]))
        )
    for place in range(channels // width):
        out_ref[0, :, place * width : (place + 1) * width] = total_ref[place].astype(BF16)


def kernel_gen(info, params):
    dirs, kinds, modes, channels = params.shape
    width = 128 if channels % 128 == 0 else channels
    lags = LENGTH // 2
    return pl.pallas_call(
        kernel_gen_body,
        out_shape=jax.ShapeDtypeStruct((dirs, lags, channels), BF16),
        grid_spec=pltpu.PrefetchScalarGridSpec(
            num_scalar_prefetch=1,
            grid=(dirs,),
            in_specs=[pl.BlockSpec((1, kinds, modes, channels), lambda k, info: (k, 0, 0, 0))],
            out_specs=pl.BlockSpec((1, lags, channels), lambda k, info: (k, 0, 0)),
            scratch_shapes=[
                pltpu.VMEM((LOW, modes, channels), F32),
                pltpu.VMEM((LOW, modes, channels), F32),
                pltpu.VMEM((channels // width, lags, width), F32),
            ],
        ),
        compiler_params=pltpu.CompilerParams(vmem_limit_bytes=VMEM),
        cost_estimate=cost(9),
        name="kernel_gen",
    )(info, params)


def pass_body(*refs):
    pass


def pass_after(value, after):
    return pl.pallas_call(
        pass_body,
        out_shape=jax.ShapeDtypeStruct(value.shape, value.dtype),
        in_specs=[ANY] * (1 + len(after)),
        out_specs=ANY,
        input_output_aliases={0: 0},
        cost_estimate=cost(1),
        name="pass_after",
    )(value, *after)


def stack_body(*refs, count, inner):
    for index, ref in enumerate(refs[:count]):
        if inner:
            refs[-1][:, index] = ref[...]
        else:
            refs[-1][index] = ref[...]


def stack_pieces(pieces, after, inner=False):
    shape = pieces[0].shape
    out = (len(pieces),) + shape
    if inner:
        out = shape[:1] + (len(pieces),) + shape[1:]
    result = pl.pallas_call(
        functools.partial(stack_body, count=len(pieces), inner=inner),
        out_shape=jax.ShapeDtypeStruct(out, pieces[0].dtype),
        grid=(1,),
        in_specs=[pl.BlockSpec(shape, lambda t: (0,) * len(shape))] * len(pieces)
        + [ANY] * len(after),
        out_specs=pl.BlockSpec(out, lambda t: (0,) * len(out)),
        cost_estimate=cost(3),
        name="stack_pieces",
    )(*pieces, *after)
    return result.reshape((-1,) + shape[1:]) if inner else result


def params_grad_body(info_ref, par_ref, mine_ref, other_ref, *rest):
    out_ref, low_re, low_im, up_ref = rest[-4:]
    parts, rows = mine_ref.shape[:2]
    half = parts * rows // 2
    first_is_mine = info_ref[0] == 0
    for index in range(parts // 2):
        place = (pl.program_id(0) * (parts // 2) + index) ^ (info_ref[3] >> 1)
        mine, other = mine_ref[place].astype(F32), other_ref[place].astype(F32)
        up_ref[pl.ds(index * rows, rows), :] = jnp.where(first_is_mine, mine, other)
        up_ref[pl.ds(half + index * rows, rows), :] = jnp.where(first_is_mine, other, mine)
    powers = powers_of(par_ref[0, 0], par_ref[0, 1], 5)
    one = (jnp.ones_like(powers[0][0]), jnp.zeros_like(powers[0][0]))
    current = one
    for j in range(LOW):
        low_re[j] = current[0]
        low_im[j] = current[1]
        current = cmul(current, powers[0])
    zero = jnp.zeros_like(one[0])

    def some_lags(i, carry):
        high, plain, ramped = carry
        for part in range(4):
            first = pl.multiple_of((4 * i + part) * LOW, LOW)
            grads = up_ref[pl.ds(first, LOW), :]
            sums, ramps = [zero] * 2, [zero] * 2
            for j in reversed(range(LOW)):
                sums[0] = sums[0] + grads[j : j + 1, :] * low_re[j]
                sums[1] = sums[1] + grads[j : j + 1, :] * low_im[j]
                if j:
                    ramps = [ramps[0] + sums[0], ramps[1] + sums[1]]
            start = first.astype(F32)
            lagged = (ramps[0] + start * sums[0], ramps[1] + start * sums[1])
            plain = tuple(a + b for a, b in zip(plain, cmul(high, sums)))
            ramped = tuple(a + b for a, b in zip(ramped, cmul(high, lagged)))
            high = cmul(high, powers[4])
        return high, plain, ramped

    carry = (one, (zero, zero), (zero, zero))
    _, plain, ramped = lax.fori_loop(0, up_ref.shape[0] // (4 * LOW), some_lags, carry)
    real, imag = par_ref[0, 2], par_ref[0, 3]
    out_ref[0, 0] = imag * ramped[1] - real * ramped[0]
    out_ref[0, 1] = -(real * ramped[1] + imag * ramped[0])
    out_ref[0, 2] = plain[0]
    out_ref[0, 3] = -plain[1]


def params_grad_of(info, params, mine, other, n_dp, after):
    dirs, kinds, modes, channels = params.shape
    own = modes // n_dp
    place = lambda k, info: (k, 0, info[3], 0)
    if own % 8:
        params = lax.dynamic_slice_in_dim(params, lax.axis_index("dp") * own, own, 2)
        place = lambda k, info: (k, 0, 0, 0)
    return pl.pallas_call(
        params_grad_body,
        out_shape=jax.ShapeDtypeStruct((dirs, kinds, own, channels), F32),
        grid_spec=pltpu.PrefetchScalarGridSpec(
            num_scalar_prefetch=1,
            grid=(dirs,),
            in_specs=[
                pl.BlockSpec((1, kinds, own, channels), place),
                pl.BlockSpec(mine.shape, lambda k, info: (0, 0, 0)),
                pl.BlockSpec(mine.shape, lambda k, info: (0, 0, 0)),
            ]
            + [ANY] * len(after),
            out_specs=pl.BlockSpec((1, kinds, own, channels), lambda k, info: (k, 0, 0, 0)),
            scratch_shapes=[pltpu.VMEM((LOW, own, channels), F32)] * 2
            + [pltpu.VMEM((LENGTH, channels), F32)],
        ),
        compiler_params=pltpu.CompilerParams(vmem_limit_bytes=VMEM),
        cost_estimate=cost(5),
        name="params_grad",
    )(info, params, mine, other, *after)


def norm_stats(rows):
    centered = rows - jnp.mean(rows, axis=1, keepdims=True)
    inv_std = lax.rsqrt(jnp.mean(centered * centered, axis=1, keepdims=True) + 1e-05)
    return centered * inv_std, inv_std


def in_body(tokens_ref, gain_ref, *refs):
    *weight_refs, normed_ref = refs[:4]
    out_refs = refs[4:]

    @pl.when(pl.program_id(0) == 0)
    def _():
        for start in range(0, tokens_ref.shape[0], BLOCK):
            rows = pl.ds(start, BLOCK)
            unit, _ = norm_stats(tokens_ref[rows, :].astype(F32))
            normed_ref[rows, :] = (unit * gain_ref[...]).astype(BF16)

    size = 2 * BLOCK
    for index, w_ref in enumerate(weight_refs):
        a_ref, s_ref = out_refs[2 * index : 2 * index + 2]
        for start in range(0, normed_ref.shape[0], size):
            rows = pl.ds(start, size)
            act, slope = gelu_pair(dot(normed_ref[rows, :], w_ref[...]))
            a_ref[rows, :] = act.astype(a_ref.dtype)
            s_ref[rows, :] = slope.astype(s_ref.dtype)


def in_proj(tokens, gain, forward_weight, backward_weight, value_weight):
    width, channels = forward_weight.shape
    hidden = value_weight.shape[1]
    rows = tokens.shape[0]
    steps = 3
    whole = lambda t: (0, 0)
    column = lambda t: (0, t)
    widths = [weight.shape[1] // steps for weight in (forward_weight, backward_weight, value_weight)]
    out_widths = [channels] * 4 + [hidden] * 2
    return pl.pallas_call(
        in_body,
        out_shape=[
            jax.ShapeDtypeStruct((rows, out_width), BF16) for out_width in [width] + out_widths
        ],
        grid=(steps,),
        in_specs=[pl.BlockSpec((rows, width), whole), pl.BlockSpec((1, width), whole)]
        + [pl.BlockSpec((width, tile), column) for tile in widths],
        out_specs=[pl.BlockSpec((rows, width), whole)]
        + [pl.BlockSpec((rows, out_width // steps), column) for out_width in out_widths],
        compiler_params=pltpu.CompilerParams(vmem_limit_bytes=VMEM),
        cost_estimate=cost(14),
        name="in_proj",
    )(tokens, gain.reshape(1, -1), forward_weight, backward_weight, value_weight)


def load_block(ref, section):
    return ref[pl.ds(section * BLOCK, BLOCK), :]


def store_block(ref, section, value):
    ref[pl.ds(section * BLOCK, BLOCK), :] = value.astype(ref.dtype)


def spectra(table_ref, blocks, out_ref):
    wide = jnp.concatenate(blocks, axis=1)
    out_ref[...] = dot(table_ref[...], jnp.concatenate([wide, wide], axis=0))


def split_store(high_ref, low_ref, rows, columns, value):
    high_ref[rows, columns] = value.astype(BF16)


def inverse(inverse_ref, high_ref, low_ref):
    return dot(inverse_ref[0], high_ref[...])


CHUNK = 16


def chunks(width):
    for start in range(0, FREQ, CHUNK):
        for lane in range(0, width, 128):
            parity = start // HALF_FREQ
            columns = [pl.ds(i * width + lane, 128) for i in range(SECTIONS)]
            yield parity, pl.ds(start, CHUNK), pl.ds(FREQ + start, CHUNK), columns


def load_spectra(ref, re_rows, im_rows, columns):
    return [(ref[re_rows, column], ref[im_rows, column]) for column in columns]


def turned(value, parity):
    return (-value[1], value[0]) if parity == 0 else (value[1], -value[0])


def cadd(first, second):
    return (first[0] + second[0], first[1] + second[1])


def band_spectra(parts, parity, longer):
    bands = [parts[0]]
    for m in range(1, SECTIONS):
        re, im = cadd(parts[m], turned(parts[m - 1], parity))
        bands.append((re * longer, im * longer))
    return bands


def cfma(total, first, second, conj):
    if conj:
        re = first[0] * second[0] + first[1] * second[1]
        im = first[0] * second[1] - first[1] * second[0]
    else:
        re = first[0] * second[0] - first[1] * second[1]
        im = first[0] * second[1] + first[1] * second[0]
    return (re, im) if total is None else (total[0] + re, total[1] + im)


def conv_spectra(bands, values, ahead):
    outs = []
    for i in range(SECTIONS):
        total = None
        for m in range(SECTIONS):
            source = i + m if ahead else i - m
            if 0 <= source < SECTIONS:
                total = cfma(total, bands[m], values[source], ahead)
        outs.append(total)
    return outs


def tile_pieces(info_ref, count):
    return [j ^ (info_ref[1] & (count - 1)) for j in range(count)]


def kernel_blocks(info_ref, mine_ref, other_ref, direction):
    first_is_mine = info_ref[0] == 0
    places = tile_pieces(info_ref, mine_ref.shape[0])
    mine = [mine_ref[place, direction] for place in places]
    other = [other_ref[place, direction] for place in places]
    mine = mine[0] if len(mine) == 1 else jnp.concatenate(mine, axis=1)
    other = other[0] if len(other) == 1 else jnp.concatenate(other, axis=1)
    halves = [jnp.where(first_is_mine, mine, other), jnp.where(first_is_mine, other, mine)]
    per = halves[0].shape[0] // BLOCK
    return [half[i * BLOCK : (i + 1) * BLOCK] for half in halves for i in range(per)]


def conv_fwd_body(
    info_ref, table_ref, inverse_ref, xf_ref, xb_ref, mine_ref, other_ref, *rest
):
    prod_ref, al_ref, ag_ref = rest[-11:-8]
    scratch = rest[-8:]
    longer = info_ref[2].astype(F32)
    width = xf_ref.shape[1]
    for direction, (x_ref, out_ref) in enumerate(((xf_ref, al_ref), (xb_ref, ag_ref))):
        x_spec, k_spec, y_high, y_low = scratch[4 * direction : 4 * direction + 4]
        blocks = [load_block(x_ref, i) for i in range(SECTIONS)]
        spectra(table_ref, blocks, x_spec)
        spectra(table_ref, kernel_blocks(info_ref, mine_ref, other_ref, direction), k_spec)
        for parity, re_rows, im_rows, columns in chunks(width):
            bands = band_spectra(load_spectra(k_spec, re_rows, im_rows, columns), parity, longer)
            values = load_spectra(x_spec, re_rows, im_rows, columns)
            for column, (re, im) in zip(columns, conv_spectra(bands, values, direction == 1)):
                split_store(y_high, y_low, re_rows, column, re)
                split_store(y_high, y_low, im_rows, column, im)
        result = inverse(inverse_ref, y_high, y_low)
        for i in range(SECTIONS):
            store_block(out_ref, i, result[:, i * width : (i + 1) * width])
    prod_ref[...] = (al_ref[...] * ag_ref[...]).astype(BF16)


def kernel_spec(own, count):
    shift = count.bit_length() - 1
    return pl.BlockSpec(
        (count, 2, LENGTH // 2, own), lambda c, info: (c ^ (info[1] >> shift), 0, 0, 0)
    )


def tile_of(own):
    count = 1
    while (count * own) % 128:
        count *= 2
    return count, count * own


def conv_fwd(info, tables, act_forward, act_backward, mine, other, after):
    rows, channels = act_forward.shape
    count, width = tile_of(mine.shape[3])
    whole = lambda c, info: (0, 0)
    whole3 = lambda c, info: (0, 0, 0)
    column = lambda c, info: (0, c)
    forward, back = tables
    wide = SECTIONS * width
    return pl.pallas_call(
        conv_fwd_body,
        out_shape=[
            jax.ShapeDtypeStruct((rows, channels), BF16),
            jax.ShapeDtypeStruct((rows, channels), F32),
            jax.ShapeDtypeStruct((rows, channels), F32),
        ],
        grid_spec=pltpu.PrefetchScalarGridSpec(
            num_scalar_prefetch=1,
            grid=(channels // width,),
            in_specs=[
                pl.BlockSpec(forward.shape, whole),
                pl.BlockSpec(back.shape, whole3),
                pl.BlockSpec((rows, width), column),
                pl.BlockSpec((rows, width), column),
                kernel_spec(mine.shape[3], count),
                kernel_spec(mine.shape[3], count),
            ]
            + [ANY] * len(after),
            out_specs=[pl.BlockSpec((rows, width), column)] * 3,
            scratch_shapes=[
                pltpu.VMEM((2 * FREQ, wide), F32),
                pltpu.VMEM((2 * FREQ, wide), F32),
                pltpu.VMEM((2 * FREQ, wide), BF16),
                pltpu.VMEM((2 * FREQ, wide), BF16),
            ]
            * 2,
        ),
        compiler_params=pltpu.CompilerParams(vmem_limit_bytes=VMEM),
        cost_estimate=cost(17),
        name="conv_fwd",
    )(info, forward, back, act_forward, act_backward, mine, other, *after)


def conv_bwd_body(
    info_ref, table_ref, inverse_ref, gp_ref, al_ref, ag_ref, xf_ref, xb_ref, sf_ref, sb_ref,
    mine_ref, other_ref, *rest,
):
    gf_ref, gb_ref, keep_ref, send_ref = rest[-18:-14]
    scratch = rest[-14:]
    longer = info_ref[2].astype(F32)
    width = xf_ref.shape[1]
    ways = ((xf_ref, ag_ref, sf_ref, gf_ref), (xb_ref, al_ref, sb_ref, gb_ref))
    for direction, (x_ref, other_way, slope_ref, out_ref) in enumerate(ways):
        x_spec, k_spec, g_spec, y_high, y_low, h_high, h_low = scratch[7 * direction : 7 * direction + 7]
        upstream = [
            (
                load_block(gp_ref, i).astype(F32)
                * load_block(other_way, i)
            ).astype(BF16)
            for i in range(SECTIONS)
        ]
        spectra(table_ref, upstream, g_spec)
        spectra(table_ref, kernel_blocks(info_ref, mine_ref, other_ref, direction), k_spec)
        spectra(table_ref, [load_block(x_ref, i) for i in range(SECTIONS)], x_spec)
        for parity, re_rows, im_rows, columns in chunks(width):
            grads = load_spectra(g_spec, re_rows, im_rows, columns)
            bands = band_spectra(load_spectra(k_spec, re_rows, im_rows, columns), parity, longer)
            for column, (re, im) in zip(columns, conv_spectra(bands, grads, direction == 0)):
                split_store(y_high, y_low, re_rows, column, re)
                split_store(y_high, y_low, im_rows, column, im)
            values = load_spectra(x_spec, re_rows, im_rows, columns)
            above = None
            for m in reversed(range(SECTIONS)):
                total = None
                for i in range(m, SECTIONS):
                    if direction == 0:
                        total = cfma(total, values[i - m], grads[i], True)
                    else:
                        total = cfma(total, grads[i - m], values[i], True)
                if m:
                    total = (total[0] * longer, total[1] * longer)
                folded = total
                if above is not None:
                    folded = cadd(total, turned(above, 1 - parity))
                split_store(h_high, h_low, re_rows, columns[m], folded[0])
                split_store(h_high, h_low, im_rows, columns[m], folded[1])
                above = total
        result = inverse(inverse_ref, y_high, y_low)
        for i in range(SECTIONS):
            grad_act = result[:, i * width : (i + 1) * width].astype(BF16).astype(F32)
            slope = load_block(slope_ref, i).astype(F32)
            store_block(out_ref, i, grad_act * slope)
        result = inverse(inverse_ref, h_high, h_low).astype(BF16)
        first_is_mine = info_ref[0] == 0
        own, per = keep_ref.shape[3], keep_ref.shape[2]
        half = SECTIONS // 2
        for piece in range(keep_ref.shape[1]):
            for i in range(half):
                low = result[:, i * width + piece * own : i * width + (piece + 1) * own]
                top = (half + i) * width
                high = result[:, top + piece * own : top + (piece + 1) * own]
                for start in range(0, BLOCK, per):
                    place = ((direction * half + i) * BLOCK + start) // per
                    first, second = low[start : start + per], high[start : start + per]
                    keep_ref[place, piece] = jnp.where(first_is_mine, first, second)
                    send_ref[place, piece] = jnp.where(first_is_mine, second, first)


def conv_bwd(
    info, tables, grad_product, along, against, act_f, act_b, slope_f, slope_b, mine, other, parts,
    after,
):
    rows, channels = act_f.shape
    own = mine.shape[3]
    count, width = tile_of(own)
    whole = lambda c, info: (0, 0)
    whole3 = lambda c, info: (0, 0, 0)
    column = lambda c, info: (0, c)
    forward, back = tables
    wide = SECTIONS * width
    return pl.pallas_call(
        conv_bwd_body,
        out_shape=[
            jax.ShapeDtypeStruct((rows, channels), BF16),
            jax.ShapeDtypeStruct((rows, channels), BF16),
            jax.ShapeDtypeStruct((parts, mine.shape[0], LENGTH // parts, own), BF16),
            jax.ShapeDtypeStruct((parts, mine.shape[0], LENGTH // parts, own), BF16),
        ],
        grid_spec=pltpu.PrefetchScalarGridSpec(
            num_scalar_prefetch=1,
            grid=(channels // width,),
            in_specs=[
                pl.BlockSpec(forward.shape, whole),
                pl.BlockSpec(back.shape, whole3),
            ]
            + [pl.BlockSpec((rows, width), column)] * 7
            + [kernel_spec(own, count)] * 2
            + [ANY] * len(after),
            out_specs=[
                pl.BlockSpec((rows, width), column),
                pl.BlockSpec((rows, width), column),
                pl.BlockSpec((parts, count, LENGTH // parts, own), lambda c, info: (0, c, 0, 0)),
                pl.BlockSpec((parts, count, LENGTH // parts, own), lambda c, info: (0, c, 0, 0)),
            ],
            scratch_shapes=(
                [pltpu.VMEM((2 * FREQ, wide), F32)] * 3 + [pltpu.VMEM((2 * FREQ, wide), BF16)] * 4
            )
            * 2,
        ),
        compiler_params=pltpu.CompilerParams(vmem_limit_bytes=VMEM),
        cost_estimate=cost(28),
        name="conv_bwd",
    )(
        info, forward, back, grad_product, along, against, act_f, act_b, slope_f, slope_b,
        mine, other, *after,
    )


def packed_rows(total_ref, core, n_dp, n_seq, small, out_ref):
    size = total_ref.shape[0] // n_dp
    per = size // n_seq
    groups = n_dp // 2
    count = n_seq * small
    for group in range(groups):
        for place, which in enumerate((1 - core, core)):
            start = pl.multiple_of((2 * group + which) * size, 8)
            value = total_ref[pl.ds(start, size), :]
            for fold in range(per // small):
                first = fold * small
                rows = [value[s * per + first : s * per + first + small] for s in range(n_seq)]
                target = ((place * (per // small) + fold) * groups + group) * count
                out_ref[pl.ds(target, count), :] = jnp.concatenate(rows, axis=0).astype(out_ref.dtype)


def store_split(result, groups, folds, send_ref, keep_ref, offset):
    count = send_ref.shape[1]
    width = result.shape[1]
    for place, ref in enumerate((send_ref, keep_ref)):
        for fold in range(folds):
            for group in range(groups):
                first = ((place * folds + fold) * groups + group) * count
                columns = pl.ds(offset + fold * width, width)
                ref[group, :, columns] = result[first : first + count].astype(BF16)


def middle_body(
    info_ref, prod_ref, normed_ref, cot_ref, uw_ref, ow_ref, va_ref, vs_ref, *rest, n_dp, n_seq, small
):
    send_ref, keep_ref, og_ref, gated_ref, dv_ref, gp_ref, nt_ref = rest[:7]
    du_ref, pt_ref, flipped, gp_acc = rest[7:]
    step = pl.program_id(0)

    @pl.when(step == 0)
    def _():
        for source, target in ((prod_ref, pt_ref), (normed_ref, nt_ref)):
            rows = flipped.at[pl.ds(0, source.shape[1])]
            rows[...] = source[...].astype(F32).T
            packed_rows(rows, info_ref[0], n_dp, n_seq, small, target)
        gp_acc[...] = jnp.zeros_like(gp_acc)

    size = 2 * BLOCK
    for start in range(0, prod_ref.shape[0], size):
        rows = pl.ds(start, size)
        update_act, update_slope = gelu_pair(dot(prod_ref[rows, :], uw_ref[...]))
        grad_gated = dot_rt(cot_ref[rows, :], ow_ref[...])
        value_act = va_ref[rows, :].astype(F32)
        gated_ref[rows, :] = (update_act * value_act).astype(BF16)
        du_ref[rows, :] = (grad_gated * value_act * update_slope).astype(BF16)
        dv_ref[rows, :] = (grad_gated * update_act * vs_ref[rows, :].astype(F32)).astype(BF16)
    folds = prod_ref.shape[1] // normed_ref.shape[1]
    tile = uw_ref.shape[1]
    groups = n_dp // 2
    store_split(dot(pt_ref[...], du_ref[...]), groups, folds, send_ref, keep_ref, 0)
    store_split(dot(nt_ref[...], dv_ref[...]), groups, 1, send_ref, keep_ref, folds * tile)
    og_ref[...] = dot_lt(gated_ref[...], cot_ref[...]).astype(BF16)
    gp_acc[...] += dot_rt(du_ref[...], uw_ref[...])

    @pl.when(step == pl.num_programs(0) - 1)
    def _():
        gp_ref[...] = gp_acc[...].astype(BF16)


def middle(
    info, product, normed, cot, update_weight, output_weight, value_act, value_slope, n_dp, n_seq
):
    rows, channels = product.shape
    hidden, width = output_weight.shape
    tile = HIDDEN_TILE
    steps = hidden // tile
    small = width // (n_dp * n_seq)
    groups = n_dp // 2
    block = (channels // width + 1) * tile
    whole = lambda t, info: (0, 0)
    column = lambda t, info: (0, t)
    out_block = pl.BlockSpec((groups, n_seq * small, block), lambda t, info: (0, 0, t))
    return pl.pallas_call(
        functools.partial(middle_body, n_dp=n_dp, n_seq=n_seq, small=small),
        out_shape=[jax.ShapeDtypeStruct((groups, n_seq * small, steps * block), BF16)] * 2
        + [
            jax.ShapeDtypeStruct((hidden, width), BF16),
            jax.ShapeDtypeStruct((rows, hidden), BF16),
            jax.ShapeDtypeStruct((rows, hidden), BF16),
            jax.ShapeDtypeStruct((rows, channels), BF16),
            jax.ShapeDtypeStruct((width, rows), BF16),
        ],
        grid_spec=pltpu.PrefetchScalarGridSpec(
            num_scalar_prefetch=1,
            grid=(steps,),
            in_specs=[
                pl.BlockSpec((rows, channels), whole),
                pl.BlockSpec((rows, width), whole),
                pl.BlockSpec((rows, width), whole),
                pl.BlockSpec((channels, tile), column),
                pl.BlockSpec((tile, width), lambda t, info: (t, 0)),
                pl.BlockSpec((rows, tile), column),
                pl.BlockSpec((rows, tile), column),
            ],
            out_specs=[
                out_block,
                out_block,
                pl.BlockSpec((tile, width), lambda t, info: (t, 0)),
                pl.BlockSpec((rows, tile), column),
                pl.BlockSpec((rows, tile), column),
                pl.BlockSpec((rows, channels), whole),
                pl.BlockSpec((width, rows), whole),
            ],
            scratch_shapes=[
                pltpu.VMEM((rows, tile), BF16),
                pltpu.VMEM((channels, rows), BF16),
                pltpu.VMEM((channels, rows), F32),
                pltpu.VMEM((rows, channels), F32),
            ],
        ),
        compiler_params=pltpu.CompilerParams(vmem_limit_bytes=VMEM),
        cost_estimate=cost(40),
        name="middle",
    )(info, product, normed, cot, update_weight, output_weight, value_act, value_slope)


def layer_body(gated_ref, dv_ref, ow_ref, vw_ref, tokens_ref, *rest):
    layer_ref, gv_ref, lo_acc = rest[-3:]
    step = pl.program_id(0)

    @pl.when(step == 0)
    def _():
        lo_acc[...] = jnp.zeros_like(lo_acc)
        gv_ref[...] = jnp.zeros_like(gv_ref)

    lo_acc[...] += dot(gated_ref[...], ow_ref[...])
    gv_ref[...] += dot_rt(dv_ref[...], vw_ref[...])

    @pl.when(step == pl.num_programs(0) - 1)
    def _():
        layer_ref[...] = (tokens_ref[...].astype(F32) + lo_acc[...]).astype(BF16)


def layer_rows_of(gated, grad_value_in, output_weight, value_weight, tokens, after):
    rows, hidden = gated.shape
    width = output_weight.shape[1]
    tile = 1024
    whole = lambda t: (0, 0)
    column = lambda t: (0, t)
    return pl.pallas_call(
        layer_body,
        out_shape=[
            jax.ShapeDtypeStruct((rows, width), BF16),
            jax.ShapeDtypeStruct((rows, width), F32),
        ],
        grid=(hidden // tile,),
        in_specs=[
            pl.BlockSpec((rows, tile), column),
            pl.BlockSpec((rows, tile), column),
            pl.BlockSpec((tile, width), lambda t: (t, 0)),
            pl.BlockSpec((width, tile), column),
            pl.BlockSpec((rows, width), whole),
        ]
        + [ANY] * len(after),
        out_specs=[pl.BlockSpec((rows, width), whole)] * 2,
        scratch_shapes=[pltpu.VMEM((rows, width), F32)],
        compiler_params=pltpu.CompilerParams(vmem_limit_bytes=VMEM),
        cost_estimate=cost(9),
        name="layer_rows",
    )(gated, grad_value_in, output_weight, value_weight, tokens, *after)


def inner_grad_body(nt_ref, df_ref, db_ref, *rest, groups):
    send_ref, keep_ref = rest[-2:]
    tile = df_ref.shape[1]
    store_split(dot(nt_ref[...], df_ref[...]), groups, 1, send_ref, keep_ref, 0)
    store_split(dot(nt_ref[...], db_ref[...]), groups, 1, send_ref, keep_ref, tile)


def inner_weight_grad(normed_t, grad_f, grad_b, n_dp, n_seq, after):
    width, rows = normed_t.shape
    channels = grad_f.shape[1]
    small = width // (n_dp * n_seq)
    groups = n_dp // 2
    column = lambda t: (0, t)
    out_block = pl.BlockSpec((groups, n_seq * small, 2 * INNER), lambda t: (0, 0, t))
    return pl.pallas_call(
        functools.partial(inner_grad_body, groups=groups),
        out_shape=[jax.ShapeDtypeStruct((groups, n_seq * small, 2 * channels), BF16)] * 2,
        grid=(channels // INNER,),
        in_specs=[
            pl.BlockSpec((width, rows), lambda t: (0, 0)),
            pl.BlockSpec((rows, INNER), column),
            pl.BlockSpec((rows, INNER), column),
        ]
        + [ANY] * len(after),
        out_specs=[out_block, out_block],
        compiler_params=pltpu.CompilerParams(vmem_limit_bytes=VMEM),
        cost_estimate=cost(6),
        name="inner_weight_grad",
    )(normed_t, grad_f, grad_b, *after)


def out_body(
    tokens_ref, cot_ref, gain_ref, gv_ref, layer_ref, df_ref, db_ref, fw_ref, bw_ref, *rest
):
    out_ref, total = rest[-2:]
    step = pl.program_id(0)

    @pl.when(step == 0)
    def _():
        total[...] = gv_ref[...]

    total[...] += dot_rt(df_ref[...], fw_ref[...]) + dot_rt(db_ref[...], bw_ref[...])

    @pl.when(step == pl.num_programs(0) - 1)
    def _():
        size = out_ref.shape[2]
        for index in range(out_ref.shape[0]):
            rows = pl.ds(index * size, size)
            unit, inv_std = norm_stats(tokens_ref[rows, :].astype(F32))
            grad_unit = total[rows, :] * gain_ref[...]
            grad_input = inv_std * (
                grad_unit
                - jnp.mean(grad_unit, axis=1, keepdims=True)
                - unit * jnp.mean(grad_unit * unit, axis=1, keepdims=True)
            )
            out_ref[index, 0] = layer_ref[rows, :]
            out_ref[index, 1] = (cot_ref[rows, :].astype(F32) + grad_input).astype(BF16)


def out_proj(
    tokens, cot, gain, grad_value_part, layer_rows, grad_f, grad_b, forward_weight, backward_weight,
    n_seq, after,
):
    rows, channels = grad_f.shape
    width = tokens.shape[1]
    tile = INNER
    whole = lambda t: (0, 0)
    column = lambda t: (0, t)
    shape = (n_seq, 2, rows // n_seq, width)
    return pl.pallas_call(
        out_body,
        out_shape=jax.ShapeDtypeStruct(shape, BF16),
        grid=(channels // tile,),
        in_specs=[
            pl.BlockSpec((rows, width), whole),
            pl.BlockSpec((rows, width), whole),
            pl.BlockSpec((1, width), whole),
            pl.BlockSpec((rows, width), whole),
            pl.BlockSpec((rows, width), whole),
            pl.BlockSpec((rows, tile), column),
            pl.BlockSpec((rows, tile), column),
            pl.BlockSpec((width, tile), column),
            pl.BlockSpec((width, tile), column),
        ]
        + [ANY] * len(after),
        out_specs=pl.BlockSpec(shape, lambda t: (0, 0, 0, 0)),
        scratch_shapes=[pltpu.VMEM((rows, width), F32)],
        compiler_params=pltpu.CompilerParams(vmem_limit_bytes=VMEM),
        cost_estimate=cost(10),
        name="out_proj",
    )(
        tokens, cot, gain.reshape(1, -1), grad_value_part, layer_rows, grad_f, grad_b,
        forward_weight, backward_weight, *after,
    )


def swap(value, axis, mask):
    return lax.ppermute(value, axis, [(i, i ^ mask) for i in range(lax.axis_size(axis))])


def total_of(pieces):
    total = pieces[0].astype(F32)
    for piece in pieces[1:]:
        total = total + piece.astype(F32)
    return total


def with_bit(index, place, bit):
    low = index & ((1 << place) - 1)
    return ((index >> place) << (place + 1)) | (bit << place) | low


SLOT = {"dp": 3, "seq": 1}


def grid_place(step, grid):
    if grid[0] * grid[1] == 1:
        return [0, 0]
    step = jnp.minimum(step, grid[0] * grid[1] - 1)
    if grid[1] == 1:
        return [step, 0]
    return [step // grid[1], step % grid[1]] if grid[0] > 1 else [0, step]


class Scatter:

    def __init__(self, info, pieces, shape, order):
        self.info, self.shape, self.order = info, shape, list(order)
        self.pieces = list(pieces)
        self.stages = []

    def place(self, axis, bit):
        dim, place = (0, bit - 1) if axis == "dp" else (1, bit)
        lower = [b for a, b, _, _ in self.stages if a == axis and b < bit]
        return dim, place - len(lower)

    def index_map(self, level, column, last, grid):
        stages = self.stages[level:]

        def found(step, info):
            coords = grid_place(step, grid)
            if last is not None:
                axis, bit, dim, place = last
                coords[dim] = with_bit(coords[dim], place, 1 - ((info[SLOT[axis]] >> bit) & 1))
            for axis, bit, dim, place in reversed(stages):
                coords[dim] = with_bit(coords[dim], place, (info[SLOT[axis]] >> bit) & 1)
            return (coords[0], coords[1], 0, column)

        return found

    def sizes(self, stages):
        sizes = list(self.shape[:2])
        for _, _, dim, _ in stages:
            sizes[dim] //= 2
        return sizes

    def specs(self, last):
        stages = self.stages + ([last] if last else [])
        touched = {stage[2] for stage in stages}
        sizes = self.sizes(stages)
        lead = [1 if dim in touched else self.shape[dim] for dim in range(2)]
        grid = [sizes[dim] // lead[dim] for dim in range(2)]
        block = tuple(lead) + self.shape[2:]
        specs = [
            pl.BlockSpec(block, self.index_map(level, column, last, grid))
            for level, column, _ in self.pieces
        ]
        return block, grid, specs

    def next_stage(self):
        axis, bit = self.order[0]
        return (axis, bit) + self.place(axis, bit)


def add_body(info_ref, *refs, layout, first_out):
    refs = list(refs)
    out_refs = refs[first_out:]
    for count, out, column in layout:
        total = total_of([refs.pop(0)[...] for _ in range(count)]).astype(BF16)
        width = total.shape[3]
        out_refs[out][:, :, :, column * width : (column + 1) * width] = total


def step_apart(groups, after=(), passed=()):
    arrays, in_specs, out_specs, out_shape, layout, steps = [], [], [], [], [], 1
    for group in groups:
        merged = len({scatter.order[0] for scatter in group}) == 1
        for index, scatter in enumerate(group):
            stage = scatter.next_stage()
            block, grid, specs = scatter.specs(stage)
            sizes = scatter.sizes(scatter.stages + [stage])
            arrays += [piece for _, _, piece in scatter.pieces]
            in_specs += specs
            steps = max(steps, grid[0] * grid[1])
            width = scatter.shape[3]

            def out_map(step, info, grid=grid):
                return (*grid_place(step, grid), 0, 0)

            layout.append((len(specs), len(out_shape) - (1 if merged and index else 0), index if merged else 0))
            if merged and index:
                continue
            wide = width * len(group) if merged else width
            out_shape.append(jax.ShapeDtypeStruct(tuple(sizes) + (scatter.shape[2], wide), BF16))
            out_specs.append(pl.BlockSpec(block[:3] + (wide,), out_map))
    sums = len(out_shape)
    first_passed = 1 + len(arrays) + len(after)
    out_shape += [jax.ShapeDtypeStruct(value.shape, value.dtype) for value in passed]
    sent = pl.pallas_call(
        functools.partial(add_body, layout=tuple(layout), first_out=len(arrays) + len(after) + len(passed)),
        out_shape=out_shape,
        grid_spec=pltpu.PrefetchScalarGridSpec(
            num_scalar_prefetch=1,
            grid=(steps,),
            in_specs=in_specs + [ANY] * (len(after) + len(passed)),
            out_specs=out_specs + [ANY] * len(passed),
        ),
        input_output_aliases={first_passed + i: sums + i for i in range(len(passed))},
        compiler_params=pltpu.CompilerParams(vmem_limit_bytes=FULL_VMEM),
        cost_estimate=cost(3),
        name="add_sent",
    )(groups[0][0].info, *arrays, *after, *passed)
    arrived = {}
    for scatter, (_, out, column) in zip([s for group in groups for s in group], layout):
        axis, bit = scatter.order[0]
        if out not in arrived:
            arrived[out] = swap(sent[out], axis, 1 << bit)
        scatter.stages.append(scatter.next_stage())
        scatter.order.pop(0)
        scatter.pieces.append((len(scatter.stages), column, arrived[out]))
    return [sent[0], *sent[sums:]] if passed else sent[0]


def partner_body(info_ref, *refs, count, partners):
    outs = refs[-partners:]
    for index, out_ref in enumerate(outs):
        out_ref[...] = total_of([ref[0, 0] for ref in refs[index * count : (index + 1) * count]]).astype(BF16)


def sums_for_partners(scatter, partners, after):
    specs = []
    for mask in range(partners):
        for level, column, _ in scatter.pieces:
            whole = scatter.index_map(level, column, None, [1, 1])

            def found(step, info, whole=whole, mask=mask):
                place = whole(step, info)
                return (place[0], info[SLOT["seq"]] ^ mask, 0, 0)

            specs.append(pl.BlockSpec((1, 1) + scatter.shape[2:], found))
    count = len(scatter.pieces)
    shape = scatter.shape[2:]
    return pl.pallas_call(
        functools.partial(partner_body, count=count, partners=partners),
        out_shape=[jax.ShapeDtypeStruct(shape, BF16)] * partners,
        grid_spec=pltpu.PrefetchScalarGridSpec(
            num_scalar_prefetch=1,
            grid=(1,),
            in_specs=specs + [ANY] * len(after),
            out_specs=[pl.BlockSpec(shape, lambda t, info: (0, 0))] * partners,
        ),
        compiler_params=pltpu.CompilerParams(vmem_limit_bytes=VMEM),
        cost_estimate=cost(3),
        name="partner_sums",
    )(scatter.info, *[piece for _, _, piece in scatter.pieces] * partners, *after)


def sum_body(*refs, count):
    refs[-1][0] = total_of([ref[...] for ref in refs[:count]]).astype(BF16)


def sum_of(pieces, after):
    shape = pieces[0].shape
    return pl.pallas_call(
        functools.partial(sum_body, count=len(pieces)),
        out_shape=jax.ShapeDtypeStruct((1,) + shape, BF16),
        grid=(1,),
        in_specs=[pl.BlockSpec(shape, lambda t: (0, 0))] * len(pieces) + [ANY] * len(after),
        out_specs=pl.BlockSpec((1,) + shape, lambda t: (0, 0, 0)),
        cost_estimate=cost(3),
        name="sum_of",
    )(*pieces, *after)


def finish(scatters, out_shape, write, after, name):
    arrays, specs, counts = [], [], []
    for scatter in scatters:
        own = scatter.specs(None)[2]
        specs += own
        arrays += [piece for _, _, piece in scatter.pieces]
        counts.append(len(own))

    def body(info_ref, *refs):
        refs = list(refs)
        sums = [total_of([refs.pop(0)[0, 0] for _ in range(count)]) for count in counts]
        write(sums, *refs[len(after) :])

    return pl.pallas_call(
        body,
        out_shape=out_shape,
        grid_spec=pltpu.PrefetchScalarGridSpec(
            num_scalar_prefetch=1,
            grid=(1,),
            in_specs=specs + [ANY] * len(after),
            out_specs=[
                pl.BlockSpec(shape.shape, lambda t, info: (0, 0)) for shape in out_shape
            ],
        ),
        compiler_params=pltpu.CompilerParams(vmem_limit_bytes=VMEM),
        cost_estimate=cost(3),
        name=name,
    )(scatters[0].info, *arrays, *after)


def to_row(value):
    moved = lax.all_to_all(value, "seq", split_axis=0, concat_axis=0, tiled=True)
    return moved.reshape(-1, value.shape[2])


def on_device(
    tokens,
    doc_ids,
    norm_gain,
    value_weight,
    forward_weight,
    backward_weight,
    update_weight,
    output_weight,
    kernel_params,
    cotangent,
):
    n_dp, n_seq = lax.axis_size("dp"), lax.axis_size("seq")
    dp_index, seq_index = lax.axis_index("dp"), lax.axis_index("seq")
    channels = forward_weight.shape[1]
    own_channels = kernel_params.shape[3]
    core = dp_index % 2
    docs = lax.dynamic_index_in_dim(doc_ids, seq_index, 0, keepdims=False)
    longer = (docs[0] == docs[-1]).astype(jnp.int32)
    info = jnp.stack([core, seq_index, longer, dp_index]).astype(jnp.int32)
    tables = fourier_tables()

    row_tokens = to_row(tokens)
    half = pass_after(kernel_gen(info, kernel_params), [row_tokens])
    halves = [half if mask == 0 else swap(half, "seq", mask) for mask in range(n_seq)]
    normed, act_f, slope_f, act_b, slope_b, value_act, value_slope = in_proj(
        row_tokens, norm_gain, forward_weight, backward_weight, value_weight
    )
    mine = stack_pieces(halves, [value_act])
    other = swap(mine, "dp", 1)
    cot = to_row(cotangent)
    product, along, against = conv_fwd(info, tables, act_f, act_b, mine, other, [])

    seq_bits = [("seq", bit) for bit in range(n_seq.bit_length() - 1)]
    dp_bits = [("dp", bit) for bit in range(1, n_dp.bit_length() - 1)]
    shape = (n_dp // 2, n_seq, tokens.shape[2] // (n_dp * n_seq))

    def scatter_of(send, keep, order, columns=None):
        width = send.shape[2] // (columns or 1)
        whole = shape + (send.shape[2],)
        arrays = [keep.reshape(whole), swap(send, "dp", 1).reshape(whole)]
        return [
            Scatter(info, [(0, column, array) for array in arrays], shape + (width,), order[column])
            for column in range(columns or 1)
        ]

    send, keep, output_part, gated, grad_value_in, grad_product, normed_t = middle(
        info, product, normed, cot, update_weight, output_weight, value_act, value_slope, n_dp, n_seq
    )
    output_sum = lax.psum_scatter(output_part, "dp", scatter_dimension=0, tiled=True)
    layer_rows, grad_value_part = layer_rows_of(
        gated, grad_value_in, output_weight, value_weight, row_tokens, []
    )
    both = scatter_of(send, keep, [seq_bits + dp_bits, seq_bits[::-1] + dp_bits], 2)
    sent = step_apart([both[:1], both[1:]], [layer_rows])
    parts = n_dp // 2
    grad_f, grad_b, kernel_keep, kernel_send = conv_bwd(
        info, tables, grad_product, along, against, act_f, act_b, slope_f, slope_b, mine, other,
        parts, [sent],
    )
    send, keep = inner_weight_grad(normed_t, grad_f, grad_b, n_dp, n_seq, [])

    sent, send, kernel_send = step_apart([both[:1], both[1:]], [], [send, kernel_send])
    inner = scatter_of(send, keep, [seq_bits + dp_bits, seq_bits[::-1] + dp_bits], 2)
    blocks = kernel_keep.shape
    kernel = [
        Scatter(
            info,
            [(0, 0, kernel_keep), (0, 0, swap(kernel_send, "dp", 1))],
            blocks,
            dp_bits,
        )
    ]
    for _ in range(n_seq.bit_length() - 3):
        sent = step_apart([both[:1], both[1:]], [sent])
    sent = step_apart([inner[:1], inner[1:], kernel], [sent])
    out_pieces = out_proj(
        row_tokens, cot, norm_gain, grad_value_part, layer_rows, grad_f, grad_b,
        forward_weight, backward_weight, n_seq, [sent],
    )
    sent = step_apart([both, kernel], [sent, out_pieces])
    while kernel[0].order:
        sent = step_apart([kernel], [sent])
    output_blocks = (1, n_seq, output_sum.shape[0] // n_seq, output_sum.shape[1])
    output = [Scatter(info, [(0, 0, output_sum.reshape(output_blocks))], output_blocks, seq_bits[::-1])]
    for _ in range(n_seq.bit_length() - 2):
        sent = step_apart([inner[:1], inner[1:], output], [sent])
    halves = sums_for_partners(kernel[0], n_seq, [sent])
    halves = [half if mask == 0 else swap(half, "seq", mask) for mask, half in enumerate(halves)]
    sent = step_apart([inner, output], [halves[0]])
    while both[0].order:
        sent = step_apart([both], [sent])
    part = sum_of(halves, [sent])
    parts = [part if mask == 0 else swap(part, "dp", mask << 1) for mask in range(n_dp // 2)]
    while inner[0].order:
        sent = step_apart([inner], [part])
    width = tokens.shape[2]
    small = width // (n_dp * n_seq)
    hidden = update_weight.shape[1]
    folds = channels // width
    tile = HIDDEN_TILE

    def write_first(sums, update_ref, value_ref, output_ref):
        column = 0
        output_ref[...] = sums[-1]
        for total in sums[:-1]:
            for start in range(0, total.shape[1], (folds + 1) * tile):
                columns = pl.ds(column, tile)
                for fold in range(folds):
                    part = total[:, start + fold * tile : start + (fold + 1) * tile]
                    update_ref[pl.ds(fold * small, small), columns] = part
                value_ref[:, columns] = total[:, start + folds * tile : start + (folds + 1) * tile]
                column += tile

    def write_inner(sums, forward_ref, backward_ref):
        for index, total in enumerate(sums):
            columns = pl.ds(index * INNER, INNER)
            forward_ref[:, columns] = total[:, :INNER]
            backward_ref[:, columns] = total[:, INNER : 2 * INNER]

    shape_of = lambda *shape: jax.ShapeDtypeStruct(shape, F32)
    first_shapes = [shape_of(folds * small, hidden), shape_of(small, hidden), shape_of(*output_blocks[2:])]
    update_grad, value_grad, output_grad = finish(
        both + output, first_shapes, write_first, [sent], "first_sums"
    )
    gathered = stack_pieces(parts, [update_grad]).reshape((-1,) + part.shape[1:])
    others = swap(gathered, "dp", 1)
    moved = lax.all_to_all(out_pieces, "seq", split_axis=0, concat_axis=0, tiled=True)

    forward_grad, backward_grad = finish(
        inner, [shape_of(small, channels)] * 2, write_inner, [gathered], "inner_sums"
    )
    params_grad = params_grad_of(info, kernel_params, gathered, others, n_dp, [forward_grad])

    layer_out, tokens_grad = moved[:, 0], moved[:, 1]

    own_rows = lambda value: lax.dynamic_slice_in_dim(value, (dp_index * n_seq + seq_index) * small, small, 0)
    gain_sums = sum(
        jnp.sum(own_rows(weight).astype(F32) * grad, axis=1)
        for weight, grad in (
            (value_weight, value_grad), (forward_weight, forward_grad), (backward_weight, backward_grad)
        )
    )
    gain_grad = gain_sums / own_rows(norm_gain)
    return (
        layer_out,
        tokens_grad,
        gain_grad,
        value_grad,
        forward_grad,
        backward_grad,
        update_grad,
        output_grad,
        params_grad,
    )


def solution(mesh):
    placed = (
        P("dp", "seq", None),
        P("dp", None),
        P(),
        P(),
        P(),
        P(),
        P(),
        P(),
        P(None, None, None, "seq"),
        P("dp", "seq", None),
    )
    return jax.shard_map(
        on_device,
        mesh=mesh,
        in_specs=placed,
        out_specs=(
            P("dp", "seq", None),
            P("dp", "seq", None),
            P(("dp", "seq")),
            P(("dp", "seq"), None),
            P(("dp", "seq"), None),
            P(("dp", "seq"), None),
            P(("dp", "seq"), None),
            P(("dp", "seq"), None),
            P(None, None, "dp", "seq"),
        ),
        check_vma=False,
    )
```

```python
import functools
import math

import jax
import jax.numpy as jnp
import ml_dtypes
import numpy as np
from jax import lax
from jax.experimental import pallas as pl
from jax.experimental.pallas import tpu as pltpu
from jax.sharding import PartitionSpec as P

LENGTH = 512
BLOCK = 128
SECTIONS = LENGTH // BLOCK
FREQ = 128
HALF_FREQ = FREQ // 2
LOW = 16
INNER = 768
HIDDEN_TILE = 512
ANY = pl.BlockSpec(memory_space=pl.ANY)
VMEM = 63 * 1024 * 1024
FULL_VMEM = 63 * 1024 * 1024
BF16 = jnp.bfloat16
F32 = jnp.float32


def cost(microseconds):
    return pl.CostEstimate(flops=int(microseconds * 2e+07), bytes_accessed=0, transcendentals=0)


def dot(first_mat, second_mat):
    return jnp.dot(first_mat, second_mat, preferred_element_type=F32)


def dot_rt(first_mat, second_mat):
    return lax.dot_general(
        first_mat, second_mat, (((1,), (1,)), ((), ())), preferred_element_type=F32
    )


def dot_lt(first_mat, second_mat):
    return lax.dot_general(
        first_mat, second_mat, (((0,), (0,)), ((), ())), preferred_element_type=F32
    )


def fourier_tables():
    order = np.concatenate([np.arange(0, FREQ, 2), np.arange(1, FREQ, 2)])
    angle = 2.0 * np.pi * (order[:, None] + 0.5) * np.arange(BLOCK)[None, :] / (2 * BLOCK)
    table = np.concatenate([np.cos(angle), -np.sin(angle)], axis=0)
    high = table.astype(ml_dtypes.bfloat16)
    low = (table - high.astype(np.float64)).astype(ml_dtypes.bfloat16)
    forward = np.concatenate([high, low], axis=1)
    scale = ml_dtypes.bfloat16(1.0 / FREQ)
    inverse = np.stack([high.T * scale, low.T * scale]).astype(ml_dtypes.bfloat16)
    return jnp.asarray(forward), jnp.asarray(inverse)


def gelu_pair(v):
    cdf = 0.5 * lax.erf(v * (1.0 / math.sqrt(2.0))) + 0.5
    bell = jnp.exp(v * v * -0.5)
    return v * cdf, cdf + v * (1.0 / math.sqrt(2.0 * math.pi)) * bell


def cmul(first, second):
    return (
        first[0] * second[0] - first[1] * second[1],
        first[0] * second[1] + first[1] * second[0],
    )


def turn_of(angle):
    part = angle * 0.25
    square = part * part
    sin = part * (1.0 + square * (-1 / 6 + square * (1 / 120 + square * (-1 / 5040 + square / 362880))))
    cos = 1.0 + square * (
        -0.5 + square * (1 / 24 + square * (-1 / 720 + square * (1 / 40320 - square / 3628800)))
    )
    for _ in range(2):
        cos, sin = 1.0 - 2.0 * sin * sin, 2.0 * sin * cos
    return cos, sin


def powers_of(decay, frequency, count):
    mag = jnp.exp(-decay)
    cos, sin = turn_of(frequency)
    powers = [(mag * cos, mag * sin)]
    for _ in range(count - 1):
        powers.append(cmul(powers[-1], powers[-1]))
    return powers


def kernel_gen_body(info_ref, par_ref, out_ref, low_re, low_im, total_ref):
    channels = par_ref.shape[3]
    width = 128 if channels % 128 == 0 else channels
    for lane in range(0, channels, width):
        lanes = pl.ds(lane, width)
        powers = powers_of(par_ref[0, 0, :, lanes], par_ref[0, 1, :, lanes], 9)
        current = (jnp.ones_like(powers[0][0]), jnp.zeros_like(powers[0][0]))
        for j in range(LOW):
            low_re[j, :, lanes] = current[0]
            low_im[j, :, lanes] = current[1]
            current = cmul(current, powers[0])
        second_half = info_ref[0] == 1
        start = (
            jnp.where(second_half, powers[8][0], 1.0),
            jnp.where(second_half, powers[8][1], 0.0),
        )

        def some_lags(i, highs, lanes=lanes, place=lane // width, step=powers[5]):
            for j in range(LOW):
                re, im = low_re[j, :, lanes], low_im[j, :, lanes]
                for half, high in enumerate(highs):
                    terms = high[0] * re - high[1] * im
                    row = pl.ds((2 * i + half) * LOW + j, 1)
                    total_ref[place, row, :] = jnp.sum(terms, axis=0, keepdims=True)
            return tuple(cmul(high, step) for high in highs)

        first = cmul((par_ref[0, 2, :, lanes], par_ref[0, 3, :, lanes]), start)
        lax.fori_loop(
            0, out_ref.shape[1] // (2 * LOW), some_lags, (first, cmul(first, powers[4]))
        )
    for place in range(channels // width):
        out_ref[0, :, place * width : (place + 1) * width] = total_ref[place].astype(BF16)


def kernel_gen(info, params):
    dirs, kinds, modes, channels = params.shape
    width = 128 if channels % 128 == 0 else channels
    lags = LENGTH // 2
    return pl.pallas_call(
        kernel_gen_body,
        out_shape=jax.ShapeDtypeStruct((dirs, lags, channels), BF16),
        grid_spec=pltpu.PrefetchScalarGridSpec(
            num_scalar_prefetch=1,
            grid=(dirs,),
            in_specs=[pl.BlockSpec((1, kinds, modes, channels), lambda k, info: (k, 0, 0, 0))],
            out_specs=pl.BlockSpec((1, lags, channels), lambda k, info: (k, 0, 0)),
            scratch_shapes=[
                pltpu.VMEM((LOW, modes, channels), F32),
                pltpu.VMEM((LOW, modes, channels), F32),
                pltpu.VMEM((channels // width, lags, width), F32),
            ],
        ),
        compiler_params=pltpu.CompilerParams(vmem_limit_bytes=VMEM),
        cost_estimate=cost(9),
        name="kernel_gen",
    )(info, params)


def pass_body(*refs):
    pass


def pass_after(value, after):
    return pl.pallas_call(
        pass_body,
        out_shape=jax.ShapeDtypeStruct(value.shape, value.dtype),
        in_specs=[ANY] * (1 + len(after)),
        out_specs=ANY,
        input_output_aliases={0: 0},
        cost_estimate=cost(1),
        name="pass_after",
    )(value, *after)


def stack_body(*refs, count, inner):
    for index, ref in enumerate(refs[:count]):
        if inner:
            refs[-1][:, index] = ref[...]
        else:
            refs[-1][index] = ref[...]


def stack_pieces(pieces, after, inner=False):
    shape = pieces[0].shape
    out = (len(pieces),) + shape
    if inner:
        out = shape[:1] + (len(pieces),) + shape[1:]
    result = pl.pallas_call(
        functools.partial(stack_body, count=len(pieces), inner=inner),
        out_shape=jax.ShapeDtypeStruct(out, pieces[0].dtype),
        grid=(1,),
        in_specs=[pl.BlockSpec(shape, lambda t: (0,) * len(shape))] * len(pieces)
        + [ANY] * len(after),
        out_specs=pl.BlockSpec(out, lambda t: (0,) * len(out)),
        cost_estimate=cost(3),
        name="stack_pieces",
    )(*pieces, *after)
    return result.reshape((-1,) + shape[1:]) if inner else result


def params_grad_body(info_ref, par_ref, mine_ref, other_ref, *rest):
    out_ref, low_re, low_im, up_ref = rest[-4:]
    parts, rows = mine_ref.shape[:2]
    half = parts * rows // 2
    first_is_mine = info_ref[0] == 0
    for index in range(parts // 2):
        place = (pl.program_id(0) * (parts // 2) + index) ^ (info_ref[3] >> 1)
        mine, other = mine_ref[place].astype(F32), other_ref[place].astype(F32)
        up_ref[pl.ds(index * rows, rows), :] = jnp.where(first_is_mine, mine, other)
        up_ref[pl.ds(half + index * rows, rows), :] = jnp.where(first_is_mine, other, mine)
    powers = powers_of(par_ref[0, 0], par_ref[0, 1], 5)
    one = (jnp.ones_like(powers[0][0]), jnp.zeros_like(powers[0][0]))
    current = one
    for j in range(LOW):
        low_re[j] = current[0]
        low_im[j] = current[1]
        current = cmul(current, powers[0])
    zero = jnp.zeros_like(one[0])

    def some_lags(i, carry):
        high, plain, ramped = carry
        for part in range(4):
            first = pl.multiple_of((4 * i + part) * LOW, LOW)
            grads = up_ref[pl.ds(first, LOW), :]
            sums, ramps = [zero] * 2, [zero] * 2
            for j in reversed(range(LOW)):
                sums[0] = sums[0] + grads[j : j + 1, :] * low_re[j]
                sums[1] = sums[1] + grads[j : j + 1, :] * low_im[j]
                if j:
                    ramps = [ramps[0] + sums[0], ramps[1] + sums[1]]
            start = first.astype(F32)
            lagged = (ramps[0] + start * sums[0], ramps[1] + start * sums[1])
            plain = tuple(a + b for a, b in zip(plain, cmul(high, sums)))
            ramped = tuple(a + b for a, b in zip(ramped, cmul(high, lagged)))
            high = cmul(high, powers[4])
        return high, plain, ramped

    carry = (one, (zero, zero), (zero, zero))
    _, plain, ramped = lax.fori_loop(0, up_ref.shape[0] // (4 * LOW), some_lags, carry)
    real, imag = par_ref[0, 2], par_ref[0, 3]
    out_ref[0, 0] = imag * ramped[1] - real * ramped[0]
    out_ref[0, 1] = -(real * ramped[1] + imag * ramped[0])
    out_ref[0, 2] = plain[0]
    out_ref[0, 3] = -plain[1]


def params_grad_of(info, params, mine, other, n_dp, after):
    dirs, kinds, modes, channels = params.shape
    own = modes // n_dp
    place = lambda k, info: (k, 0, info[3], 0)
    if own % 8:
        params = lax.dynamic_slice_in_dim(params, lax.axis_index("dp") * own, own, 2)
        place = lambda k, info: (k, 0, 0, 0)
    return pl.pallas_call(
        params_grad_body,
        out_shape=jax.ShapeDtypeStruct((dirs, kinds, own, channels), F32),
        grid_spec=pltpu.PrefetchScalarGridSpec(
            num_scalar_prefetch=1,
            grid=(dirs,),
            in_specs=[
                pl.BlockSpec((1, kinds, own, channels), place),
                pl.BlockSpec(mine.shape, lambda k, info: (0, 0, 0)),
                pl.BlockSpec(mine.shape, lambda k, info: (0, 0, 0)),
            ]
            + [ANY] * len(after),
            out_specs=pl.BlockSpec((1, kinds, own, channels), lambda k, info: (k, 0, 0, 0)),
            scratch_shapes=[pltpu.VMEM((LOW, own, channels), F32)] * 2
            + [pltpu.VMEM((LENGTH, channels), F32)],
        ),
        compiler_params=pltpu.CompilerParams(vmem_limit_bytes=VMEM),
        cost_estimate=cost(5),
        name="params_grad",
    )(info, params, mine, other, *after)


def norm_stats(rows):
    centered = rows - jnp.mean(rows, axis=1, keepdims=True)
    inv_std = lax.rsqrt(jnp.mean(centered * centered, axis=1, keepdims=True) + 1e-05)
    return centered * inv_std, inv_std


def in_body(tokens_ref, gain_ref, *refs):
    *weight_refs, normed_ref = refs[:4]
    out_refs = refs[4:]

    @pl.when(pl.program_id(0) == 0)
    def _():
        for start in range(0, tokens_ref.shape[0], BLOCK):
            rows = pl.ds(start, BLOCK)
            unit, _ = norm_stats(tokens_ref[rows, :].astype(F32))
            normed_ref[rows, :] = (unit * gain_ref[...]).astype(BF16)

    size = 2 * BLOCK
    for index, w_ref in enumerate(weight_refs):
        a_ref, s_ref = out_refs[2 * index : 2 * index + 2]
        for start in range(0, normed_ref.shape[0], size):
            rows = pl.ds(start, size)
            act, slope = gelu_pair(dot(normed_ref[rows, :], w_ref[...]))
            a_ref[rows, :] = act.astype(a_ref.dtype)
            s_ref[rows, :] = slope.astype(s_ref.dtype)


def in_proj(tokens, gain, forward_weight, backward_weight, value_weight):
    width, channels = forward_weight.shape
    hidden = value_weight.shape[1]
    rows = tokens.shape[0]
    steps = 6
    whole = lambda t: (0, 0)
    column = lambda t: (0, t)
    widths = [weight.shape[1] // steps for weight in (forward_weight, backward_weight, value_weight)]
    out_widths = [channels] * 4 + [hidden] * 2
    return pl.pallas_call(
        in_body,
        out_shape=[
            jax.ShapeDtypeStruct((rows, out_width), BF16) for out_width in [width] + out_widths
        ],
        grid=(steps,),
        in_specs=[pl.BlockSpec((rows, width), whole), pl.BlockSpec((1, width), whole)]
        + [pl.BlockSpec((width, tile), column) for tile in widths],
        out_specs=[pl.BlockSpec((rows, width), whole)]
        + [pl.BlockSpec((rows, out_width // steps), column) for out_width in out_widths],
        compiler_params=pltpu.CompilerParams(vmem_limit_bytes=VMEM),
        cost_estimate=cost(14),
        name="in_proj",
    )(tokens, gain.reshape(1, -1), forward_weight, backward_weight, value_weight)


def load_block(ref, section):
    return ref[pl.ds(section * BLOCK, BLOCK), :]


def store_block(ref, section, value):
    ref[pl.ds(section * BLOCK, BLOCK), :] = value.astype(ref.dtype)


def spectra(table_ref, blocks, out_ref):
    wide = jnp.concatenate(blocks, axis=1)
    out_ref[...] = dot(table_ref[...], jnp.concatenate([wide, wide], axis=0))


def split_store(high_ref, low_ref, rows, columns, value):
    high_ref[rows, columns] = value.astype(BF16)


def inverse(inverse_ref, high_ref, low_ref):
    return dot(inverse_ref[0], high_ref[...])


CHUNK = 16


def chunks(width):
    for start in range(0, FREQ, CHUNK):
        for lane in range(0, width, 128):
            parity = start // HALF_FREQ
            columns = [pl.ds(i * width + lane, 128) for i in range(SECTIONS)]
            yield parity, pl.ds(start, CHUNK), pl.ds(FREQ + start, CHUNK), columns


def load_spectra(ref, re_rows, im_rows, columns):
    return [(ref[re_rows, column], ref[im_rows, column]) for column in columns]


def turned(value, parity):
    return (-value[1], value[0]) if parity == 0 else (value[1], -value[0])


def cadd(first, second):
    return (first[0] + second[0], first[1] + second[1])


def band_spectra(parts, parity, longer):
    bands = [parts[0]]
    for m in range(1, SECTIONS):
        re, im = cadd(parts[m], turned(parts[m - 1], parity))
        bands.append((re * longer, im * longer))
    return bands


def cfma(total, first, second, conj):
    if conj:
        re = first[0] * second[0] + first[1] * second[1]
        im = first[0] * second[1] - first[1] * second[0]
    else:
        re = first[0] * second[0] - first[1] * second[1]
        im = first[0] * second[1] + first[1] * second[0]
    return (re, im) if total is None else (total[0] + re, total[1] + im)


def conv_spectra(bands, values, ahead):
    outs = []
    for i in range(SECTIONS):
        total = None
        for m in range(SECTIONS):
            source = i + m if ahead else i - m
            if 0 <= source < SECTIONS:
                total = cfma(total, bands[m], values[source], ahead)
        outs.append(total)
    return outs


def tile_pieces(info_ref, count):
    return [j ^ (info_ref[1] & (count - 1)) for j in range(count)]


def kernel_blocks(info_ref, mine_ref, other_ref, direction):
    first_is_mine = info_ref[0] == 0
    places = tile_pieces(info_ref, mine_ref.shape[0])
    mine = [mine_ref[place, direction] for place in places]
    other = [other_ref[place, direction] for place in places]
    mine = mine[0] if len(mine) == 1 else jnp.concatenate(mine, axis=1)
    other = other[0] if len(other) == 1 else jnp.concatenate(other, axis=1)
    halves = [jnp.where(first_is_mine, mine, other), jnp.where(first_is_mine, other, mine)]
    per = halves[0].shape[0] // BLOCK
    return [half[i * BLOCK : (i + 1) * BLOCK] for half in halves for i in range(per)]


def conv_fwd_body(
    info_ref, table_ref, inverse_ref, xf_ref, xb_ref, mine_ref, other_ref, *rest
):
    prod_ref, al_ref, ag_ref = rest[-11:-8]
    scratch = rest[-8:]
    longer = info_ref[2].astype(F32)
    width = xf_ref.shape[1]
    for direction, (x_ref, out_ref) in enumerate(((xf_ref, al_ref), (xb_ref, ag_ref))):
        x_spec, k_spec, y_high, y_low = scratch[4 * direction : 4 * direction + 4]
        blocks = [load_block(x_ref, i) for i in range(SECTIONS)]
        spectra(table_ref, blocks, x_spec)
        spectra(table_ref, kernel_blocks(info_ref, mine_ref, other_ref, direction), k_spec)
        for parity, re_rows, im_rows, columns in chunks(width):
            bands = band_spectra(load_spectra(k_spec, re_rows, im_rows, columns), parity, longer)
            values = load_spectra(x_spec, re_rows, im_rows, columns)
            for column, (re, im) in zip(columns, conv_spectra(bands, values, direction == 1)):
                split_store(y_high, y_low, re_rows, column, re)
                split_store(y_high, y_low, im_rows, column, im)
        result = inverse(inverse_ref, y_high, y_low)
        for i in range(SECTIONS):
            place = slice(i * width, (i + 1) * width)
            store_block(out_ref, i, result[:, place])
            if direction == 0:
                x_spec[:BLOCK, place] = result[:, place]
            else:
                store_block(prod_ref, i, scratch[0][:BLOCK, place] * result[:, place])


def kernel_spec(own, count):
    shift = count.bit_length() - 1
    return pl.BlockSpec(
        (count, 2, LENGTH // 2, own), lambda c, info: (c ^ (info[1] >> shift), 0, 0, 0)
    )


def tile_of(own):
    count = 1
    while (count * own) % 128:
        count *= 2
    return count, count * own


def conv_fwd(info, tables, act_forward, act_backward, mine, other, after):
    rows, channels = act_forward.shape
    count, width = tile_of(mine.shape[3])
    whole = lambda c, info: (0, 0)
    whole3 = lambda c, info: (0, 0, 0)
    column = lambda c, info: (0, c)
    forward, back = tables
    wide = SECTIONS * width
    return pl.pallas_call(
        conv_fwd_body,
        out_shape=[
            jax.ShapeDtypeStruct((rows, channels), BF16),
            jax.ShapeDtypeStruct((rows, channels), BF16),
            jax.ShapeDtypeStruct((rows, channels), BF16),
        ],
        grid_spec=pltpu.PrefetchScalarGridSpec(
            num_scalar_prefetch=1,
            grid=(channels // width,),
            in_specs=[
                pl.BlockSpec(forward.shape, whole),
                pl.BlockSpec(back.shape, whole3),
                pl.BlockSpec((rows, width), column),
                pl.BlockSpec((rows, width), column),
                kernel_spec(mine.shape[3], count),
                kernel_spec(mine.shape[3], count),
            ]
            + [ANY] * len(after),
            out_specs=[pl.BlockSpec((rows, width), column)] * 3,
            scratch_shapes=[
                pltpu.VMEM((2 * FREQ, wide), F32),
                pltpu.VMEM((2 * FREQ, wide), F32),
                pltpu.VMEM((2 * FREQ, wide), BF16),
                pltpu.VMEM((2 * FREQ, wide), BF16),
            ]
            * 2,
        ),
        compiler_params=pltpu.CompilerParams(vmem_limit_bytes=VMEM),
        cost_estimate=cost(17),
        name="conv_fwd",
    )(info, forward, back, act_forward, act_backward, mine, other, *after)


def conv_bwd_body(
    info_ref, table_ref, inverse_ref, gp_ref, al_ref, ag_ref, xf_ref, xb_ref, sf_ref, sb_ref,
    mine_ref, other_ref, *rest,
):
    gf_ref, gb_ref, keep_ref, send_ref = rest[-18:-14]
    scratch = rest[-14:]
    longer = info_ref[2].astype(F32)
    width = xf_ref.shape[1]
    ways = ((xf_ref, ag_ref, sf_ref, gf_ref), (xb_ref, al_ref, sb_ref, gb_ref))
    for direction, (x_ref, other_way, slope_ref, out_ref) in enumerate(ways):
        x_spec, k_spec, g_spec, y_high, y_low, h_high, h_low = scratch[7 * direction : 7 * direction + 7]
        upstream = [
            (
                load_block(gp_ref, i).astype(F32)
                * load_block(other_way, i).astype(F32)
            ).astype(BF16)
            for i in range(SECTIONS)
        ]
        spectra(table_ref, upstream, g_spec)
        spectra(table_ref, kernel_blocks(info_ref, mine_ref, other_ref, direction), k_spec)
        spectra(table_ref, [load_block(x_ref, i) for i in range(SECTIONS)], x_spec)
        for parity, re_rows, im_rows, columns in chunks(width):
            grads = load_spectra(g_spec, re_rows, im_rows, columns)
            bands = band_spectra(load_spectra(k_spec, re_rows, im_rows, columns), parity, longer)
            for column, (re, im) in zip(columns, conv_spectra(bands, grads, direction == 0)):
                split_store(y_high, y_low, re_rows, column, re)
                split_store(y_high, y_low, im_rows, column, im)
            values = load_spectra(x_spec, re_rows, im_rows, columns)
            above = None
            for m in reversed(range(SECTIONS)):
                total = None
                for i in range(m, SECTIONS):
                    if direction == 0:
                        total = cfma(total, values[i - m], grads[i], True)
                    else:
                        total = cfma(total, grads[i - m], values[i], True)
                if m:
                    total = (total[0] * longer, total[1] * longer)
                folded = total
                if above is not None:
                    folded = cadd(total, turned(above, 1 - parity))
                split_store(h_high, h_low, re_rows, columns[m], folded[0])
                split_store(h_high, h_low, im_rows, columns[m], folded[1])
                above = total
        result = inverse(inverse_ref, y_high, y_low)
        for i in range(SECTIONS):
            grad_act = result[:, i * width : (i + 1) * width].astype(BF16).astype(F32)
            slope = load_block(slope_ref, i).astype(F32)
            store_block(out_ref, i, grad_act * slope)
        result = inverse(inverse_ref, h_high, h_low).astype(BF16)
        first_is_mine = info_ref[0] == 0
        own, per = keep_ref.shape[3], keep_ref.shape[2]
        half = SECTIONS // 2
        for piece in range(keep_ref.shape[1]):
            for i in range(half):
                low = result[:, i * width + piece * own : i * width + (piece + 1) * own]
                top = (half + i) * width
                high = result[:, top + piece * own : top + (piece + 1) * own]
                for start in range(0, BLOCK, per):
                    place = ((direction * half + i) * BLOCK + start) // per
                    first, second = low[start : start + per], high[start : start + per]
                    keep_ref[place, piece] = jnp.where(first_is_mine, first, second)
                    send_ref[place, piece] = jnp.where(first_is_mine, second, first)


def conv_bwd(
    info, tables, grad_product, along, against, act_f, act_b, slope_f, slope_b, mine, other, parts,
    after,
):
    rows, channels = act_f.shape
    own = mine.shape[3]
    count, width = tile_of(own)
    whole = lambda c, info: (0, 0)
    whole3 = lambda c, info: (0, 0, 0)
    column = lambda c, info: (0, c)
    forward, back = tables
    wide = SECTIONS * width
    return pl.pallas_call(
        conv_bwd_body,
        out_shape=[
            jax.ShapeDtypeStruct((rows, channels), BF16),
            jax.ShapeDtypeStruct((rows, channels), BF16),
            jax.ShapeDtypeStruct((parts, mine.shape[0], LENGTH // parts, own), BF16),
            jax.ShapeDtypeStruct((parts, mine.shape[0], LENGTH // parts, own), BF16),
        ],
        grid_spec=pltpu.PrefetchScalarGridSpec(
            num_scalar_prefetch=1,
            grid=(channels // width,),
            in_specs=[
                pl.BlockSpec(forward.shape, whole),
                pl.BlockSpec(back.shape, whole3),
            ]
            + [pl.BlockSpec((rows, width), column)] * 7
            + [kernel_spec(own, count)] * 2
            + [ANY] * len(after),
            out_specs=[
                pl.BlockSpec((rows, width), column),
                pl.BlockSpec((rows, width), column),
                pl.BlockSpec((parts, count, LENGTH // parts, own), lambda c, info: (0, c, 0, 0)),
                pl.BlockSpec((parts, count, LENGTH // parts, own), lambda c, info: (0, c, 0, 0)),
            ],
            scratch_shapes=(
                [pltpu.VMEM((2 * FREQ, wide), F32)] * 3 + [pltpu.VMEM((2 * FREQ, wide), BF16)] * 4
            )
            * 2,
        ),
        compiler_params=pltpu.CompilerParams(vmem_limit_bytes=VMEM),
        cost_estimate=cost(28),
        name="conv_bwd",
    )(
        info, forward, back, grad_product, along, against, act_f, act_b, slope_f, slope_b,
        mine, other, *after,
    )


def packed_rows(total_ref, core, n_dp, n_seq, small, out_ref):
    size = total_ref.shape[0] // n_dp
    per = size // n_seq
    groups = n_dp // 2
    count = n_seq * small
    for group in range(groups):
        for place, which in enumerate((1 - core, core)):
            start = pl.multiple_of((2 * group + which) * size, 8)
            value = total_ref[pl.ds(start, size), :]
            for fold in range(per // small):
                first = fold * small
                rows = [value[s * per + first : s * per + first + small] for s in range(n_seq)]
                target = ((place * (per // small) + fold) * groups + group) * count
                out_ref[pl.ds(target, count), :] = jnp.concatenate(rows, axis=0).astype(out_ref.dtype)


def store_split(result, groups, folds, send_ref, keep_ref, offset):
    count = send_ref.shape[1]
    width = result.shape[1]
    for place, ref in enumerate((send_ref, keep_ref)):
        for fold in range(folds):
            for group in range(groups):
                first = ((place * folds + fold) * groups + group) * count
                columns = pl.ds(offset + fold * width, width)
                ref[group, :, columns] = result[first : first + count].astype(BF16)


def middle_body(
    info_ref, prod_ref, normed_ref, cot_ref, uw_ref, ow_ref, va_ref, vs_ref, *rest, n_dp, n_seq, small
):
    send_ref, keep_ref, og_ref, gated_ref, dv_ref, gp_ref, nt_ref = rest[:7]
    du_ref, pt_ref, flipped, gp_acc = rest[7:]
    step = pl.program_id(0)

    @pl.when(step == 0)
    def _():
        for source, target in ((prod_ref, pt_ref), (normed_ref, nt_ref)):
            rows = flipped.at[pl.ds(0, source.shape[1])]
            rows[...] = source[...].astype(F32).T
            packed_rows(rows, info_ref[0], n_dp, n_seq, small, target)
        gp_acc[...] = jnp.zeros_like(gp_acc)

    size = 2 * BLOCK
    for start in range(0, prod_ref.shape[0], size):
        rows = pl.ds(start, size)
        update_act, update_slope = gelu_pair(dot(prod_ref[rows, :], uw_ref[...]))
        grad_gated = dot_rt(cot_ref[rows, :], ow_ref[...])
        value_act = va_ref[rows, :].astype(F32)
        gated_ref[rows, :] = (update_act * value_act).astype(BF16)
        du_ref[rows, :] = (grad_gated * value_act * update_slope).astype(BF16)
        dv_ref[rows, :] = (grad_gated * update_act * vs_ref[rows, :].astype(F32)).astype(BF16)
    folds = prod_ref.shape[1] // normed_ref.shape[1]
    tile = uw_ref.shape[1]
    groups = n_dp // 2
    store_split(dot(pt_ref[...], du_ref[...]), groups, folds, send_ref, keep_ref, 0)
    store_split(dot(nt_ref[...], dv_ref[...]), groups, 1, send_ref, keep_ref, folds * tile)
    og_ref[...] = dot_lt(gated_ref[...], cot_ref[...]).astype(BF16)
    gp_acc[...] += dot_rt(du_ref[...], uw_ref[...])

    @pl.when(step == pl.num_programs(0) - 1)
    def _():
        gp_ref[...] = gp_acc[...].astype(BF16)


def middle(
    info, product, normed, cot, update_weight, output_weight, value_act, value_slope, n_dp, n_seq
):
    rows, channels = product.shape
    hidden, width = output_weight.shape
    tile = HIDDEN_TILE
    steps = hidden // tile
    small = width // (n_dp * n_seq)
    groups = n_dp // 2
    block = (channels // width + 1) * tile
    whole = lambda t, info: (0, 0)
    column = lambda t, info: (0, t)
    out_block = pl.BlockSpec((groups, n_seq * small, block), lambda t, info: (0, 0, t))
    return pl.pallas_call(
        functools.partial(middle_body, n_dp=n_dp, n_seq=n_seq, small=small),
        out_shape=[jax.ShapeDtypeStruct((groups, n_seq * small, steps * block), BF16)] * 2
        + [
            jax.ShapeDtypeStruct((hidden, width), BF16),
            jax.ShapeDtypeStruct((rows, hidden), BF16),
            jax.ShapeDtypeStruct((rows, hidden), BF16),
            jax.ShapeDtypeStruct((rows, channels), BF16),
            jax.ShapeDtypeStruct((width, rows), BF16),
        ],
        grid_spec=pltpu.PrefetchScalarGridSpec(
            num_scalar_prefetch=1,
            grid=(steps,),
            in_specs=[
                pl.BlockSpec((rows, channels), whole),
                pl.BlockSpec((rows, width), whole),
                pl.BlockSpec((rows, width), whole),
                pl.BlockSpec((channels, tile), column),
                pl.BlockSpec((tile, width), lambda t, info: (t, 0)),
                pl.BlockSpec((rows, tile), column),
                pl.BlockSpec((rows, tile), column),
            ],
            out_specs=[
                out_block,
                out_block,
                pl.BlockSpec((tile, width), lambda t, info: (t, 0)),
                pl.BlockSpec((rows, tile), column),
                pl.BlockSpec((rows, tile), column),
                pl.BlockSpec((rows, channels), whole),
                pl.BlockSpec((width, rows), whole),
            ],
            scratch_shapes=[
                pltpu.VMEM((rows, tile), BF16),
                pltpu.VMEM((channels, rows), BF16),
                pltpu.VMEM((channels, rows), F32),
                pltpu.VMEM((rows, channels), F32),
            ],
        ),
        compiler_params=pltpu.CompilerParams(vmem_limit_bytes=VMEM),
        cost_estimate=cost(40),
        name="middle",
    )(info, product, normed, cot, update_weight, output_weight, value_act, value_slope)


def layer_body(gated_ref, dv_ref, ow_ref, vw_ref, tokens_ref, *rest):
    layer_ref, gv_ref, lo_acc = rest[-3:]
    step = pl.program_id(0)

    @pl.when(step == 0)
    def _():
        lo_acc[...] = jnp.zeros_like(lo_acc)
        gv_ref[...] = jnp.zeros_like(gv_ref)

    lo_acc[...] += dot(gated_ref[...], ow_ref[...])
    gv_ref[...] += dot_rt(dv_ref[...], vw_ref[...])

    @pl.when(step == pl.num_programs(0) - 1)
    def _():
        layer_ref[...] = (tokens_ref[...].astype(F32) + lo_acc[...]).astype(BF16)


def layer_rows_of(gated, grad_value_in, output_weight, value_weight, tokens, after):
    rows, hidden = gated.shape
    width = output_weight.shape[1]
    tile = 1024
    whole = lambda t: (0, 0)
    column = lambda t: (0, t)
    return pl.pallas_call(
        layer_body,
        out_shape=[
            jax.ShapeDtypeStruct((rows, width), BF16),
            jax.ShapeDtypeStruct((rows, width), F32),
        ],
        grid=(hidden // tile,),
        in_specs=[
            pl.BlockSpec((rows, tile), column),
            pl.BlockSpec((rows, tile), column),
            pl.BlockSpec((tile, width), lambda t: (t, 0)),
            pl.BlockSpec((width, tile), column),
            pl.BlockSpec((rows, width), whole),
        ]
        + [ANY] * len(after),
        out_specs=[pl.BlockSpec((rows, width), whole)] * 2,
        scratch_shapes=[pltpu.VMEM((rows, width), F32)],
        compiler_params=pltpu.CompilerParams(vmem_limit_bytes=VMEM),
        cost_estimate=cost(9),
        name="layer_rows",
    )(gated, grad_value_in, output_weight, value_weight, tokens, *after)


def inner_grad_body(nt_ref, df_ref, db_ref, *rest, groups):
    send_ref, keep_ref = rest[-2:]
    tile = df_ref.shape[1]
    store_split(dot(nt_ref[...], df_ref[...]), groups, 1, send_ref, keep_ref, 0)
    store_split(dot(nt_ref[...], db_ref[...]), groups, 1, send_ref, keep_ref, tile)


def inner_weight_grad(normed_t, grad_f, grad_b, n_dp, n_seq, after):
    width, rows = normed_t.shape
    channels = grad_f.shape[1]
    small = width // (n_dp * n_seq)
    groups = n_dp // 2
    column = lambda t: (0, t)
    out_block = pl.BlockSpec((groups, n_seq * small, 2 * INNER), lambda t: (0, 0, t))
    return pl.pallas_call(
        functools.partial(inner_grad_body, groups=groups),
        out_shape=[jax.ShapeDtypeStruct((groups, n_seq * small, 2 * channels), BF16)] * 2,
        grid=(channels // INNER,),
        in_specs=[
            pl.BlockSpec((width, rows), lambda t: (0, 0)),
            pl.BlockSpec((rows, INNER), column),
            pl.BlockSpec((rows, INNER), column),
        ]
        + [ANY] * len(after),
        out_specs=[out_block, out_block],
        compiler_params=pltpu.CompilerParams(vmem_limit_bytes=VMEM),
        cost_estimate=cost(6),
        name="inner_weight_grad",
    )(normed_t, grad_f, grad_b, *after)


def out_body(
    tokens_ref, cot_ref, gain_ref, gv_ref, layer_ref, df_ref, db_ref, fw_ref, bw_ref, *rest
):
    out_ref, total = rest[-2:]
    step = pl.program_id(0)

    @pl.when(step == 0)
    def _():
        total[...] = gv_ref[...]

    total[...] += dot_rt(df_ref[...], fw_ref[...]) + dot_rt(db_ref[...], bw_ref[...])

    @pl.when(step == pl.num_programs(0) - 1)
    def _():
        size = out_ref.shape[2]
        for index in range(out_ref.shape[0]):
            rows = pl.ds(index * size, size)
            unit, inv_std = norm_stats(tokens_ref[rows, :].astype(F32))
            grad_unit = total[rows, :] * gain_ref[...]
            grad_input = inv_std * (
                grad_unit
                - jnp.mean(grad_unit, axis=1, keepdims=True)
                - unit * jnp.mean(grad_unit * unit, axis=1, keepdims=True)
            )
            out_ref[index, 0] = layer_ref[rows, :]
            out_ref[index, 1] = (cot_ref[rows, :].astype(F32) + grad_input).astype(BF16)


def out_proj(
    tokens, cot, gain, grad_value_part, layer_rows, grad_f, grad_b, forward_weight, backward_weight,
    n_seq, after,
):
    rows, channels = grad_f.shape
    width = tokens.shape[1]
    tile = INNER
    whole = lambda t: (0, 0)
    column = lambda t: (0, t)
    shape = (n_seq, 2, rows // n_seq, width)
    return pl.pallas_call(
        out_body,
        out_shape=jax.ShapeDtypeStruct(shape, BF16),
        grid=(channels // tile,),
        in_specs=[
            pl.BlockSpec((rows, width), whole),
            pl.BlockSpec((rows, width), whole),
            pl.BlockSpec((1, width), whole),
            pl.BlockSpec((rows, width), whole),
            pl.BlockSpec((rows, width), whole),
            pl.BlockSpec((rows, tile), column),
            pl.BlockSpec((rows, tile), column),
            pl.BlockSpec((width, tile), column),
            pl.BlockSpec((width, tile), column),
        ]
        + [ANY] * len(after),
        out_specs=pl.BlockSpec(shape, lambda t: (0, 0, 0, 0)),
        scratch_shapes=[pltpu.VMEM((rows, width), F32)],
        compiler_params=pltpu.CompilerParams(vmem_limit_bytes=VMEM),
        cost_estimate=cost(10),
        name="out_proj",
    )(
        tokens, cot, gain.reshape(1, -1), grad_value_part, layer_rows, grad_f, grad_b,
        forward_weight, backward_weight, *after,
    )


def swap(value, axis, mask):
    return lax.ppermute(value, axis, [(i, i ^ mask) for i in range(lax.axis_size(axis))])


def total_of(pieces):
    total = pieces[0].astype(F32)
    for piece in pieces[1:]:
        total = total + piece.astype(F32)
    return total


def with_bit(index, place, bit):
    low = index & ((1 << place) - 1)
    return ((index >> place) << (place + 1)) | (bit << place) | low


SLOT = {"dp": 3, "seq": 1}


def grid_place(step, grid):
    if grid[0] * grid[1] == 1:
        return [0, 0]
    step = jnp.minimum(step, grid[0] * grid[1] - 1)
    if grid[1] == 1:
        return [step, 0]
    return [step // grid[1], step % grid[1]] if grid[0] > 1 else [0, step]


class Scatter:

    def __init__(self, info, pieces, shape, order):
        self.info, self.shape, self.order = info, shape, list(order)
        self.pieces = list(pieces)
        self.stages = []

    def place(self, axis, bit):
        dim, place = (0, bit - 1) if axis == "dp" else (1, bit)
        lower = [b for a, b, _, _ in self.stages if a == axis and b < bit]
        return dim, place - len(lower)

    def index_map(self, level, column, last, grid):
        stages = self.stages[level:]

        def found(step, info):
            coords = grid_place(step, grid)
            if last is not None:
                axis, bit, dim, place = last
                coords[dim] = with_bit(coords[dim], place, 1 - ((info[SLOT[axis]] >> bit) & 1))
            for axis, bit, dim, place in reversed(stages):
                coords[dim] = with_bit(coords[dim], place, (info[SLOT[axis]] >> bit) & 1)
            return (coords[0], coords[1], 0, column)

        return found

    def sizes(self, stages):
        sizes = list(self.shape[:2])
        for _, _, dim, _ in stages:
            sizes[dim] //= 2
        return sizes

    def specs(self, last):
        stages = self.stages + ([last] if last else [])
        touched = {stage[2] for stage in stages}
        sizes = self.sizes(stages)
        lead = [1 if dim in touched else self.shape[dim] for dim in range(2)]
        grid = [sizes[dim] // lead[dim] for dim in range(2)]
        block = tuple(lead) + self.shape[2:]
        specs = [
            pl.BlockSpec(block, self.index_map(level, column, last, grid))
            for level, column, _ in self.pieces
        ]
        return block, grid, specs

    def next_stage(self):
        axis, bit = self.order[0]
        return (axis, bit) + self.place(axis, bit)


def add_body(info_ref, *refs, layout, first_out):
    refs = list(refs)
    out_refs = refs[first_out:]
    for count, out, column in layout:
        total = total_of([refs.pop(0)[...] for _ in range(count)]).astype(BF16)
        width = total.shape[3]
        out_refs[out][:, :, :, column * width : (column + 1) * width] = total


def step_apart(groups, after=(), passed=()):
    arrays, in_specs, out_specs, out_shape, layout, steps = [], [], [], [], [], 1
    for group in groups:
        merged = len({scatter.order[0] for scatter in group}) == 1
        for index, scatter in enumerate(group):
            stage = scatter.next_stage()
            block, grid, specs = scatter.specs(stage)
            sizes = scatter.sizes(scatter.stages + [stage])
            arrays += [piece for _, _, piece in scatter.pieces]
            in_specs += specs
            steps = max(steps, grid[0] * grid[1])
            width = scatter.shape[3]

            def out_map(step, info, grid=grid):
                return (*grid_place(step, grid), 0, 0)

            layout.append((len(specs), len(out_shape) - (1 if merged and index else 0), index if merged else 0))
            if merged and index:
                continue
            wide = width * len(group) if merged else width
            out_shape.append(jax.ShapeDtypeStruct(tuple(sizes) + (scatter.shape[2], wide), BF16))
            out_specs.append(pl.BlockSpec(block[:3] + (wide,), out_map))
    sums = len(out_shape)
    first_passed = 1 + len(arrays) + len(after)
    out_shape += [jax.ShapeDtypeStruct(value.shape, value.dtype) for value in passed]
    sent = pl.pallas_call(
        functools.partial(add_body, layout=tuple(layout), first_out=len(arrays) + len(after) + len(passed)),
        out_shape=out_shape,
        grid_spec=pltpu.PrefetchScalarGridSpec(
            num_scalar_prefetch=1,
            grid=(steps,),
            in_specs=in_specs + [ANY] * (len(after) + len(passed)),
            out_specs=out_specs + [ANY] * len(passed),
        ),
        input_output_aliases={first_passed + i: sums + i for i in range(len(passed))},
        compiler_params=pltpu.CompilerParams(vmem_limit_bytes=FULL_VMEM),
        cost_estimate=cost(3),
        name="add_sent",
    )(groups[0][0].info, *arrays, *after, *passed)
    arrived = {}
    for scatter, (_, out, column) in zip([s for group in groups for s in group], layout):
        axis, bit = scatter.order[0]
        if out not in arrived:
            arrived[out] = swap(sent[out], axis, 1 << bit)
        scatter.stages.append(scatter.next_stage())
        scatter.order.pop(0)
        scatter.pieces.append((len(scatter.stages), column, arrived[out]))
    return [sent[0], *sent[sums:]] if passed else sent[0]


def partner_body(info_ref, *refs, count, partners):
    outs = refs[-partners:]
    for index, out_ref in enumerate(outs):
        out_ref[...] = total_of([ref[0, 0] for ref in refs[index * count : (index + 1) * count]]).astype(BF16)


def sums_for_partners(scatter, partners, after):
    specs = []
    for mask in range(partners):
        for level, column, _ in scatter.pieces:
            whole = scatter.index_map(level, column, None, [1, 1])

            def found(step, info, whole=whole, mask=mask):
                place = whole(step, info)
                return (place[0], info[SLOT["seq"]] ^ mask, 0, 0)

            specs.append(pl.BlockSpec((1, 1) + scatter.shape[2:], found))
    count = len(scatter.pieces)
    shape = scatter.shape[2:]
    return pl.pallas_call(
        functools.partial(partner_body, count=count, partners=partners),
        out_shape=[jax.ShapeDtypeStruct(shape, BF16)] * partners,
        grid_spec=pltpu.PrefetchScalarGridSpec(
            num_scalar_prefetch=1,
            grid=(1,),
            in_specs=specs + [ANY] * len(after),
            out_specs=[pl.BlockSpec(shape, lambda t, info: (0, 0))] * partners,
        ),
        compiler_params=pltpu.CompilerParams(vmem_limit_bytes=VMEM),
        cost_estimate=cost(3),
        name="partner_sums",
    )(scatter.info, *[piece for _, _, piece in scatter.pieces] * partners, *after)


def sum_body(*refs, count):
    refs[-1][0] = total_of([ref[...] for ref in refs[:count]]).astype(BF16)


def sum_of(pieces, after):
    shape = pieces[0].shape
    return pl.pallas_call(
        functools.partial(sum_body, count=len(pieces)),
        out_shape=jax.ShapeDtypeStruct((1,) + shape, BF16),
        grid=(1,),
        in_specs=[pl.BlockSpec(shape, lambda t: (0, 0))] * len(pieces) + [ANY] * len(after),
        out_specs=pl.BlockSpec((1,) + shape, lambda t: (0, 0, 0)),
        cost_estimate=cost(3),
        name="sum_of",
    )(*pieces, *after)


def finish(scatters, out_shape, write, after, name):
    arrays, specs, counts = [], [], []
    for scatter in scatters:
        own = scatter.specs(None)[2]
        specs += own
        arrays += [piece for _, _, piece in scatter.pieces]
        counts.append(len(own))

    def body(info_ref, *refs):
        refs = list(refs)
        sums = [total_of([refs.pop(0)[0, 0] for _ in range(count)]) for count in counts]
        write(sums, *refs[len(after) :])

    return pl.pallas_call(
        body,
        out_shape=out_shape,
        grid_spec=pltpu.PrefetchScalarGridSpec(
            num_scalar_prefetch=1,
            grid=(1,),
            in_specs=specs + [ANY] * len(after),
            out_specs=[
                pl.BlockSpec(shape.shape, lambda t, info: (0, 0)) for shape in out_shape
            ],
        ),
        compiler_params=pltpu.CompilerParams(vmem_limit_bytes=VMEM),
        cost_estimate=cost(3),
        name=name,
    )(scatters[0].info, *arrays, *after)


def to_row(value):
    moved = lax.all_to_all(value, "seq", split_axis=0, concat_axis=0, tiled=True)
    return moved.reshape(-1, value.shape[2])


def on_device(
    tokens,
    doc_ids,
    norm_gain,
    value_weight,
    forward_weight,
    backward_weight,
    update_weight,
    output_weight,
    kernel_params,
    cotangent,
):
    n_dp, n_seq = lax.axis_size("dp"), lax.axis_size("seq")
    dp_index, seq_index = lax.axis_index("dp"), lax.axis_index("seq")
    channels = forward_weight.shape[1]
    own_channels = kernel_params.shape[3]
    core = dp_index % 2
    docs = lax.dynamic_index_in_dim(doc_ids, seq_index, 0, keepdims=False)
    longer = (docs[0] == docs[-1]).astype(jnp.int32)
    info = jnp.stack([core, seq_index, longer, dp_index]).astype(jnp.int32)
    tables = fourier_tables()

    row_tokens = to_row(tokens)
    half = pass_after(kernel_gen(info, kernel_params), [row_tokens])
    halves = [half if mask == 0 else swap(half, "seq", mask) for mask in range(n_seq)]
    normed, act_f, slope_f, act_b, slope_b, value_act, value_slope = in_proj(
        row_tokens, norm_gain, forward_weight, backward_weight, value_weight
    )
    mine = stack_pieces(halves, [value_act])
    other = swap(mine, "dp", 1)
    cot = to_row(cotangent)
    product, along, against = conv_fwd(info, tables, act_f, act_b, mine, other, [])

    seq_bits = [("seq", bit) for bit in range(n_seq.bit_length() - 1)]
    dp_bits = [("dp", bit) for bit in range(1, n_dp.bit_length() - 1)]
    shape = (n_dp // 2, n_seq, tokens.shape[2] // (n_dp * n_seq))

    def scatter_of(send, keep, order, columns=None):
        width = send.shape[2] // (columns or 1)
        whole = shape + (send.shape[2],)
        arrays = [keep.reshape(whole), swap(send, "dp", 1).reshape(whole)]
        return [
            Scatter(info, [(0, column, array) for array in arrays], shape + (width,), order[column])
            for column in range(columns or 1)
        ]

    send, keep, output_part, gated, grad_value_in, grad_product, normed_t = middle(
        info, product, normed, cot, update_weight, output_weight, value_act, value_slope, n_dp, n_seq
    )
    output_sum = lax.psum_scatter(output_part, "dp", scatter_dimension=0, tiled=True)
    layer_rows, grad_value_part = layer_rows_of(
        gated, grad_value_in, output_weight, value_weight, row_tokens, []
    )
    both = scatter_of(send, keep, [seq_bits + dp_bits, seq_bits[::-1] + dp_bits], 2)
    sent = step_apart([both[:1], both[1:]], [layer_rows])
    parts = n_dp // 2
    grad_f, grad_b, kernel_keep, kernel_send = conv_bwd(
        info, tables, grad_product, along, against, act_f, act_b, slope_f, slope_b, mine, other,
        parts, [sent],
    )
    send, keep = inner_weight_grad(normed_t, grad_f, grad_b, n_dp, n_seq, [])

    sent, send, kernel_send = step_apart([both[:1], both[1:]], [], [send, kernel_send])
    inner = scatter_of(send, keep, [seq_bits + dp_bits, seq_bits[::-1] + dp_bits], 2)
    blocks = kernel_keep.shape
    kernel = [
        Scatter(
            info,
            [(0, 0, kernel_keep), (0, 0, swap(kernel_send, "dp", 1))],
            blocks,
            dp_bits,
        )
    ]
    for _ in range(n_seq.bit_length() - 3):
        sent = step_apart([both[:1], both[1:]], [sent])
    sent = step_apart([inner[:1], inner[1:], kernel], [sent])
    out_pieces = out_proj(
        row_tokens, cot, norm_gain, grad_value_part, layer_rows, grad_f, grad_b,
        forward_weight, backward_weight, n_seq, [sent],
    )
    sent = step_apart([both, kernel], [sent, out_pieces])
    while kernel[0].order:
        sent = step_apart([kernel], [sent])
    output_blocks = (1, n_seq, output_sum.shape[0] // n_seq, output_sum.shape[1])
    output = [Scatter(info, [(0, 0, output_sum.reshape(output_blocks))], output_blocks, seq_bits[::-1])]
    for _ in range(n_seq.bit_length() - 2):
        sent = step_apart([inner[:1], inner[1:], output], [sent])
    halves = sums_for_partners(kernel[0], n_seq, [sent])
    halves = [half if mask == 0 else swap(half, "seq", mask) for mask, half in enumerate(halves)]
    sent = step_apart([inner, output], [halves[0]])
    while both[0].order:
        sent = step_apart([both], [sent])
    part = sum_of(halves, [sent])
    parts = [part if mask == 0 else swap(part, "dp", mask << 1) for mask in range(n_dp // 2)]
    while inner[0].order:
        sent = step_apart([inner], [part])
    width = tokens.shape[2]
    small = width // (n_dp * n_seq)
    hidden = update_weight.shape[1]
    folds = channels // width
    tile = HIDDEN_TILE

    def write_first(sums, update_ref, value_ref, output_ref):
        column = 0
        output_ref[...] = sums[-1]
        for total in sums[:-1]:
            for start in range(0, total.shape[1], (folds + 1) * tile):
                columns = pl.ds(column, tile)
                for fold in range(folds):
                    part = total[:, start + fold * tile : start + (fold + 1) * tile]
                    update_ref[pl.ds(fold * small, small), columns] = part
                value_ref[:, columns] = total[:, start + folds * tile : start + (folds + 1) * tile]
                column += tile

    def write_inner(sums, forward_ref, backward_ref):
        for index, total in enumerate(sums):
            columns = pl.ds(index * INNER, INNER)
            forward_ref[:, columns] = total[:, :INNER]
            backward_ref[:, columns] = total[:, INNER : 2 * INNER]

    shape_of = lambda *shape: jax.ShapeDtypeStruct(shape, F32)
    first_shapes = [shape_of(folds * small, hidden), shape_of(small, hidden), shape_of(*output_blocks[2:])]
    update_grad, value_grad, output_grad = finish(
        both + output, first_shapes, write_first, [sent], "first_sums"
    )
    gathered = stack_pieces(parts, [update_grad]).reshape((-1,) + part.shape[1:])
    others = swap(gathered, "dp", 1)
    moved = lax.all_to_all(out_pieces, "seq", split_axis=0, concat_axis=0, tiled=True)

    forward_grad, backward_grad = finish(
        inner, [shape_of(small, channels)] * 2, write_inner, [gathered], "inner_sums"
    )
    params_grad = params_grad_of(info, kernel_params, gathered, others, n_dp, [forward_grad])

    layer_out, tokens_grad = moved[:, 0], moved[:, 1]

    own_rows = lambda value: lax.dynamic_slice_in_dim(value, (dp_index * n_seq + seq_index) * small, small, 0)
    gain_sums = sum(
        jnp.sum(own_rows(weight).astype(F32) * grad, axis=1)
        for weight, grad in (
            (value_weight, value_grad), (forward_weight, forward_grad), (backward_weight, backward_grad)
        )
    )
    gain_grad = gain_sums / own_rows(norm_gain)
    return (
        layer_out,
        tokens_grad,
        gain_grad,
        value_grad,
        forward_grad,
        backward_grad,
        update_grad,
        output_grad,
        params_grad,
    )


def solution(mesh):
    placed = (
        P("dp", "seq", None),
        P("dp", None),
        P(),
        P(),
        P(),
        P(),
        P(),
        P(),
        P(None, None, None, "seq"),
        P("dp", "seq", None),
    )
    return jax.shard_map(
        on_device,
        mesh=mesh,
        in_specs=placed,
        out_specs=(
            P("dp", "seq", None),
            P("dp", "seq", None),
            P(("dp", "seq")),
            P(("dp", "seq"), None),
            P(("dp", "seq"), None),
            P(("dp", "seq"), None),
            P(("dp", "seq"), None),
            P(("dp", "seq"), None),
            P(None, None, "dp", "seq"),
        ),
        check_vma=False,
    )
```

```python
import functools
import math

import jax
import jax.numpy as jnp
import ml_dtypes
import numpy as np
from jax import lax
from jax.experimental import pallas as pl
from jax.experimental.pallas import tpu as pltpu
from jax.sharding import PartitionSpec as P

LENGTH = 512
BLOCK = 128
SECTIONS = LENGTH // BLOCK
FREQ = 128
HALF_FREQ = FREQ // 2
LOW = 16
INNER = 768
HIDDEN_TILE = 768
ANY = pl.BlockSpec(memory_space=pl.ANY)
VMEM = 63 * 1024 * 1024
FULL_VMEM = 63 * 1024 * 1024
BF16 = jnp.bfloat16
F32 = jnp.float32


def cost(microseconds):
    return pl.CostEstimate(flops=int(microseconds * 2e+07), bytes_accessed=0, transcendentals=0)


def dot(first_mat, second_mat):
    return jnp.dot(first_mat, second_mat, preferred_element_type=F32)


def dot_rt(first_mat, second_mat):
    return lax.dot_general(
        first_mat, second_mat, (((1,), (1,)), ((), ())), preferred_element_type=F32
    )


def dot_lt(first_mat, second_mat):
    return lax.dot_general(
        first_mat, second_mat, (((0,), (0,)), ((), ())), preferred_element_type=F32
    )


def fourier_tables():
    order = np.concatenate([np.arange(0, FREQ, 2), np.arange(1, FREQ, 2)])
    angle = 2.0 * np.pi * (order[:, None] + 0.5) * np.arange(BLOCK)[None, :] / (2 * BLOCK)
    table = np.concatenate([np.cos(angle), -np.sin(angle)], axis=0)
    high = table.astype(ml_dtypes.bfloat16)
    low = (table - high.astype(np.float64)).astype(ml_dtypes.bfloat16)
    forward = np.concatenate([high, low], axis=1)
    scale = ml_dtypes.bfloat16(1.0 / FREQ)
    inverse = np.stack([high.T * scale, low.T * scale]).astype(ml_dtypes.bfloat16)
    return jnp.asarray(forward), jnp.asarray(inverse)


def gelu_pair(v):
    cdf = 0.5 * lax.erf(v * (1.0 / math.sqrt(2.0))) + 0.5
    bell = jnp.exp(v * v * -0.5)
    return v * cdf, cdf + v * (1.0 / math.sqrt(2.0 * math.pi)) * bell


def cmul(first, second):
    return (
        first[0] * second[0] - first[1] * second[1],
        first[0] * second[1] + first[1] * second[0],
    )


def turn_of(angle):
    part = angle * 0.25
    square = part * part
    sin = part * (1.0 + square * (-1 / 6 + square * (1 / 120 + square * (-1 / 5040 + square / 362880))))
    cos = 1.0 + square * (
        -0.5 + square * (1 / 24 + square * (-1 / 720 + square * (1 / 40320 - square / 3628800)))
    )
    for _ in range(2):
        cos, sin = 1.0 - 2.0 * sin * sin, 2.0 * sin * cos
    return cos, sin


def powers_of(decay, frequency, count):
    mag = jnp.exp(-decay)
    cos, sin = turn_of(frequency)
    powers = [(mag * cos, mag * sin)]
    for _ in range(count - 1):
        powers.append(cmul(powers[-1], powers[-1]))
    return powers


def kernel_gen_body(info_ref, par_ref, out_ref, low_re, low_im, total_ref):
    channels = par_ref.shape[3]
    width = 128 if channels % 128 == 0 else channels
    for lane in range(0, channels, width):
        lanes = pl.ds(lane, width)
        powers = powers_of(par_ref[0, 0, :, lanes], par_ref[0, 1, :, lanes], 9)
        current = (jnp.ones_like(powers[0][0]), jnp.zeros_like(powers[0][0]))
        for j in range(LOW):
            low_re[j, :, lanes] = current[0]
            low_im[j, :, lanes] = current[1]
            current = cmul(current, powers[0])
        second_half = info_ref[0] == 1
        start = (
            jnp.where(second_half, powers[8][0], 1.0),
            jnp.where(second_half, powers[8][1], 0.0),
        )

        def some_lags(i, highs, lanes=lanes, place=lane // width, step=powers[5]):
            for j in range(LOW):
                re, im = low_re[j, :, lanes], low_im[j, :, lanes]
                for half, high in enumerate(highs):
                    terms = high[0] * re - high[1] * im
                    row = pl.ds((2 * i + half) * LOW + j, 1)
                    total_ref[place, row, :] = jnp.sum(terms, axis=0, keepdims=True)
            return tuple(cmul(high, step) for high in highs)

        first = cmul((par_ref[0, 2, :, lanes], par_ref[0, 3, :, lanes]), start)
        lax.fori_loop(
            0, out_ref.shape[1] // (2 * LOW), some_lags, (first, cmul(first, powers[4]))
        )
    for place in range(channels // width):
        out_ref[0, :, place * width : (place + 1) * width] = total_ref[place].astype(BF16)


def kernel_gen(info, params):
    dirs, kinds, modes, channels = params.shape
    width = 128 if channels % 128 == 0 else channels
    lags = LENGTH // 2
    return pl.pallas_call(
        kernel_gen_body,
        out_shape=jax.ShapeDtypeStruct((dirs, lags, channels), BF16),
        grid_spec=pltpu.PrefetchScalarGridSpec(
            num_scalar_prefetch=1,
            grid=(dirs,),
            in_specs=[pl.BlockSpec((1, kinds, modes, channels), lambda k, info: (k, 0, 0, 0))],
            out_specs=pl.BlockSpec((1, lags, channels), lambda k, info: (k, 0, 0)),
            scratch_shapes=[
                pltpu.VMEM((LOW, modes, channels), F32),
                pltpu.VMEM((LOW, modes, channels), F32),
                pltpu.VMEM((channels // width, lags, width), F32),
            ],
        ),
        compiler_params=pltpu.CompilerParams(vmem_limit_bytes=VMEM),
        cost_estimate=cost(9),
        name="kernel_gen",
    )(info, params)


def pass_body(*refs):
    pass


def pass_after(value, after):
    return pl.pallas_call(
        pass_body,
        out_shape=jax.ShapeDtypeStruct(value.shape, value.dtype),
        in_specs=[ANY] * (1 + len(after)),
        out_specs=ANY,
        input_output_aliases={0: 0},
        cost_estimate=cost(1),
        name="pass_after",
    )(value, *after)


def stack_body(*refs, count, inner):
    for index, ref in enumerate(refs[:count]):
        if inner:
            refs[-1][:, index] = ref[...]
        else:
            refs[-1][index] = ref[...]


def stack_pieces(pieces, after, inner=False):
    shape = pieces[0].shape
    out = (len(pieces),) + shape
    if inner:
        out = shape[:1] + (len(pieces),) + shape[1:]
    result = pl.pallas_call(
        functools.partial(stack_body, count=len(pieces), inner=inner),
        out_shape=jax.ShapeDtypeStruct(out, pieces[0].dtype),
        grid=(1,),
        in_specs=[pl.BlockSpec(shape, lambda t: (0,) * len(shape))] * len(pieces)
        + [ANY] * len(after),
        out_specs=pl.BlockSpec(out, lambda t: (0,) * len(out)),
        cost_estimate=cost(3),
        name="stack_pieces",
    )(*pieces, *after)
    return result.reshape((-1,) + shape[1:]) if inner else result


def params_grad_body(info_ref, par_ref, mine_ref, other_ref, *rest):
    out_ref, low_re, low_im, up_ref = rest[-4:]
    parts, rows = mine_ref.shape[:2]
    half = parts * rows // 2
    first_is_mine = info_ref[0] == 0
    for index in range(parts // 2):
        place = (pl.program_id(0) * (parts // 2) + index) ^ (info_ref[3] >> 1)
        mine, other = mine_ref[place].astype(F32), other_ref[place].astype(F32)
        up_ref[pl.ds(index * rows, rows), :] = jnp.where(first_is_mine, mine, other)
        up_ref[pl.ds(half + index * rows, rows), :] = jnp.where(first_is_mine, other, mine)
    powers = powers_of(par_ref[0, 0], par_ref[0, 1], 5)
    one = (jnp.ones_like(powers[0][0]), jnp.zeros_like(powers[0][0]))
    current = one
    for j in range(LOW):
        low_re[j] = current[0]
        low_im[j] = current[1]
        current = cmul(current, powers[0])
    zero = jnp.zeros_like(one[0])

    def some_lags(i, carry):
        high, plain, ramped = carry
        for part in range(4):
            first = pl.multiple_of((4 * i + part) * LOW, LOW)
            grads = up_ref[pl.ds(first, LOW), :]
            sums, ramps = [zero] * 2, [zero] * 2
            for j in reversed(range(LOW)):
                sums[0] = sums[0] + grads[j : j + 1, :] * low_re[j]
                sums[1] = sums[1] + grads[j : j + 1, :] * low_im[j]
                if j:
                    ramps = [ramps[0] + sums[0], ramps[1] + sums[1]]
            start = first.astype(F32)
            lagged = (ramps[0] + start * sums[0], ramps[1] + start * sums[1])
            plain = tuple(a + b for a, b in zip(plain, cmul(high, sums)))
            ramped = tuple(a + b for a, b in zip(ramped, cmul(high, lagged)))
            high = cmul(high, powers[4])
        return high, plain, ramped

    carry = (one, (zero, zero), (zero, zero))
    _, plain, ramped = lax.fori_loop(0, up_ref.shape[0] // (4 * LOW), some_lags, carry)
    real, imag = par_ref[0, 2], par_ref[0, 3]
    out_ref[0, 0] = imag * ramped[1] - real * ramped[0]
    out_ref[0, 1] = -(real * ramped[1] + imag * ramped[0])
    out_ref[0, 2] = plain[0]
    out_ref[0, 3] = -plain[1]


def params_grad_of(info, params, mine, other, n_dp, after):
    dirs, kinds, modes, channels = params.shape
    own = modes // n_dp
    place = lambda k, info: (k, 0, info[3], 0)
    if own % 8:
        params = lax.dynamic_slice_in_dim(params, lax.axis_index("dp") * own, own, 2)
        place = lambda k, info: (k, 0, 0, 0)
    return pl.pallas_call(
        params_grad_body,
        out_shape=jax.ShapeDtypeStruct((dirs, kinds, own, channels), F32),
        grid_spec=pltpu.PrefetchScalarGridSpec(
            num_scalar_prefetch=1,
            grid=(dirs,),
            in_specs=[
                pl.BlockSpec((1, kinds, own, channels), place),
                pl.BlockSpec(mine.shape, lambda k, info: (0, 0, 0)),
                pl.BlockSpec(mine.shape, lambda k, info: (0, 0, 0)),
            ]
            + [ANY] * len(after),
            out_specs=pl.BlockSpec((1, kinds, own, channels), lambda k, info: (k, 0, 0, 0)),
            scratch_shapes=[pltpu.VMEM((LOW, own, channels), F32)] * 2
            + [pltpu.VMEM((LENGTH, channels), F32)],
        ),
        compiler_params=pltpu.CompilerParams(vmem_limit_bytes=VMEM),
        cost_estimate=cost(5),
        name="params_grad",
    )(info, params, mine, other, *after)


def norm_stats(rows):
    centered = rows - jnp.mean(rows, axis=1, keepdims=True)
    inv_std = lax.rsqrt(jnp.mean(centered * centered, axis=1, keepdims=True) + 1e-05)
    return centered * inv_std, inv_std


def in_body(tokens_ref, gain_ref, *refs):
    *weight_refs, normed_ref = refs[:4]
    out_refs = refs[4:]

    @pl.when(pl.program_id(0) == 0)
    def _():
        for start in range(0, tokens_ref.shape[0], BLOCK):
            rows = pl.ds(start, BLOCK)
            unit, _ = norm_stats(tokens_ref[rows, :].astype(F32))
            normed_ref[rows, :] = (unit * gain_ref[...]).astype(BF16)

    size = 2 * BLOCK
    for index, w_ref in enumerate(weight_refs):
        a_ref, s_ref = out_refs[2 * index : 2 * index + 2]
        for start in range(0, normed_ref.shape[0], size):
            rows = pl.ds(start, size)
            act, slope = gelu_pair(dot(normed_ref[rows, :], w_ref[...]))
            a_ref[rows, :] = act.astype(a_ref.dtype)
            s_ref[rows, :] = slope.astype(s_ref.dtype)


def in_proj(tokens, gain, forward_weight, backward_weight, value_weight):
    width, channels = forward_weight.shape
    hidden = value_weight.shape[1]
    rows = tokens.shape[0]
    steps = 6
    whole = lambda t: (0, 0)
    column = lambda t: (0, t)
    widths = [weight.shape[1] // steps for weight in (forward_weight, backward_weight, value_weight)]
    out_widths = [channels] * 4 + [hidden] * 2
    return pl.pallas_call(
        in_body,
        out_shape=[
            jax.ShapeDtypeStruct((rows, out_width), BF16) for out_width in [width] + out_widths
        ],
        grid=(steps,),
        in_specs=[pl.BlockSpec((rows, width), whole), pl.BlockSpec((1, width), whole)]
        + [pl.BlockSpec((width, tile), column) for tile in widths],
        out_specs=[pl.BlockSpec((rows, width), whole)]
        + [pl.BlockSpec((rows, out_width // steps), column) for out_width in out_widths],
        compiler_params=pltpu.CompilerParams(vmem_limit_bytes=VMEM),
        cost_estimate=cost(14),
        name="in_proj",
    )(tokens, gain.reshape(1, -1), forward_weight, backward_weight, value_weight)


def load_block(ref, section):
    return ref[pl.ds(section * BLOCK, BLOCK), :]


def store_block(ref, section, value):
    ref[pl.ds(section * BLOCK, BLOCK), :] = value.astype(ref.dtype)


def spectra(table_ref, blocks, out_ref):
    wide = jnp.concatenate(blocks, axis=1)
    out_ref[...] = dot(table_ref[...], jnp.concatenate([wide, wide], axis=0))


def split_store(high_ref, low_ref, rows, columns, value):
    high_ref[rows, columns] = value.astype(BF16)


def inverse(inverse_ref, high_ref, low_ref):
    return dot(inverse_ref[0], high_ref[...])


CHUNK = 16


def chunks(width):
    for start in range(0, FREQ, CHUNK):
        for lane in range(0, width, 128):
            parity = start // HALF_FREQ
            columns = [pl.ds(i * width + lane, 128) for i in range(SECTIONS)]
            yield parity, pl.ds(start, CHUNK), pl.ds(FREQ + start, CHUNK), columns


def load_spectra(ref, re_rows, im_rows, columns):
    return [(ref[re_rows, column], ref[im_rows, column]) for column in columns]


def turned(value, parity):
    return (-value[1], value[0]) if parity == 0 else (value[1], -value[0])


def cadd(first, second):
    return (first[0] + second[0], first[1] + second[1])


def band_spectra(parts, parity, longer):
    bands = [parts[0]]
    for m in range(1, SECTIONS):
        re, im = cadd(parts[m], turned(parts[m - 1], parity))
        bands.append((re * longer, im * longer))
    return bands


def cfma(total, first, second, conj):
    if conj:
        re = first[0] * second[0] + first[1] * second[1]
        im = first[0] * second[1] - first[1] * second[0]
    else:
        re = first[0] * second[0] - first[1] * second[1]
        im = first[0] * second[1] + first[1] * second[0]
    return (re, im) if total is None else (total[0] + re, total[1] + im)


def conv_spectra(bands, values, ahead):
    outs = []
    for i in range(SECTIONS):
        total = None
        for m in range(SECTIONS):
            source = i + m if ahead else i - m
            if 0 <= source < SECTIONS:
                total = cfma(total, bands[m], values[source], ahead)
        outs.append(total)
    return outs


def tile_pieces(info_ref, count):
    return [j ^ (info_ref[1] & (count - 1)) for j in range(count)]


def kernel_blocks(info_ref, mine_ref, other_ref, direction):
    first_is_mine = info_ref[0] == 0
    places = tile_pieces(info_ref, mine_ref.shape[0])
    mine = [mine_ref[place, direction] for place in places]
    other = [other_ref[place, direction] for place in places]
    mine = mine[0] if len(mine) == 1 else jnp.concatenate(mine, axis=1)
    other = other[0] if len(other) == 1 else jnp.concatenate(other, axis=1)
    halves = [jnp.where(first_is_mine, mine, other), jnp.where(first_is_mine, other, mine)]
    per = halves[0].shape[0] // BLOCK
    return [half[i * BLOCK : (i + 1) * BLOCK] for half in halves for i in range(per)]


def conv_fwd_body(
    info_ref, table_ref, inverse_ref, xf_ref, xb_ref, mine_ref, other_ref, *rest
):
    prod_ref, al_ref, ag_ref = rest[-11:-8]
    scratch = rest[-8:]
    longer = info_ref[2].astype(F32)
    width = xf_ref.shape[1]
    for direction, (x_ref, out_ref) in enumerate(((xf_ref, al_ref), (xb_ref, ag_ref))):
        x_spec, k_spec, y_high, y_low = scratch[4 * direction : 4 * direction + 4]
        blocks = [load_block(x_ref, i) for i in range(SECTIONS)]
        spectra(table_ref, blocks, x_spec)
        spectra(table_ref, kernel_blocks(info_ref, mine_ref, other_ref, direction), k_spec)
        for parity, re_rows, im_rows, columns in chunks(width):
            bands = band_spectra(load_spectra(k_spec, re_rows, im_rows, columns), parity, longer)
            values = load_spectra(x_spec, re_rows, im_rows, columns)
            for column, (re, im) in zip(columns, conv_spectra(bands, values, direction == 1)):
                split_store(y_high, y_low, re_rows, column, re)
                split_store(y_high, y_low, im_rows, column, im)
        result = inverse(inverse_ref, y_high, y_low)
        for i in range(SECTIONS):
            place = slice(i * width, (i + 1) * width)
            store_block(out_ref, i, result[:, place])
            if direction == 0:
                x_spec[:BLOCK, place] = result[:, place]
            else:
                store_block(prod_ref, i, scratch[0][:BLOCK, place] * result[:, place])


def kernel_spec(own, count):
    shift = count.bit_length() - 1
    return pl.BlockSpec(
        (count, 2, LENGTH // 2, own), lambda c, info: (c ^ (info[1] >> shift), 0, 0, 0)
    )


def tile_of(own):
    count = 1
    while (count * own) % 128:
        count *= 2
    return count, count * own


def conv_fwd(info, tables, act_forward, act_backward, mine, other, after):
    rows, channels = act_forward.shape
    count, width = tile_of(mine.shape[3])
    whole = lambda c, info: (0, 0)
    whole3 = lambda c, info: (0, 0, 0)
    column = lambda c, info: (0, c)
    forward, back = tables
    wide = SECTIONS * width
    return pl.pallas_call(
        conv_fwd_body,
        out_shape=[
            jax.ShapeDtypeStruct((rows, channels), BF16),
            jax.ShapeDtypeStruct((rows, channels), BF16),
            jax.ShapeDtypeStruct((rows, channels), BF16),
        ],
        grid_spec=pltpu.PrefetchScalarGridSpec(
            num_scalar_prefetch=1,
            grid=(channels // width,),
            in_specs=[
                pl.BlockSpec(forward.shape, whole),
                pl.BlockSpec(back.shape, whole3),
                pl.BlockSpec((rows, width), column),
                pl.BlockSpec((rows, width), column),
                kernel_spec(mine.shape[3], count),
                kernel_spec(mine.shape[3], count),
            ]
            + [ANY] * len(after),
            out_specs=[pl.BlockSpec((rows, width), column)] * 3,
            scratch_shapes=[
                pltpu.VMEM((2 * FREQ, wide), F32),
                pltpu.VMEM((2 * FREQ, wide), F32),
                pltpu.VMEM((2 * FREQ, wide), BF16),
                pltpu.VMEM((2 * FREQ, wide), BF16),
            ]
            * 2,
        ),
        compiler_params=pltpu.CompilerParams(vmem_limit_bytes=VMEM),
        cost_estimate=cost(17),
        name="conv_fwd",
    )(info, forward, back, act_forward, act_backward, mine, other, *after)


def conv_bwd_body(
    info_ref, table_ref, inverse_ref, gp_ref, al_ref, ag_ref, xf_ref, xb_ref, sf_ref, sb_ref,
    mine_ref, other_ref, *rest,
):
    gf_ref, gb_ref, keep_ref, send_ref = rest[-18:-14]
    scratch = rest[-14:]
    longer = info_ref[2].astype(F32)
    width = xf_ref.shape[1]
    ways = ((xf_ref, ag_ref, sf_ref, gf_ref), (xb_ref, al_ref, sb_ref, gb_ref))
    for direction, (x_ref, other_way, slope_ref, out_ref) in enumerate(ways):
        x_spec, k_spec, g_spec, y_high, y_low, h_high, h_low = scratch[7 * direction : 7 * direction + 7]
        upstream = [
            (
                load_block(gp_ref, i).astype(F32)
                * load_block(other_way, i).astype(F32)
            ).astype(BF16)
            for i in range(SECTIONS)
        ]
        spectra(table_ref, upstream, g_spec)
        spectra(table_ref, kernel_blocks(info_ref, mine_ref, other_ref, direction), k_spec)
        spectra(table_ref, [load_block(x_ref, i) for i in range(SECTIONS)], x_spec)
        for parity, re_rows, im_rows, columns in chunks(width):
            grads = load_spectra(g_spec, re_rows, im_rows, columns)
            bands = band_spectra(load_spectra(k_spec, re_rows, im_rows, columns), parity, longer)
            for column, (re, im) in zip(columns, conv_spectra(bands, grads, direction == 0)):
                split_store(y_high, y_low, re_rows, column, re)
                split_store(y_high, y_low, im_rows, column, im)
            values = load_spectra(x_spec, re_rows, im_rows, columns)
            above = None
            for m in reversed(range(SECTIONS)):
                total = None
                for i in range(m, SECTIONS):
                    if direction == 0:
                        total = cfma(total, values[i - m], grads[i], True)
                    else:
                        total = cfma(total, grads[i - m], values[i], True)
                if m:
                    total = (total[0] * longer, total[1] * longer)
                folded = total
                if above is not None:
                    folded = cadd(total, turned(above, 1 - parity))
                split_store(h_high, h_low, re_rows, columns[m], folded[0])
                split_store(h_high, h_low, im_rows, columns[m], folded[1])
                above = total
        result = inverse(inverse_ref, y_high, y_low)
        for i in range(SECTIONS):
            grad_act = result[:, i * width : (i + 1) * width].astype(BF16).astype(F32)
            slope = load_block(slope_ref, i).astype(F32)
            store_block(out_ref, i, grad_act * slope)
        result = inverse(inverse_ref, h_high, h_low).astype(BF16)
        first_is_mine = info_ref[0] == 0
        own, per = keep_ref.shape[3], keep_ref.shape[2]
        half = SECTIONS // 2
        for piece in range(keep_ref.shape[1]):
            for i in range(half):
                low = result[:, i * width + piece * own : i * width + (piece + 1) * own]
                top = (half + i) * width
                high = result[:, top + piece * own : top + (piece + 1) * own]
                for start in range(0, BLOCK, per):
                    place = ((direction * half + i) * BLOCK + start) // per
                    first, second = low[start : start + per], high[start : start + per]
                    keep_ref[place, piece] = jnp.where(first_is_mine, first, second)
                    send_ref[place, piece] = jnp.where(first_is_mine, second, first)


def conv_bwd(
    info, tables, grad_product, along, against, act_f, act_b, slope_f, slope_b, mine, other, parts,
    after,
):
    rows, channels = act_f.shape
    own = mine.shape[3]
    count, width = tile_of(own)
    whole = lambda c, info: (0, 0)
    whole3 = lambda c, info: (0, 0, 0)
    column = lambda c, info: (0, c)
    forward, back = tables
    wide = SECTIONS * width
    return pl.pallas_call(
        conv_bwd_body,
        out_shape=[
            jax.ShapeDtypeStruct((rows, channels), BF16),
            jax.ShapeDtypeStruct((rows, channels), BF16),
            jax.ShapeDtypeStruct((parts, mine.shape[0], LENGTH // parts, own), BF16),
            jax.ShapeDtypeStruct((parts, mine.shape[0], LENGTH // parts, own), BF16),
        ],
        grid_spec=pltpu.PrefetchScalarGridSpec(
            num_scalar_prefetch=1,
            grid=(channels // width,),
            in_specs=[
                pl.BlockSpec(forward.shape, whole),
                pl.BlockSpec(back.shape, whole3),
            ]
            + [pl.BlockSpec((rows, width), column)] * 7
            + [kernel_spec(own, count)] * 2
            + [ANY] * len(after),
            out_specs=[
                pl.BlockSpec((rows, width), column),
                pl.BlockSpec((rows, width), column),
                pl.BlockSpec((parts, count, LENGTH // parts, own), lambda c, info: (0, c, 0, 0)),
                pl.BlockSpec((parts, count, LENGTH // parts, own), lambda c, info: (0, c, 0, 0)),
            ],
            scratch_shapes=(
                [pltpu.VMEM((2 * FREQ, wide), F32)] * 3 + [pltpu.VMEM((2 * FREQ, wide), BF16)] * 4
            )
            * 2,
        ),
        compiler_params=pltpu.CompilerParams(vmem_limit_bytes=VMEM),
        cost_estimate=cost(28),
        name="conv_bwd",
    )(
        info, forward, back, grad_product, along, against, act_f, act_b, slope_f, slope_b,
        mine, other, *after,
    )


def packed_rows(total_ref, core, n_dp, n_seq, small, out_ref):
    size = total_ref.shape[0] // n_dp
    per = size // n_seq
    groups = n_dp // 2
    count = n_seq * small
    for group in range(groups):
        for place, which in enumerate((1 - core, core)):
            start = pl.multiple_of((2 * group + which) * size, 8)
            value = total_ref[pl.ds(start, size), :]
            for fold in range(per // small):
                first = fold * small
                rows = [value[s * per + first : s * per + first + small] for s in range(n_seq)]
                target = ((place * (per // small) + fold) * groups + group) * count
                out_ref[pl.ds(target, count), :] = jnp.concatenate(rows, axis=0).astype(out_ref.dtype)


def store_split(result, groups, folds, send_ref, keep_ref, offset):
    count = send_ref.shape[1]
    width = result.shape[1]
    for place, ref in enumerate((send_ref, keep_ref)):
        for fold in range(folds):
            for group in range(groups):
                first = ((place * folds + fold) * groups + group) * count
                columns = pl.ds(offset + fold * width, width)
                ref[group, :, columns] = result[first : first + count].astype(BF16)


def middle_body(
    info_ref, prod_ref, normed_ref, cot_ref, uw_ref, ow_ref, va_ref, vs_ref, *rest, n_dp, n_seq, small
):
    send_ref, keep_ref, og_ref, gated_ref, dv_ref, gp_ref, nt_ref = rest[:7]
    du_ref, pt_ref, flipped, gp_acc = rest[7:]
    step = pl.program_id(0)

    @pl.when(step == 0)
    def _():
        for source, target in ((prod_ref, pt_ref), (normed_ref, nt_ref)):
            rows = flipped.at[pl.ds(0, source.shape[1])]
            rows[...] = source[...].astype(F32).T
            packed_rows(rows, info_ref[0], n_dp, n_seq, small, target)
        gp_acc[...] = jnp.zeros_like(gp_acc)

    size = 2 * BLOCK
    for start in range(0, prod_ref.shape[0], size):
        rows = pl.ds(start, size)
        update_act, update_slope = gelu_pair(dot(prod_ref[rows, :], uw_ref[...]))
        grad_gated = dot_rt(cot_ref[rows, :], ow_ref[...])
        value_act = va_ref[rows, :].astype(F32)
        gated_ref[rows, :] = (update_act * value_act).astype(BF16)
        du_ref[rows, :] = (grad_gated * value_act * update_slope).astype(BF16)
        dv_ref[rows, :] = (grad_gated * update_act * vs_ref[rows, :].astype(F32)).astype(BF16)
    folds = prod_ref.shape[1] // normed_ref.shape[1]
    tile = uw_ref.shape[1]
    groups = n_dp // 2
    store_split(dot(pt_ref[...], du_ref[...]), groups, folds, send_ref, keep_ref, 0)
    store_split(dot(nt_ref[...], dv_ref[...]), groups, 1, send_ref, keep_ref, folds * tile)
    og_ref[...] = dot_lt(gated_ref[...], cot_ref[...]).astype(BF16)
    gp_acc[...] += dot_rt(du_ref[...], uw_ref[...])

    @pl.when(step == pl.num_programs(0) - 1)
    def _():
        gp_ref[...] = gp_acc[...].astype(BF16)


def middle(
    info, product, normed, cot, update_weight, output_weight, value_act, value_slope, n_dp, n_seq
):
    rows, channels = product.shape
    hidden, width = output_weight.shape
    tile = HIDDEN_TILE
    steps = hidden // tile
    small = width // (n_dp * n_seq)
    groups = n_dp // 2
    block = (channels // width + 1) * tile
    whole = lambda t, info: (0, 0)
    column = lambda t, info: (0, t)
    out_block = pl.BlockSpec((groups, n_seq * small, block), lambda t, info: (0, 0, t))
    return pl.pallas_call(
        functools.partial(middle_body, n_dp=n_dp, n_seq=n_seq, small=small),
        out_shape=[jax.ShapeDtypeStruct((groups, n_seq * small, steps * block), BF16)] * 2
        + [
            jax.ShapeDtypeStruct((hidden, width), BF16),
            jax.ShapeDtypeStruct((rows, hidden), BF16),
            jax.ShapeDtypeStruct((rows, hidden), BF16),
            jax.ShapeDtypeStruct((rows, channels), BF16),
            jax.ShapeDtypeStruct((width, rows), BF16),
        ],
        grid_spec=pltpu.PrefetchScalarGridSpec(
            num_scalar_prefetch=1,
            grid=(steps,),
            in_specs=[
                pl.BlockSpec((rows, channels), whole),
                pl.BlockSpec((rows, width), whole),
                pl.BlockSpec((rows, width), whole),
                pl.BlockSpec((channels, tile), column),
                pl.BlockSpec((tile, width), lambda t, info: (t, 0)),
                pl.BlockSpec((rows, tile), column),
                pl.BlockSpec((rows, tile), column),
            ],
            out_specs=[
                out_block,
                out_block,
                pl.BlockSpec((tile, width), lambda t, info: (t, 0)),
                pl.BlockSpec((rows, tile), column),
                pl.BlockSpec((rows, tile), column),
                pl.BlockSpec((rows, channels), whole),
                pl.BlockSpec((width, rows), whole),
            ],
            scratch_shapes=[
                pltpu.VMEM((rows, tile), BF16),
                pltpu.VMEM((channels, rows), BF16),
                pltpu.VMEM((channels, rows), F32),
                pltpu.VMEM((rows, channels), F32),
            ],
        ),
        compiler_params=pltpu.CompilerParams(vmem_limit_bytes=VMEM),
        cost_estimate=cost(40),
        name="middle",
    )(info, product, normed, cot, update_weight, output_weight, value_act, value_slope)


def layer_body(gated_ref, dv_ref, ow_ref, vw_ref, tokens_ref, *rest):
    layer_ref, gv_ref, lo_acc = rest[-3:]
    step = pl.program_id(0)

    @pl.when(step == 0)
    def _():
        lo_acc[...] = jnp.zeros_like(lo_acc)
        gv_ref[...] = jnp.zeros_like(gv_ref)

    lo_acc[...] += dot(gated_ref[...], ow_ref[...])
    gv_ref[...] += dot_rt(dv_ref[...], vw_ref[...])

    @pl.when(step == pl.num_programs(0) - 1)
    def _():
        layer_ref[...] = (tokens_ref[...].astype(F32) + lo_acc[...]).astype(BF16)


def layer_rows_of(gated, grad_value_in, output_weight, value_weight, tokens, after):
    rows, hidden = gated.shape
    width = output_weight.shape[1]
    tile = 1024
    whole = lambda t: (0, 0)
    column = lambda t: (0, t)
    return pl.pallas_call(
        layer_body,
        out_shape=[
            jax.ShapeDtypeStruct((rows, width), BF16),
            jax.ShapeDtypeStruct((rows, width), F32),
        ],
        grid=(hidden // tile,),
        in_specs=[
            pl.BlockSpec((rows, tile), column),
            pl.BlockSpec((rows, tile), column),
            pl.BlockSpec((tile, width), lambda t: (t, 0)),
            pl.BlockSpec((width, tile), column),
            pl.BlockSpec((rows, width), whole),
        ]
        + [ANY] * len(after),
        out_specs=[pl.BlockSpec((rows, width), whole)] * 2,
        scratch_shapes=[pltpu.VMEM((rows, width), F32)],
        compiler_params=pltpu.CompilerParams(vmem_limit_bytes=VMEM),
        cost_estimate=cost(9),
        name="layer_rows",
    )(gated, grad_value_in, output_weight, value_weight, tokens, *after)


def inner_grad_body(nt_ref, df_ref, db_ref, *rest, groups):
    send_ref, keep_ref = rest[-2:]
    tile = df_ref.shape[1]
    store_split(dot(nt_ref[...], df_ref[...]), groups, 1, send_ref, keep_ref, 0)
    store_split(dot(nt_ref[...], db_ref[...]), groups, 1, send_ref, keep_ref, tile)


def inner_weight_grad(normed_t, grad_f, grad_b, n_dp, n_seq, after):
    width, rows = normed_t.shape
    channels = grad_f.shape[1]
    small = width // (n_dp * n_seq)
    groups = n_dp // 2
    column = lambda t: (0, t)
    out_block = pl.BlockSpec((groups, n_seq * small, 2 * INNER), lambda t: (0, 0, t))
    return pl.pallas_call(
        functools.partial(inner_grad_body, groups=groups),
        out_shape=[jax.ShapeDtypeStruct((groups, n_seq * small, 2 * channels), BF16)] * 2,
        grid=(channels // INNER,),
        in_specs=[
            pl.BlockSpec((width, rows), lambda t: (0, 0)),
            pl.BlockSpec((rows, INNER), column),
            pl.BlockSpec((rows, INNER), column),
        ]
        + [ANY] * len(after),
        out_specs=[out_block, out_block],
        compiler_params=pltpu.CompilerParams(vmem_limit_bytes=VMEM),
        cost_estimate=cost(6),
        name="inner_weight_grad",
    )(normed_t, grad_f, grad_b, *after)


def out_body(
    tokens_ref, cot_ref, gain_ref, gv_ref, layer_ref, df_ref, db_ref, fw_ref, bw_ref, *rest
):
    out_ref, total = rest[-2:]
    step = pl.program_id(0)

    @pl.when(step == 0)
    def _():
        total[...] = gv_ref[...]

    total[...] += dot_rt(df_ref[...], fw_ref[...]) + dot_rt(db_ref[...], bw_ref[...])

    @pl.when(step == pl.num_programs(0) - 1)
    def _():
        size = out_ref.shape[2]
        for index in range(out_ref.shape[0]):
            rows = pl.ds(index * size, size)
            unit, inv_std = norm_stats(tokens_ref[rows, :].astype(F32))
            grad_unit = total[rows, :] * gain_ref[...]
            grad_input = inv_std * (
                grad_unit
                - jnp.mean(grad_unit, axis=1, keepdims=True)
                - unit * jnp.mean(grad_unit * unit, axis=1, keepdims=True)
            )
            out_ref[index, 0] = layer_ref[rows, :]
            out_ref[index, 1] = (cot_ref[rows, :].astype(F32) + grad_input).astype(BF16)


def out_proj(
    tokens, cot, gain, grad_value_part, layer_rows, grad_f, grad_b, forward_weight, backward_weight,
    n_seq, after,
):
    rows, channels = grad_f.shape
    width = tokens.shape[1]
    tile = INNER
    whole = lambda t: (0, 0)
    column = lambda t: (0, t)
    shape = (n_seq, 2, rows // n_seq, width)
    return pl.pallas_call(
        out_body,
        out_shape=jax.ShapeDtypeStruct(shape, BF16),
        grid=(channels // tile,),
        in_specs=[
            pl.BlockSpec((rows, width), whole),
            pl.BlockSpec((rows, width), whole),
            pl.BlockSpec((1, width), whole),
            pl.BlockSpec((rows, width), whole),
            pl.BlockSpec((rows, width), whole),
            pl.BlockSpec((rows, tile), column),
            pl.BlockSpec((rows, tile), column),
            pl.BlockSpec((width, tile), column),
            pl.BlockSpec((width, tile), column),
        ]
        + [ANY] * len(after),
        out_specs=pl.BlockSpec(shape, lambda t: (0, 0, 0, 0)),
        scratch_shapes=[pltpu.VMEM((rows, width), F32)],
        compiler_params=pltpu.CompilerParams(vmem_limit_bytes=VMEM),
        cost_estimate=cost(10),
        name="out_proj",
    )(
        tokens, cot, gain.reshape(1, -1), grad_value_part, layer_rows, grad_f, grad_b,
        forward_weight, backward_weight, *after,
    )


def swap(value, axis, mask):
    return lax.ppermute(value, axis, [(i, i ^ mask) for i in range(lax.axis_size(axis))])


def total_of(pieces):
    total = pieces[0].astype(F32)
    for piece in pieces[1:]:
        total = total + piece.astype(F32)
    return total


def with_bit(index, place, bit):
    low = index & ((1 << place) - 1)
    return ((index >> place) << (place + 1)) | (bit << place) | low


SLOT = {"dp": 3, "seq": 1}


def grid_place(step, grid):
    if grid[0] * grid[1] == 1:
        return [0, 0]
    step = jnp.minimum(step, grid[0] * grid[1] - 1)
    if grid[1] == 1:
        return [step, 0]
    return [step // grid[1], step % grid[1]] if grid[0] > 1 else [0, step]


class Scatter:

    def __init__(self, info, pieces, shape, order):
        self.info, self.shape, self.order = info, shape, list(order)
        self.pieces = list(pieces)
        self.stages = []

    def place(self, axis, bit):
        dim, place = (0, bit - 1) if axis == "dp" else (1, bit)
        lower = [b for a, b, _, _ in self.stages if a == axis and b < bit]
        return dim, place - len(lower)

    def index_map(self, level, column, last, grid):
        stages = self.stages[level:]

        def found(step, info):
            coords = grid_place(step, grid)
            if last is not None:
                axis, bit, dim, place = last
                coords[dim] = with_bit(coords[dim], place, 1 - ((info[SLOT[axis]] >> bit) & 1))
            for axis, bit, dim, place in reversed(stages):
                coords[dim] = with_bit(coords[dim], place, (info[SLOT[axis]] >> bit) & 1)
            return (coords[0], coords[1], 0, column)

        return found

    def sizes(self, stages):
        sizes = list(self.shape[:2])
        for _, _, dim, _ in stages:
            sizes[dim] //= 2
        return sizes

    def specs(self, last):
        stages = self.stages + ([last] if last else [])
        touched = {stage[2] for stage in stages}
        sizes = self.sizes(stages)
        lead = [1 if dim in touched else self.shape[dim] for dim in range(2)]
        grid = [sizes[dim] // lead[dim] for dim in range(2)]
        block = tuple(lead) + self.shape[2:]
        specs = [
            pl.BlockSpec(block, self.index_map(level, column, last, grid))
            for level, column, _ in self.pieces
        ]
        return block, grid, specs

    def next_stage(self):
        axis, bit = self.order[0]
        return (axis, bit) + self.place(axis, bit)


def add_body(info_ref, *refs, layout, first_out):
    refs = list(refs)
    out_refs = refs[first_out:]
    for count, out, column in layout:
        total = total_of([refs.pop(0)[...] for _ in range(count)]).astype(BF16)
        width = total.shape[3]
        out_refs[out][:, :, :, column * width : (column + 1) * width] = total


def step_apart(groups, after=(), passed=()):
    arrays, in_specs, out_specs, out_shape, layout, steps = [], [], [], [], [], 1
    for group in groups:
        merged = len({scatter.order[0] for scatter in group}) == 1
        for index, scatter in enumerate(group):
            stage = scatter.next_stage()
            block, grid, specs = scatter.specs(stage)
            sizes = scatter.sizes(scatter.stages + [stage])
            arrays += [piece for _, _, piece in scatter.pieces]
            in_specs += specs
            steps = max(steps, grid[0] * grid[1])
            width = scatter.shape[3]

            def out_map(step, info, grid=grid):
                return (*grid_place(step, grid), 0, 0)

            layout.append((len(specs), len(out_shape) - (1 if merged and index else 0), index if merged else 0))
            if merged and index:
                continue
            wide = width * len(group) if merged else width
            out_shape.append(jax.ShapeDtypeStruct(tuple(sizes) + (scatter.shape[2], wide), BF16))
            out_specs.append(pl.BlockSpec(block[:3] + (wide,), out_map))
    sums = len(out_shape)
    first_passed = 1 + len(arrays) + len(after)
    out_shape += [jax.ShapeDtypeStruct(value.shape, value.dtype) for value in passed]
    sent = pl.pallas_call(
        functools.partial(add_body, layout=tuple(layout), first_out=len(arrays) + len(after) + len(passed)),
        out_shape=out_shape,
        grid_spec=pltpu.PrefetchScalarGridSpec(
            num_scalar_prefetch=1,
            grid=(steps,),
            in_specs=in_specs + [ANY] * (len(after) + len(passed)),
            out_specs=out_specs + [ANY] * len(passed),
        ),
        input_output_aliases={first_passed + i: sums + i for i in range(len(passed))},
        compiler_params=pltpu.CompilerParams(vmem_limit_bytes=FULL_VMEM),
        cost_estimate=cost(3),
        name="add_sent",
    )(groups[0][0].info, *arrays, *after, *passed)
    arrived = {}
    for scatter, (_, out, column) in zip([s for group in groups for s in group], layout):
        axis, bit = scatter.order[0]
        if out not in arrived:
            arrived[out] = swap(sent[out], axis, 1 << bit)
        scatter.stages.append(scatter.next_stage())
        scatter.order.pop(0)
        scatter.pieces.append((len(scatter.stages), column, arrived[out]))
    return [sent[0], *sent[sums:]] if passed else sent[0]


def partner_body(info_ref, *refs, count, partners):
    outs = refs[-partners:]
    for index, out_ref in enumerate(outs):
        out_ref[...] = total_of([ref[0, 0] for ref in refs[index * count : (index + 1) * count]]).astype(BF16)


def sums_for_partners(scatter, partners, after):
    specs = []
    for mask in range(partners):
        for level, column, _ in scatter.pieces:
            whole = scatter.index_map(level, column, None, [1, 1])

            def found(step, info, whole=whole, mask=mask):
                place = whole(step, info)
                return (place[0], info[SLOT["seq"]] ^ mask, 0, 0)

            specs.append(pl.BlockSpec((1, 1) + scatter.shape[2:], found))
    count = len(scatter.pieces)
    shape = scatter.shape[2:]
    return pl.pallas_call(
        functools.partial(partner_body, count=count, partners=partners),
        out_shape=[jax.ShapeDtypeStruct(shape, BF16)] * partners,
        grid_spec=pltpu.PrefetchScalarGridSpec(
            num_scalar_prefetch=1,
            grid=(1,),
            in_specs=specs + [ANY] * len(after),
            out_specs=[pl.BlockSpec(shape, lambda t, info: (0, 0))] * partners,
        ),
        compiler_params=pltpu.CompilerParams(vmem_limit_bytes=VMEM),
        cost_estimate=cost(3),
        name="partner_sums",
    )(scatter.info, *[piece for _, _, piece in scatter.pieces] * partners, *after)


def sum_body(*refs, count):
    refs[-1][0] = total_of([ref[...] for ref in refs[:count]]).astype(BF16)


def sum_of(pieces, after):
    shape = pieces[0].shape
    return pl.pallas_call(
        functools.partial(sum_body, count=len(pieces)),
        out_shape=jax.ShapeDtypeStruct((1,) + shape, BF16),
        grid=(1,),
        in_specs=[pl.BlockSpec(shape, lambda t: (0, 0))] * len(pieces) + [ANY] * len(after),
        out_specs=pl.BlockSpec((1,) + shape, lambda t: (0, 0, 0)),
        cost_estimate=cost(3),
        name="sum_of",
    )(*pieces, *after)


def finish(scatters, out_shape, write, after, name):
    arrays, specs, counts = [], [], []
    for scatter in scatters:
        own = scatter.specs(None)[2]
        specs += own
        arrays += [piece for _, _, piece in scatter.pieces]
        counts.append(len(own))

    def body(info_ref, *refs):
        refs = list(refs)
        sums = [total_of([refs.pop(0)[0, 0] for _ in range(count)]) for count in counts]
        write(sums, *refs[len(after) :])

    return pl.pallas_call(
        body,
        out_shape=out_shape,
        grid_spec=pltpu.PrefetchScalarGridSpec(
            num_scalar_prefetch=1,
            grid=(1,),
            in_specs=specs + [ANY] * len(after),
            out_specs=[
                pl.BlockSpec(shape.shape, lambda t, info: (0, 0)) for shape in out_shape
            ],
        ),
        compiler_params=pltpu.CompilerParams(vmem_limit_bytes=VMEM),
        cost_estimate=cost(3),
        name=name,
    )(scatters[0].info, *arrays, *after)


def to_row(value):
    moved = lax.all_to_all(value, "seq", split_axis=0, concat_axis=0, tiled=True)
    return moved.reshape(-1, value.shape[2])


def on_device(
    tokens,
    doc_ids,
    norm_gain,
    value_weight,
    forward_weight,
    backward_weight,
    update_weight,
    output_weight,
    kernel_params,
    cotangent,
):
    n_dp, n_seq = lax.axis_size("dp"), lax.axis_size("seq")
    dp_index, seq_index = lax.axis_index("dp"), lax.axis_index("seq")
    channels = forward_weight.shape[1]
    own_channels = kernel_params.shape[3]
    core = dp_index % 2
    docs = lax.dynamic_index_in_dim(doc_ids, seq_index, 0, keepdims=False)
    longer = (docs[0] == docs[-1]).astype(jnp.int32)
    info = jnp.stack([core, seq_index, longer, dp_index]).astype(jnp.int32)
    tables = fourier_tables()

    row_tokens = to_row(tokens)
    half = pass_after(kernel_gen(info, kernel_params), [row_tokens])
    halves = [half if mask == 0 else swap(half, "seq", mask) for mask in range(n_seq)]
    normed, act_f, slope_f, act_b, slope_b, value_act, value_slope = in_proj(
        row_tokens, norm_gain, forward_weight, backward_weight, value_weight
    )
    mine = stack_pieces(halves, [value_act])
    other = swap(mine, "dp", 1)
    cot = to_row(cotangent)
    product, along, against = conv_fwd(info, tables, act_f, act_b, mine, other, [])

    seq_bits = [("seq", bit) for bit in range(n_seq.bit_length() - 1)]
    dp_bits = [("dp", bit) for bit in range(1, n_dp.bit_length() - 1)]
    shape = (n_dp // 2, n_seq, tokens.shape[2] // (n_dp * n_seq))

    def scatter_of(send, keep, order, columns=None):
        width = send.shape[2] // (columns or 1)
        whole = shape + (send.shape[2],)
        arrays = [keep.reshape(whole), swap(send, "dp", 1).reshape(whole)]
        return [
            Scatter(info, [(0, column, array) for array in arrays], shape + (width,), order[column])
            for column in range(columns or 1)
        ]

    send, keep, output_part, gated, grad_value_in, grad_product, normed_t = middle(
        info, product, normed, cot, update_weight, output_weight, value_act, value_slope, n_dp, n_seq
    )
    output_sum = lax.psum_scatter(output_part, "dp", scatter_dimension=0, tiled=True)
    layer_rows, grad_value_part = layer_rows_of(
        gated, grad_value_in, output_weight, value_weight, row_tokens, []
    )
    both = scatter_of(send, keep, [seq_bits + dp_bits, seq_bits[::-1] + dp_bits], 2)
    sent = step_apart([both[:1], both[1:]], [layer_rows])
    parts = n_dp // 2
    grad_f, grad_b, kernel_keep, kernel_send = conv_bwd(
        info, tables, grad_product, along, against, act_f, act_b, slope_f, slope_b, mine, other,
        parts, [sent],
    )
    send, keep = inner_weight_grad(normed_t, grad_f, grad_b, n_dp, n_seq, [])

    sent, send, kernel_send = step_apart([both[:1], both[1:]], [], [send, kernel_send])
    inner = scatter_of(send, keep, [seq_bits + dp_bits, seq_bits[::-1] + dp_bits], 2)
    blocks = kernel_keep.shape
    kernel = [
        Scatter(
            info,
            [(0, 0, kernel_keep), (0, 0, swap(kernel_send, "dp", 1))],
            blocks,
            dp_bits,
        )
    ]
    for _ in range(n_seq.bit_length() - 3):
        sent = step_apart([both[:1], both[1:]], [sent])
    sent = step_apart([inner[:1], inner[1:], kernel], [sent])
    out_pieces = out_proj(
        row_tokens, cot, norm_gain, grad_value_part, layer_rows, grad_f, grad_b,
        forward_weight, backward_weight, n_seq, [sent],
    )
    sent = step_apart([both, kernel], [sent, out_pieces])
    while kernel[0].order:
        sent = step_apart([kernel], [sent])
    output_blocks = (1, n_seq, output_sum.shape[0] // n_seq, output_sum.shape[1])
    output = [Scatter(info, [(0, 0, output_sum.reshape(output_blocks))], output_blocks, seq_bits[::-1])]
    for _ in range(n_seq.bit_length() - 2):
        sent = step_apart([inner[:1], inner[1:], output], [sent])
    halves = sums_for_partners(kernel[0], n_seq, [sent])
    halves = [half if mask == 0 else swap(half, "seq", mask) for mask, half in enumerate(halves)]
    sent = step_apart([inner, output], [halves[0]])
    while both[0].order:
        sent = step_apart([both], [sent])
    part = sum_of(halves, [sent])
    parts = [part if mask == 0 else swap(part, "dp", mask << 1) for mask in range(n_dp // 2)]
    while inner[0].order:
        sent = step_apart([inner], [part])
    width = tokens.shape[2]
    small = width // (n_dp * n_seq)
    hidden = update_weight.shape[1]
    folds = channels // width
    tile = HIDDEN_TILE

    def write_first(sums, update_ref, value_ref, output_ref):
        column = 0
        output_ref[...] = sums[-1]
        for total in sums[:-1]:
            for start in range(0, total.shape[1], (folds + 1) * tile):
                columns = pl.ds(column, tile)
                for fold in range(folds):
                    part = total[:, start + fold * tile : start + (fold + 1) * tile]
                    update_ref[pl.ds(fold * small, small), columns] = part
                value_ref[:, columns] = total[:, start + folds * tile : start + (folds + 1) * tile]
                column += tile

    def write_inner(sums, forward_ref, backward_ref):
        for index, total in enumerate(sums):
            columns = pl.ds(index * INNER, INNER)
            forward_ref[:, columns] = total[:, :INNER]
            backward_ref[:, columns] = total[:, INNER : 2 * INNER]

    shape_of = lambda *shape: jax.ShapeDtypeStruct(shape, F32)
    first_shapes = [shape_of(folds * small, hidden), shape_of(small, hidden), shape_of(*output_blocks[2:])]
    update_grad, value_grad, output_grad = finish(
        both + output, first_shapes, write_first, [sent], "first_sums"
    )
    gathered = stack_pieces(parts, [update_grad]).reshape((-1,) + part.shape[1:])
    others = swap(gathered, "dp", 1)
    moved = lax.all_to_all(out_pieces, "seq", split_axis=0, concat_axis=0, tiled=True)

    forward_grad, backward_grad = finish(
        inner, [shape_of(small, channels)] * 2, write_inner, [gathered], "inner_sums"
    )
    params_grad = params_grad_of(info, kernel_params, gathered, others, n_dp, [forward_grad])

    layer_out, tokens_grad = moved[:, 0], moved[:, 1]

    own_rows = lambda value: lax.dynamic_slice_in_dim(value, (dp_index * n_seq + seq_index) * small, small, 0)
    gain_sums = sum(
        jnp.sum(own_rows(weight).astype(F32) * grad, axis=1)
        for weight, grad in (
            (value_weight, value_grad), (forward_weight, forward_grad), (backward_weight, backward_grad)
        )
    )
    gain_grad = gain_sums / own_rows(norm_gain)
    return (
        layer_out,
        tokens_grad,
        gain_grad,
        value_grad,
        forward_grad,
        backward_grad,
        update_grad,
        output_grad,
        params_grad,
    )


def solution(mesh):
    placed = (
        P("dp", "seq", None),
        P("dp", None),
        P(),
        P(),
        P(),
        P(),
        P(),
        P(),
        P(None, None, None, "seq"),
        P("dp", "seq", None),
    )
    return jax.shard_map(
        on_device,
        mesh=mesh,
        in_specs=placed,
        out_specs=(
            P("dp", "seq", None),
            P("dp", "seq", None),
            P(("dp", "seq")),
            P(("dp", "seq"), None),
            P(("dp", "seq"), None),
            P(("dp", "seq"), None),
            P(("dp", "seq"), None),
            P(("dp", "seq"), None),
            P(None, None, "dp", "seq"),
        ),
        check_vma=False,
    )
```
